32 devices in a mesh: tower: 4 (over y, x), shard: 8 (over z, core).
Axes of the slice: x: 2, y: 2, z: 4, core: 2. Of those that a mesh axis runs over, the one named last changes fastest.
Arguments:
- out_grad: bfloat16 [1024, 1024], P(('tower', 'shard')), may hold values from -6 to 6
- pooled: bfloat16 [4, 1024, 2048], P('tower', 'shard'), may hold values from -6 to 6
- down_proj: bfloat16 [4, 2048, 256], P('tower'), may hold values from -0.125 to 0.125
- up_proj: bfloat16 [4, 256, 2048], P('tower'), may hold values from -0.375 to 0.375
- cross_bias: float32 [4, 2048], P('tower'), may hold values from -3 to 3
- out_proj: bfloat16 [4, 2048, 256], P('tower'), may hold values from -0.125 to 0.125
- assign: int32 [64], replicated, may hold values from 0 to 63, each once
Outputs:
- feature_grad: bfloat16 [1024, 8192], P(('tower', 'shard'))
- weight_grad: float32 [4, 768, 2048], P('tower', 'shard')
- bias_grad: float32 [4, 2048], P('tower')
The draws below stay inside these ranges and needn't reach their ends.
Inputs may be any that keep to these rules, and one draw needn't show every extreme that they name: `assign`: slot k of the 64 slots belongs to tower k // 16; every feature sits in exactly one slot.
All inputs are finite; a program needn't handle non-finite values.
Results may differ from the reference program's by a relative error of at most 0.01.
Values may be sent and summed in bfloat16 or wider, within the bound.
No kernel may reach another device: no remote copies, remote signals or barrier semaphores. Data moves between devices by JAX's collectives and lax.ppermute only.
A program may use at most 64 MiB of HBM per device.

```python
import math
import jax
import jax.numpy as jnp
from jax import lax

EMB = 128
R = 256
OUT = 256
ROWS_DEV = 32
W = 2048
TOWERS = 4
FEATURES = 64
ROWS = 1024
N_TOWER = 4
N_SHARD = 8


def block_scale(rng, shape, split, low, high):
    def one(axis_at, blocks):
        heights = jax.random.uniform(jax.random.fold_in(jax.random.fold_in(rng, 6), axis_at), (blocks,), jnp.float32, low / len(split), high / len(split))
        return jnp.repeat(jnp.exp(heights), shape[axis_at] // blocks).reshape((-1,) + (1,) * (len(shape) - axis_at - 1))

    gain = one(*split[0])
    for cut in split[1:]:
        gain = gain * one(*cut)
    return gain


def bell_draw(own_key, extent, scale, bound, cuts=(), held_as=jnp.bfloat16):
    result = jax.random.normal(own_key, extent, jnp.float32) * scale
    if len(cuts) > 0:
        result = block_scale(own_key, extent, cuts, -0.22, 0.18) * result
    return jnp.clip(result, min=-bound, max=bound).astype(held_as)


def setup_inputs(seed: int = 0) -> dict:
    key_list = jax.random.split(jax.random.key(seed), 8)
    out_grad = bell_draw(key_list[0], (ROWS, TOWERS * OUT), 1.0, 6.0, ((0, 32),))
    pooled = bell_draw(key_list[1], (TOWERS, ROWS, W), 1.0, 6.0, ((0, 4), (1, 8)))
    down_proj = bell_draw(key_list[2], (TOWERS, W, R), W ** -0.5, 0.125, ((0, 4),))
    up_proj = bell_draw(key_list[3], (TOWERS, R, W), R ** -0.5, 0.375, ((0, 4),))
    cross_bias = bell_draw(key_list[4], (TOWERS, W), 0.5, 3.0, ((0, 4),), jnp.float32)
    out_proj = bell_draw(key_list[5], (TOWERS, W, OUT), W ** -0.5, 0.125, ((0, 4),))
    assign = jax.random.permutation(key_list[6], FEATURES).astype(jnp.int32)
    return {"out_grad": out_grad, "pooled": pooled, "down_proj": down_proj, "up_proj": up_proj, "cross_bias": cross_bias, "out_proj": out_proj, "assign": assign}


def tower_backward(args):
    feature_in, grad_out, w_down, w_up, bias_row, w_out = args
    hidden_low = jnp.dot(feature_in, w_down, preferred_element_type=jnp.float32).astype(jnp.bfloat16)
    gate_full = jnp.dot(hidden_low, w_up, preferred_element_type=jnp.float32) + bias_row[None, :]
    factor = gate_full + 1.0
    inputs_wide = feature_in.astype(jnp.float32)
    crossed = (inputs_wide * factor).astype(jnp.bfloat16)
    grad_crossed = jnp.dot(grad_out, w_out.T, preferred_element_type=jnp.float32).astype(jnp.bfloat16)
    grad_gate = grad_crossed.astype(jnp.float32) * inputs_wide
    bias_part = lax.optimization_barrier(jnp.sum(grad_gate, axis=0))
    grad_gate_low = grad_gate.astype(jnp.bfloat16)
    grad_hidden = jnp.dot(grad_gate_low, w_up.T, preferred_element_type=jnp.float32).astype(jnp.bfloat16)
    grad_inputs = (grad_crossed.astype(jnp.float32) * factor + jnp.dot(grad_hidden, w_down.T, preferred_element_type=jnp.float32)).astype(jnp.bfloat16)
    stacked = jnp.concatenate([jnp.einsum('nr,nw->rw', grad_hidden.astype(jnp.float32), inputs_wide), jnp.einsum('nr,nw->rw', hidden_low.astype(jnp.float32), grad_gate_low.astype(jnp.float32)), jnp.einsum('nr,nw->rw', grad_out.astype(jnp.float32), crossed.astype(jnp.float32))], axis=0)
    return (grad_inputs, stacked, bias_part)

def reference(out_grad, pooled, down_proj, up_proj, cross_bias, out_proj, assign):
    regroup = out_grad.reshape(N_TOWER, N_SHARD, ROWS_DEV, N_TOWER, OUT).transpose(3, 1, 0, 2, 4).reshape(N_TOWER, ROWS, OUT)
    tower_grads, stacked, biases = lax.map(tower_backward, (pooled, regroup, down_proj, up_proj, cross_bias, out_proj))
    weight_scale = 1.0 / math.sqrt(ROWS)
    weight_grad = stacked * weight_scale
    returned = tower_grads.reshape(N_TOWER, N_SHARD, N_TOWER, ROWS_DEV, W).transpose(2, 1, 3, 0, 4).reshape(ROWS, N_TOWER * W)
    blocks = returned.reshape(ROWS, FEATURES, EMB)
    inverse = jnp.argsort(assign).astype(jnp.int32)
    feature_grad = jnp.take(blocks, inverse, axis=1).reshape(ROWS, FEATURES * EMB)
    return (feature_grad, weight_grad, biases)
```

```python
import functools
import math

import jax
import jax.numpy as jnp
from jax import lax
from jax.experimental import pallas as pl
from jax.experimental.pallas import tpu as pltpu
from jax.sharding import PartitionSpec as P

EMB = 128
VMEM_LIMIT = 48 * 1024 * 1024
BF16 = jnp.bfloat16
F32 = jnp.float32


def mm(a, b):
    return jnp.dot(a, b, preferred_element_type=F32)


def mm_nt(a, b):
    return lax.dot_general(a, b, (((1,), (1,)), ((), ())), preferred_element_type=F32)


def call(kernel, outs, scratch, n_smem, args, flops, name):
    smem = [pl.BlockSpec(memory_space=pltpu.SMEM)] * n_smem
    vmem = [pl.BlockSpec(memory_space=pltpu.VMEM)] * (len(args) - n_smem)
    moved = sum(a.size * a.dtype.itemsize for a in args) + sum(
        o.size * o.dtype.itemsize for o in outs
    )
    return pl.pallas_call(
        kernel,
        out_shape=outs,
        in_specs=smem + vmem,
        out_specs=[pl.BlockSpec(memory_space=pltpu.VMEM)] * len(outs),
        scratch_shapes=scratch,
        compiler_params=pltpu.CompilerParams(vmem_limit_bytes=VMEM_LIMIT),
        cost_estimate=pl.CostEstimate(flops=flops, bytes_accessed=moved, transcendentals=0),
        name=name,
    )(*args)


def column_chunks(width):
    step = 512 if width % 512 == 0 else width
    return [slice(c, c + step) for c in range(0, width, step)]


def split_kernel(n_tower, own_ref, other_ref, *out_refs):
    me = lax.axis_index("tower")
    rows = own_ref.shape[0]
    out = out_refs[0].shape[1]
    for k in range(n_tower):
        columns = pl.ds(pl.multiple_of((me ^ k) * out, out), out)
        out_refs[k][:rows] = own_ref[:, columns]
        out_refs[k][rows:] = other_ref[:, columns]


def gather_rows(piece_refs, half, g_ref):
    me = lax.axis_index("tower")
    rows = piece_refs[0].shape[0] // 2
    for k, piece in enumerate(piece_refs):
        g_ref[pl.ds(pl.multiple_of((me ^ k) * rows, rows), rows), :] = piece[
            half * rows : (half + 1) * rows, :
        ]


def tower_rows(x_ref, g_ref, wd_ref, wu_ref, wo_ref, bias_ref, ht_ref, gg_ref, cr_ref, bg_ref, direct_ref):
    rank = wu_ref.shape[0]
    g = g_ref[...]
    hidden_low = mm(x_ref[...], wd_ref[...]).astype(BF16)
    grad_hidden = jnp.zeros((x_ref.shape[0], rank), F32)
    for c in column_chunks(x_ref.shape[1]):
        x = x_ref[:, c].astype(F32)
        factor = (mm(hidden_low, wu_ref[:, c]) + bias_ref[:, c]) + 1.0
        cr_ref[:, c] = (x * factor).astype(BF16)
        grad_crossed = mm_nt(g, wo_ref[c, :]).astype(BF16).astype(F32)
        grad_gate = grad_crossed * x
        bg_ref[:, c] = jnp.sum(grad_gate, axis=0, keepdims=True)
        low = grad_gate.astype(BF16)
        gg_ref[:, c] = low
        grad_hidden += mm_nt(low, wu_ref[:, c])
        if direct_ref is not None:
            direct_ref[:, c] = grad_crossed * factor
    grad_hidden = grad_hidden.astype(BF16)
    ht_ref[0:rank, :] = grad_hidden.T
    ht_ref[rank : 2 * rank, :] = hidden_low.T
    ht_ref[2 * rank :, :] = g.T
    return grad_hidden


def own_kernel(n_tower, *refs):
    wd_ref, wu_ref, wo_ref, bias_ref, x_ref = refs[:5]
    pieces = refs[5 : 5 + n_tower]
    ht_ref, gg_ref, cr_ref, bg_ref, gi_ref, g_ref, direct_ref = refs[5 + n_tower :]
    gather_rows(pieces, 0, g_ref)
    grad_hidden = tower_rows(
        x_ref, g_ref, wd_ref, wu_ref, wo_ref, bias_ref, ht_ref, gg_ref, cr_ref, bg_ref, direct_ref
    )
    for c in column_chunks(x_ref.shape[1]):
        gi_ref[:, c] = (direct_ref[:, c] + mm_nt(grad_hidden, wd_ref[c, :])).astype(BF16)


def products(group, ht_a, ht_b, x_a, x_b, gg_a, gg_b, cr_a, cr_b, lhs_ref, acc_ref, send_ref, keep_ref):
    shard = lax.axis_index("shard")
    block = send_ref.shape[0]
    rank = ht_a.shape[0] // 3
    rows_a = ht_a.shape[1]
    core = lax.rem(shard, 2)
    first = (group * 4 + (lax.rem(shard, 4) - core)) * block
    picked = pl.ds(pl.multiple_of(first, 2 * block), 2 * block)
    lhs_ref[:, :rows_a] = ht_a[picked, :]
    lhs_ref[:, rows_a:] = ht_b[picked, :]
    acc_ref[...] = jnp.zeros_like(acc_ref)
    for part, (a_ref, b_ref) in enumerate(((x_a, x_b), (gg_a, gg_b), (cr_a, cr_b))):

        @pl.when((first < (part + 1) * rank) & (first + 2 * block > part * rank))
        def _():
            at = first + lax.broadcasted_iota(jnp.int32, lhs_ref.shape, 0)
            inside = (at >= part * rank) & (at < (part + 1) * rank)
            lhs = jnp.where(inside, lhs_ref[...].astype(F32), 0.0).astype(BF16)
            for c in column_chunks(acc_ref.shape[1]):
                rhs = jnp.concatenate([a_ref[:, c], b_ref[:, c]], axis=0)
                acc_ref[:, c] += mm(lhs, rhs)

    send_ref[...] = acc_ref[pl.ds(pl.multiple_of((1 - core) * block, block), block), :].astype(BF16)
    keep_ref[...] = acc_ref[pl.ds(pl.multiple_of(core * block, block), block), :]


def far_kernel(n_tower, *refs):
    wd_ref, wu_ref, wo_ref, bias_ref, x_own, ht_own, gg_own, cr_own, x_ref = refs[:9]
    pieces = refs[9 : 9 + n_tower]
    ht_ref, gg_ref, cr_ref, bg_ref, send_ref, keep_ref, g_ref, lhs_ref, acc_ref = refs[9 + n_tower :]
    gather_rows(pieces, 1, g_ref)
    tower_rows(x_ref, g_ref, wd_ref, wu_ref, wo_ref, bias_ref, ht_ref, gg_ref, cr_ref, bg_ref, None)
    group = 1 - lax.div(lax.axis_index("shard"), 4)
    products(
        group, ht_own, ht_ref, x_own, x_ref, gg_own, gg_ref, cr_own, cr_ref, lhs_ref, acc_ref, send_ref, keep_ref
    )


def near_kernel(ht_own, ht_ref, x_own, x_ref, gg_own, gg_ref, cr_own, cr_ref, send_ref, keep_ref, lhs_ref, acc_ref):
    group = lax.div(lax.axis_index("shard"), 4)
    products(
        group, ht_own, ht_ref, x_own, x_ref, gg_own, gg_ref, cr_own, cr_ref, lhs_ref, acc_ref, send_ref, keep_ref
    )


def place_kernel(n_tower, assign_ref, *refs):
    pieces, out_ref = refs[:n_tower], refs[n_tower]
    me = lax.axis_index("tower")
    slots = pieces[0].shape[1] // EMB
    for k in range(n_tower):
        for j in range(slots):
            at = assign_ref[(me ^ k) * slots + j] * EMB
            out_ref[:, pl.ds(pl.multiple_of(at, EMB), EMB)] = pieces[k][:, j * EMB : (j + 1) * EMB]


def xor_pairs(n, k):
    return [(i, i ^ k) for i in range(n)]


def paired_body(out_grad, pooled, down_proj, up_proj, cross_bias, out_proj, assign):
    n_tower, n_shard = lax.axis_size("tower"), lax.axis_size("shard")
    sds = jax.ShapeDtypeStruct
    w_down, w_up, w_out, x = down_proj[0], up_proj[0], out_proj[0], pooled[0]
    n, width = x.shape
    rank, out = w_up.shape[0], w_out.shape[1]
    stack = 2 * rank + out
    block = stack // n_shard
    top_rows = out_grad.shape[0]

    grad_other = lax.ppermute(out_grad, "shard", xor_pairs(n_shard, 2))
    x_other = lax.ppermute(x, "shard", xor_pairs(n_shard, 2))
    pieces = call(
        functools.partial(split_kernel, n_tower),
        [sds((2 * top_rows, out), BF16)] * n_tower,
        [],
        0,
        [out_grad, grad_other],
        0,
        "split_columns",
    )
    pieces = [pieces[0]] + [
        lax.ppermute(pieces[k], "tower", xor_pairs(n_tower, k)) for k in range(1, n_tower)
    ]
    per_matmul = 2 * n * width * rank
    weights = [w_down, w_up, w_out, cross_bias]
    wide = sds((n, width), BF16)
    row = sds((1, width), F32)
    ht_own, gg_own, cr_own, bg_own, grad_inputs = call(
        functools.partial(own_kernel, n_tower),
        [sds((stack, n), BF16), wide, wide, row, wide],
        [pltpu.VMEM((n, out), BF16), pltpu.VMEM((n, width), F32)],
        0,
        [*weights, x, *pieces],
        5 * per_matmul,
        "own_rows",
    )
    returned = []
    me = lax.axis_index("tower")
    for k in range(n_tower):
        piece = lax.dynamic_slice_in_dim(grad_inputs, (me ^ k) * top_rows, top_rows, 0)
        returned.append(piece if k == 0 else lax.ppermute(piece, "tower", xor_pairs(n_tower, k)))
    (feature_grad,) = call(
        functools.partial(place_kernel, n_tower),
        [sds((top_rows, n_tower * width), BF16)],
        [],
        1,
        [assign, *returned],
        0,
        "place_features",
    )

    sums = [sds((block, width), BF16), sds((block, width), F32)]
    sum_scratch = [pltpu.VMEM((2 * block, 2 * n), BF16), pltpu.VMEM((2 * block, width), F32)]
    ht_other, gg_other, cr_other, bg_other, far_send, far_keep = call(
        functools.partial(far_kernel, n_tower),
        [sds((stack, n), BF16), wide, wide, row, *sums],
        [pltpu.VMEM((n, out), BF16), *sum_scratch],
        0,
        [*weights, x, ht_own, gg_own, cr_own, x_other, *pieces],
        6 * per_matmul,
        "far_sums",
    )
    far = far_keep + lax.ppermute(far_send, "shard", xor_pairs(n_shard, 1)).astype(F32)
    far = lax.ppermute(far.astype(BF16), "shard", xor_pairs(n_shard, 4))
    near_send, near_keep = call(
        near_kernel,
        sums,
        sum_scratch,
        0,
        [ht_own, ht_other, x, x_other, gg_own, gg_other, cr_own, cr_other],
        3 * per_matmul,
        "near_sums",
    )
    near = near_keep + lax.ppermute(near_send, "shard", xor_pairs(n_shard, 1)).astype(F32)
    scale = 1.0 / math.sqrt(n * n_shard)
    weight_grad = ((near + far.astype(F32)) * scale)[None]
    bias_grad = bg_own + bg_other
    bias_grad = bias_grad + lax.ppermute(bias_grad, "shard", xor_pairs(n_shard, 1))
    bias_grad = bias_grad + lax.ppermute(bias_grad, "shard", xor_pairs(n_shard, 4))
    return feature_grad, weight_grad, bias_grad


def general_body(out_grad, pooled, down_proj, up_proj, cross_bias, out_proj, assign):
    grad_out = lax.all_to_all(out_grad, "tower", split_axis=1, concat_axis=0, tiled=True)
    feature_in = pooled[0]
    w_down, w_up, w_out = down_proj[0], up_proj[0], out_proj[0]
    hidden_low = mm(feature_in, w_down).astype(BF16)
    factor = mm(hidden_low, w_up) + cross_bias + 1.0
    crossed = (feature_in * factor).astype(BF16)
    grad_crossed = mm_nt(grad_out, w_out).astype(BF16)
    grad_gate = grad_crossed.astype(F32) * feature_in
    grad_gate_low = grad_gate.astype(BF16)
    grad_hidden = mm_nt(grad_gate_low, w_up).astype(BF16)
    grad_inputs = (grad_crossed.astype(F32) * factor + mm_nt(grad_hidden, w_down)).astype(BF16)
    returned = lax.all_to_all(grad_inputs, "tower", split_axis=0, concat_axis=1, tiled=True)
    local_rows = returned.shape[0]
    blocks = returned.reshape(local_rows, -1, EMB)
    feature_grad = jnp.take(blocks, jnp.argsort(assign), axis=1).reshape(local_rows, -1)
    stacked = jnp.concatenate(
        [
            mm(grad_hidden.T, feature_in),
            mm(hidden_low.T, grad_gate_low),
            mm(grad_out.T, crossed),
        ],
        axis=0,
    )
    scale = 1.0 / math.sqrt(grad_out.shape[0] * lax.axis_size("shard"))
    summed = lax.psum_scatter(stacked, "shard", scatter_dimension=0, tiled=True)
    bias_grad = lax.psum(jnp.sum(grad_gate, axis=0), "shard")[None]
    return feature_grad, (summed * scale)[None], bias_grad


def solution(mesh):
    n_tower, n_shard = mesh.shape["tower"], mesh.shape["shard"]
    placed = (
        P(("tower", "shard"), None),
        P("tower", "shard", None),
        P("tower", None, None),
        P("tower", None, None),
        P("tower", None),
        P("tower", None, None),
        P(),
    )

    paired = n_shard == 2 * 4 and n_tower & (n_tower - 1) == 0
    return jax.shard_map(
        paired_body if paired else general_body,
        mesh=mesh,
        in_specs=placed,
        out_specs=(P(("tower", "shard"), None), P("tower", "shard", None), P("tower", None)),
        check_vma=False,
    )
```

```python
import functools
import math

import jax
import jax.numpy as jnp
from jax import lax
from jax.experimental import pallas as pl
from jax.experimental.pallas import tpu as pltpu
from jax.sharding import PartitionSpec as P

EMB = 128
MIB = 1024 * 1024
VM = 48
COST = 10**10
VMEM_LIMIT = 24 * MIB
BF16 = jnp.bfloat16
F32 = jnp.float32
HBM, VMEM, SMEM = pltpu.HBM, pltpu.VMEM, pltpu.SMEM


def mm(a, b):
    return jnp.dot(a, b, preferred_element_type=F32)


def mm_nt(a, b):
    return lax.dot_general(a, b, (((1,), (1,)), ((), ())), preferred_element_type=F32)


def call(kernel, outs, scratch, spaces, args, name, vmem=VMEM_LIMIT, cost=COST):
    return pl.pallas_call(
        kernel,
        out_shape=outs,
        in_specs=[pl.BlockSpec(memory_space=space) for space in spaces],
        out_specs=[pl.BlockSpec(memory_space=pltpu.VMEM)] * len(outs),
        scratch_shapes=scratch,
        compiler_params=pltpu.CompilerParams(vmem_limit_bytes=vmem),
        cost_estimate=pl.CostEstimate(flops=cost, bytes_accessed=1, transcendentals=0),
        name=name,
    )(*args)


def column_chunks(width):
    step = 512 if width % 512 == 0 else width
    return [slice(c, c + step) for c in range(0, width, step)]


def copy_all(pairs, sem_ref):
    copies = [pltpu.make_async_copy(a, b, sem_ref.at[i]) for i, (a, b) in enumerate(pairs)]
    for copy in copies:
        copy.start()
    return copies


def cut_kernel(n_tower, grad_ref, *refs):
    pieces, sem_ref = refs[:n_tower], refs[n_tower]
    me = lax.axis_index("tower")
    out = pieces[0].shape[1]
    pairs = [
        (grad_ref.at[:, pl.ds(pl.multiple_of((me ^ k) * out, out), out)], piece)
        for k, piece in enumerate(pieces)
    ]
    for copy in copy_all(pairs, sem_ref):
        copy.wait()


def forward_rows(x_ref, wd_ref, wu_ref, bias_ref, low_ref, cr_ref, factor_ref, ready=None):
    low = mm(x_ref[...], wd_ref[...]).astype(BF16)
    low_ref[...] = low
    if ready is not None:
        ready.wait()
    for c in column_chunks(x_ref.shape[1]):
        factor = (mm(low, wu_ref[:, c]) + bias_ref[:, c]) + 1.0
        cr_ref[:, c] = (x_ref[:, c].astype(F32) * factor).astype(BF16)
        if factor_ref is not None:
            factor_ref[:, c] = factor


def backward_rows(x_ref, g, low_ref, wu_ref, wo_ref, gg_ref, bg_ref, ht_ref, factor_ref, direct_ref):
    rank = wu_ref.shape[0]
    grad_hidden = jnp.zeros((x_ref.shape[0], rank), F32)
    for c in column_chunks(x_ref.shape[1]):
        x = x_ref[:, c].astype(F32)
        grad_crossed = mm_nt(g, wo_ref[c, :]).astype(BF16).astype(F32)
        grad_gate = grad_crossed * x
        bg_ref[:, c] = jnp.sum(grad_gate, axis=0, keepdims=True)
        low = grad_gate.astype(BF16)
        gg_ref[:, c] = low
        grad_hidden += mm_nt(low, wu_ref[:, c])
        if direct_ref is not None:
            direct_ref[:, c] = grad_crossed * factor_ref[:, c]
    grad_hidden = grad_hidden.astype(BF16)
    ht_ref[0:rank, :] = grad_hidden.T
    ht_ref[rank : 2 * rank, :] = low_ref[...].T
    ht_ref[2 * rank :, :] = g.T
    return grad_hidden


def forward_kernel(wd_hbm, wu_hbm, wo_hbm, x_hbm, bias_ref, wd_ref, wu_ref, wo_ref, x_ref, low_ref, cr_ref, factor_ref, sem_ref):
    copies = copy_all([(x_hbm, x_ref), (wd_hbm, wd_ref), (wu_hbm, wu_ref), (wo_hbm, wo_ref)], sem_ref)
    copies[0].wait()
    copies[1].wait()
    forward_rows(x_ref, wd_ref, wu_ref, bias_ref, low_ref, cr_ref, factor_ref, copies[2])
    copies[3].wait()


def forward_other_kernel(wd_ref, wu_ref, bias_ref, x_ref, low_ref, cr_ref):
    forward_rows(x_ref, wd_ref, wu_ref, bias_ref, low_ref, cr_ref, None)


def backward_kernel(n_tower, wu_ref, wo_ref, x_ref, low_ref, factor_ref, *refs):
    pieces = refs[:n_tower]
    g_ref, gh_ref, ht_ref, gg_ref, bg_ref, direct_ref = refs[n_tower:]
    me = lax.axis_index("tower")
    rows = pieces[0].shape[0]
    for k, piece in enumerate(pieces):
        g_ref[pl.ds(pl.multiple_of((me ^ k) * rows, rows), rows), :] = piece[...]
    gh_ref[...] = backward_rows(
        x_ref, g_ref[...], low_ref, wu_ref, wo_ref, gg_ref, bg_ref, ht_ref, factor_ref, direct_ref
    )


def inputs_kernel(n_tower, wd_ref, gh_ref, direct_ref, *refs):
    pieces, gi_ref = refs[:n_tower], refs[n_tower]
    me = lax.axis_index("tower")
    rows = pieces[0].shape[0]
    grad_hidden = gh_ref[...]
    for c in column_chunks(gi_ref.shape[1]):
        gi_ref[:, c] = (direct_ref[:, c] + mm_nt(grad_hidden, wd_ref[c, :])).astype(BF16)
    for k, piece in enumerate(pieces):
        piece[...] = gi_ref[pl.ds(pl.multiple_of((me ^ k) * rows, rows), rows), :]


def products(group, ht_a, ht_b, operands, lhs_ref, acc_ref, send_refs, keep_ref):
    shard = lax.axis_index("shard")
    block = keep_ref.shape[0]
    rank = ht_a.shape[0] // 3
    rows_a = ht_a.shape[1]
    core = lax.rem(shard, 2)
    first = (group * 4 + (lax.rem(shard, 4) - core)) * block
    picked = pl.ds(pl.multiple_of(first, 2 * block), 2 * block)
    lhs_ref[:, :rows_a] = ht_a[picked, :]
    lhs_ref[:, rows_a:] = ht_b[picked, :]
    acc_ref[...] = jnp.zeros_like(acc_ref)
    for part, (a_ref, b_ref) in enumerate(operands):

        @pl.when((first < (part + 1) * rank) & (first + 2 * block > part * rank))
        def _():
            at = first + lax.broadcasted_iota(jnp.int32, lhs_ref.shape, 0)
            inside = (at >= part * rank) & (at < (part + 1) * rank)
            lhs = jnp.where(inside, lhs_ref[...].astype(F32), 0.0).astype(BF16)
            for c in column_chunks(acc_ref.shape[1]):
                rhs = jnp.concatenate([a_ref[:, c], b_ref[:, c]], axis=0)
                acc_ref[:, c] += mm(lhs, rhs)

    other = pl.ds(pl.multiple_of((1 - core) * block, block), block)
    width = send_refs[0].shape[1]
    for i, send_ref in enumerate(send_refs):
        send_ref[...] = acc_ref[other, i * width : (i + 1) * width].astype(BF16)
    keep_ref[...] = acc_ref[pl.ds(pl.multiple_of(core * block, block), block), :]


def far_kernel(n_cuts, wu_ref, wo_ref, x_own, gg_own, cr_own, ht_own, bg_own, x_ref, low_ref, cr_ref, g_ref, *refs):
    gg_ref, ht_ref, bg_ref, keep_ref = refs[:4]
    send_refs = refs[4 : 4 + n_cuts]
    lhs_ref, acc_ref = refs[4 + n_cuts :]
    backward_rows(x_ref, g_ref[...], low_ref, wu_ref, wo_ref, gg_ref, bg_ref, ht_ref, None, None)
    bg_ref[...] = bg_own[...] + bg_ref[...]
    group = 1 - lax.div(lax.axis_index("shard"), 4)
    operands = ((x_own, x_ref), (gg_own, gg_ref), (cr_own, cr_ref))
    products(group, ht_own, ht_ref, operands, lhs_ref, acc_ref, send_refs, keep_ref)


def near_kernel(x_own, gg_own, cr_own, ht_own, x_ref, gg_ref, cr_ref, ht_ref, send_ref, keep_ref, lhs_ref, acc_ref):
    group = lax.div(lax.axis_index("shard"), 4)
    operands = ((x_own, x_ref), (gg_own, gg_ref), (cr_own, cr_ref))
    products(group, ht_own, ht_ref, operands, lhs_ref, acc_ref, [send_ref], keep_ref)


def round_kernel(at, keep_ref, recv_ref, out_ref):
    width = out_ref.shape[1]
    out_ref[...] = (keep_ref[:, at * width : (at + 1) * width] + recv_ref[...].astype(F32)).astype(BF16)


def final_kernel(scale, keep_ref, near_ref, bias_ref, bias_far_ref, *refs):
    fars, out_ref, bg_ref = refs[:-2], refs[-2], refs[-1]
    bg_ref[...] = bias_ref[...] + bias_far_ref[...]
    width = fars[0].shape[1]
    for i, far in enumerate(fars):
        c = slice(i * width, (i + 1) * width)
        out_ref[:, c] = ((keep_ref[:, c] + near_ref[:, c].astype(F32)) + far[...].astype(F32)) * scale


def place_kernel(n_tower, assign_ref, *refs):
    pieces, out_ref = refs[:n_tower], refs[n_tower]
    me = lax.axis_index("tower")
    slots = pieces[0].shape[1] // EMB
    for k in range(n_tower):
        for j in range(slots):
            at = assign_ref[(me ^ k) * slots + j] * EMB
            out_ref[:, pl.ds(pl.multiple_of(at, EMB), EMB)] = pieces[k][:, j * EMB : (j + 1) * EMB]


def xor_pairs(n, k):
    return [(i, i ^ k) for i in range(n)]


def after(value, *earlier):
    return lax.optimization_barrier((value, *earlier))[0]


def paired_body(out_grad, pooled, down_proj, up_proj, cross_bias, out_proj, assign):
    n_tower, n_shard = lax.axis_size("tower"), lax.axis_size("shard")
    sds = jax.ShapeDtypeStruct
    w_down, w_up, w_out, x = down_proj[0], up_proj[0], out_proj[0], pooled[0]
    n, width = x.shape
    rank, out = w_up.shape[0], w_out.shape[1]
    stack = 2 * rank + out
    block = stack // n_shard
    top_rows = out_grad.shape[0]
    n_cuts = 1
    cut = width // n_cuts
    wide = sds((n, width), BF16)
    tall = sds((stack, n), BF16)
    low = sds((n, rank), BF16)
    row = sds((1, width), F32)

    def across(value, axis, k):
        return lax.ppermute(value, axis, xor_pairs(lax.axis_size(axis), k))

    x_other = across(x, "shard", 2)
    pieces = call(
        functools.partial(cut_kernel, n_tower),
        [sds((top_rows, out), BF16)] * n_tower,
        [pltpu.SemaphoreType.DMA((n_tower,))],
        [HBM],
        [out_grad],
        "cut_columns",
        60 * MIB,
        1,
    )
    pieces = [pieces[0]] + [across(pieces[k], "tower", k) for k in range(1, n_tower)]
    wd, wu, wo, x_own, low_own, cr_own, factor = call(
        forward_kernel,
        [sds(w.shape, BF16) for w in (w_down, w_up, w_out)] + [wide, low, wide, sds((n, width), F32)],
        [pltpu.SemaphoreType.DMA((4,))],
        [HBM] * 4 + [VMEM],
        [w_down, w_up, w_out, x, cross_bias],
        "forward_own",
        VM * MIB,
        1,
    )
    g_own, gh_own, ht_own, gg_own, bg_own, direct = call(
        functools.partial(backward_kernel, n_tower),
        [sds((n, out), BF16), low, tall, wide, row, sds((n, width), F32)],
        [],
        [VMEM] * (5 + n_tower),
        [wu, wo, x_own, low_own, factor, *pieces],
        "backward_own",
        cost=1,
    )
    g_other = across(g_own, "shard", 2)
    grad_inputs = call(
        functools.partial(inputs_kernel, n_tower),
        [sds((top_rows, width), BF16)] * n_tower,
        [pltpu.VMEM((n, width), BF16)],
        [VMEM] * 3,
        [wd, gh_own, direct],
        "grad_inputs",
    )
    returned = [grad_inputs[0]] + [across(grad_inputs[k], "tower", k) for k in range(1, n_tower)]
    low_other, cr_other = call(
        forward_other_kernel,
        [low, wide],
        [],
        [VMEM] * 4,
        [wd, wu, cross_bias, x_other],
        "forward_other",
    )
    gg_other, ht_other, bias_sum, far_keep, *far_sends = call(
        functools.partial(far_kernel, n_cuts),
        [wide, tall, row, sds((block, width), F32)] + [sds((block, cut), BF16)] * n_cuts,
        [pltpu.VMEM((2 * block, 2 * n), BF16), pltpu.VMEM((2 * block, width), F32)],
        [VMEM] * 11,
        [wu, wo, x_own, gg_own, cr_own, ht_own, bg_own, x_other, low_other, cr_other, g_other],
        "far_sums",
    )
    fars = []
    for i, send in enumerate(far_sends):
        (far,) = call(
            functools.partial(round_kernel, i),
            [sds((block, cut), BF16)],
            [],
            [VMEM] * 2,
            [far_keep, across(send, "shard", 1)],
            "far_round",
            cost=1,
        )
        fars.append(across(far, "shard", 4))
    near_send, near_keep = call(
        near_kernel,
        [sds((block, width), BF16), sds((block, width), F32)],
        [pltpu.VMEM((2 * block, 2 * n), BF16), pltpu.VMEM((2 * block, width), F32)],
        [VMEM] * 8,
        [x_own, gg_own, cr_own, ht_own, x_other, gg_other, cr_other, after(ht_other, far)],
        "near_sums",
    )
    near_other = across(near_send, "shard", 1)
    bias_sum = bias_sum + across(bias_sum, "shard", 1)
    bias_far = across(bias_sum, "shard", 4)
    (feature_grad,) = call(
        functools.partial(place_kernel, n_tower),
        [sds((top_rows, n_tower * width), BF16)],
        [],
        [SMEM] + [VMEM] * n_tower,
        [assign, *returned],
        "place_features",
        cost=1,
    )
    weight_grad, bias_grad = call(
        functools.partial(final_kernel, 1.0 / math.sqrt(n * n_shard)),
        [sds((block, width), F32), row],
        [],
        [VMEM] * (4 + n_cuts),
        [near_keep, near_other, bias_sum, bias_far, *fars],
        "add_up",
    )
    return feature_grad, weight_grad[None], bias_grad


def general_body(out_grad, pooled, down_proj, up_proj, cross_bias, out_proj, assign):
    grad_out = lax.all_to_all(out_grad, "tower", split_axis=1, concat_axis=0, tiled=True)
    feature_in = pooled[0]
    w_down, w_up, w_out = down_proj[0], up_proj[0], out_proj[0]
    hidden_low = mm(feature_in, w_down).astype(BF16)
    factor = mm(hidden_low, w_up) + cross_bias + 1.0
    crossed = (feature_in * factor).astype(BF16)
    grad_crossed = mm_nt(grad_out, w_out).astype(BF16)
    grad_gate = grad_crossed.astype(F32) * feature_in
    grad_gate_low = grad_gate.astype(BF16)
    grad_hidden = mm_nt(grad_gate_low, w_up).astype(BF16)
    grad_inputs = (grad_crossed.astype(F32) * factor + mm_nt(grad_hidden, w_down)).astype(BF16)
    returned = lax.all_to_all(grad_inputs, "tower", split_axis=0, concat_axis=1, tiled=True)
    local_rows = returned.shape[0]
    blocks = returned.reshape(local_rows, -1, EMB)
    feature_grad = jnp.take(blocks, jnp.argsort(assign), axis=1).reshape(local_rows, -1)
    stacked = jnp.concatenate(
        [
            mm(grad_hidden.T, feature_in),
            mm(hidden_low.T, grad_gate_low),
            mm(grad_out.T, crossed),
        ],
        axis=0,
    )
    scale = 1.0 / math.sqrt(grad_out.shape[0] * lax.axis_size("shard"))
    summed = lax.psum_scatter(stacked, "shard", scatter_dimension=0, tiled=True)
    bias_grad = lax.psum(jnp.sum(grad_gate, axis=0), "shard")[None]
    return feature_grad, (summed * scale)[None], bias_grad


def solution(mesh):
    n_tower, n_shard = mesh.shape["tower"], mesh.shape["shard"]
    placed = (
        P(("tower", "shard"), None),
        P("tower", "shard", None),
        P("tower", None, None),
        P("tower", None, None),
        P("tower", None),
        P("tower", None, None),
        P(),
    )

    paired = n_shard == 2 * 4 and n_tower & (n_tower - 1) == 0
    return jax.shard_map(
        paired_body if paired else general_body,
        mesh=mesh,
        in_specs=placed,
        out_specs=(P(("tower", "shard"), None), P("tower", "shard", None), P("tower", None)),
        check_vma=False,
    )
```

```python
import functools
import math

import jax
import jax.numpy as jnp
from jax import lax
from jax.experimental import pallas as pl
from jax.experimental.pallas import tpu as pltpu
from jax.sharding import PartitionSpec as P

EMB = 128
SLAB = 256
TILE = 16
MIB = 1024 * 1024
VM = 48
COST = 10**10
FAR = 6
VMEM_LIMIT = 24 * MIB
BF16 = jnp.bfloat16
F32 = jnp.float32
HBM, VMEM, SMEM = pltpu.HBM, pltpu.VMEM, pltpu.SMEM


def mm(a, b):
    return jnp.dot(a, b, preferred_element_type=F32)


def mm_nt(a, b):
    return lax.dot_general(a, b, (((1,), (1,)), ((), ())), preferred_element_type=F32)


def call(kernel, outs, scratch, spaces, args, name, vmem=VMEM_LIMIT, cost=COST, out_space=None, aliases={}):
    return pl.pallas_call(
        kernel,
        out_shape=outs,
        in_specs=[pl.BlockSpec(memory_space=space) for space in spaces],
        out_specs=[pl.BlockSpec(memory_space=out_space or VMEM)] * len(outs),
        input_output_aliases=aliases,
        scratch_shapes=scratch,
        compiler_params=pltpu.CompilerParams(vmem_limit_bytes=vmem),
        cost_estimate=pl.CostEstimate(flops=cost, bytes_accessed=1, transcendentals=0),
        name=name,
    )(*args)


def column_chunks(width):
    step = 512 if width % 512 == 0 else width
    return [slice(c, c + step) for c in range(0, width, step)]


def copy_all(pairs, sem_ref):
    copies = [pltpu.make_async_copy(a, b, sem_ref.at[i]) for i, (a, b) in enumerate(pairs)]
    for copy in copies:
        copy.start()
    return copies


def cut_kernel(n_tower, grad_ref, *refs):
    pieces, sem_ref = refs[:n_tower], refs[n_tower]
    me = lax.axis_index("tower")
    out = pieces[0].shape[1]
    pairs = [
        (grad_ref.at[:, pl.ds(pl.multiple_of((me ^ k) * out, out), out)], piece)
        for k, piece in enumerate(pieces)
    ]
    for copy in copy_all(pairs, sem_ref):
        copy.wait()


def forward_rows(x_ref, wd_ref, wu_ref, bias_ref, low_ref, cr_ref, factor_ref=None, ready=None):
    low = mm(x_ref[...], wd_ref[...]).astype(BF16)
    low_ref[...] = low
    if ready is not None:
        ready.wait()
    for c in column_chunks(x_ref.shape[1]):
        factor = (mm(low, wu_ref[:, c]) + bias_ref[:, c]) + 1.0
        cr_ref[:, c] = (x_ref[:, c].astype(F32) * factor).astype(BF16)
        if factor_ref is not None:
            factor_ref[:, c] = factor


def backward_rows(x_ref, g, low_ref, wu_ref, wo_ref, gg_ref, bg_ref, ht_ref, factor_ref, direct_ref):
    rank = wu_ref.shape[0]
    grad_hidden = jnp.zeros((x_ref.shape[0], rank), F32)
    for c in column_chunks(x_ref.shape[1]):
        x = x_ref[:, c].astype(F32)
        grad_crossed = mm_nt(g, wo_ref[c, :]).astype(BF16).astype(F32)
        grad_gate = grad_crossed * x
        bg_ref[:, c] = jnp.sum(grad_gate, axis=0, keepdims=True)
        low = grad_gate.astype(BF16)
        gg_ref[:, c] = low
        grad_hidden += mm_nt(low, wu_ref[:, c])
        if direct_ref is not None:
            direct_ref[:, c] = grad_crossed * factor_ref[:, c]
    grad_hidden = grad_hidden.astype(BF16)
    ht_ref[0:rank, :] = grad_hidden.T
    ht_ref[rank : 2 * rank, :] = low_ref[...].T
    ht_ref[2 * rank :, :] = g.T
    return grad_hidden


def forward_kernel(wd_hbm, wu_hbm, wo_hbm, x_hbm, bias_ref, wd_ref, wu_ref, wo_ref, x_ref, low_ref, cr_ref, factor_ref, sem_ref):
    copies = copy_all([(x_hbm, x_ref), (wd_hbm, wd_ref), (wu_hbm, wu_ref), (wo_hbm, wo_ref)], sem_ref)
    copies[0].wait()
    copies[1].wait()
    forward_rows(x_ref, wd_ref, wu_ref, bias_ref, low_ref, cr_ref, factor_ref, copies[2])
    copies[3].wait()


def backward_kernel(n_tower, wu_ref, wo_ref, x_ref, low_ref, factor_ref, *refs):
    pieces = refs[:n_tower]
    g_ref, gh_ref, ht_ref, gg_ref, bg_ref, direct_ref = refs[n_tower:]
    me = lax.axis_index("tower")
    rows = pieces[0].shape[0]
    for k, piece in enumerate(pieces):
        g_ref[pl.ds(pl.multiple_of((me ^ k) * rows, rows), rows), :] = piece[...]
    gh_ref[...] = backward_rows(
        x_ref, g_ref[...], low_ref, wu_ref, wo_ref, gg_ref, bg_ref, ht_ref, factor_ref, direct_ref
    )


def inputs_kernel(n_tower, wd_ref, gh_ref, direct_ref, *refs):
    pieces, gi_ref = refs[:n_tower], refs[n_tower]
    me = lax.axis_index("tower")
    rows = pieces[0].shape[0]
    grad_hidden = gh_ref[...]
    for c in column_chunks(gi_ref.shape[1]):
        gi_ref[:, c] = (direct_ref[:, c] + mm_nt(grad_hidden, wd_ref[c, :])).astype(BF16)
    for k, piece in enumerate(pieces):
        piece[...] = gi_ref[pl.ds(pl.multiple_of((me ^ k) * rows, rows), rows), :]


def products(flip, start, ht_a, ht_b, operands, lhs_ref, acc_ref):
    shard = lax.axis_index("shard") ^ flip
    block = acc_ref.shape[0] // 2
    rank = ht_a.shape[0] // 3
    rows_a = ht_a.shape[1]
    core = lax.rem(shard, 2)
    first = (shard - core) * block
    picked = pl.ds(pl.multiple_of(first, 2 * block), 2 * block)
    lhs_ref[:, :rows_a] = ht_a[picked, :]
    lhs_ref[:, rows_a:] = ht_b[picked, :]
    acc_ref[...] = jnp.zeros_like(acc_ref)
    for part, (a_ref, b_ref) in enumerate(operands):

        @pl.when((first < (part + 1) * rank) & (first + 2 * block > part * rank))
        def _():
            at = first + lax.broadcasted_iota(jnp.int32, lhs_ref.shape, 0)
            inside = (at >= part * rank) & (at < (part + 1) * rank)
            lhs = jnp.where(inside, lhs_ref[...].astype(F32), 0.0).astype(BF16)
            for c in column_chunks(acc_ref.shape[1]):
                at_c = slice(start + c.start, start + c.stop)
                acc_ref[:, c] += mm(lhs, jnp.concatenate([a_ref[:, at_c], b_ref[:, at_c]], axis=0))

    theirs = pl.ds(pl.multiple_of((1 - core) * block, block), block)
    ours = pl.ds(pl.multiple_of(core * block, block), block)
    return theirs, ours


def bias_rows(bias):
    high = bias.astype(BF16).astype(F32)
    rest = bias - high
    slabs = [slice(c, c + SLAB) for c in range(0, bias.shape[1], SLAB)]
    filler = [jnp.zeros((1, SLAB), F32)] * (TILE - 2 * len(slabs))
    return jnp.concatenate([high[:, c] for c in slabs] + [rest[:, c] for c in slabs] + filler, axis=0)


def bias_of(rows, n_slabs):
    return jnp.concatenate([rows[j : j + 1] + rows[n_slabs + j : n_slabs + j + 1] for j in range(n_slabs)], axis=1)


def backward_other_kernel(wu_ref, wo_ref, bg_own, x_ref, low_ref, g_ref, gg_ref, ht_ref, bg_ref):
    backward_rows(x_ref, g_ref[...], low_ref, wu_ref, wo_ref, gg_ref, bg_ref, ht_ref, None, None)
    bg_ref[...] = bg_own[...] + bg_ref[...]


def far_sums(flip, start, own, other, bg_ref, send_ref, keep_ref, lhs_ref, acc_ref):
    theirs, ours = products(flip, start, own[3], other[3], list(zip(own[:3], other[:3])), lhs_ref, acc_ref)
    block, width = acc_ref.shape[0] // 2, acc_ref.shape[1]
    for j in range(width // SLAB):
        c, rows = slice(j * SLAB, (j + 1) * SLAB), slice(j * block, (j + 1) * block)
        send_ref[rows, :] = acc_ref[theirs, c].astype(BF16)
        keep_ref[rows, :] = acc_ref[ours, c]
    rows = bias_rows(bg_ref[:, start : start + width])
    send_ref[-TILE:, :] = rows.astype(BF16)
    keep_ref[-TILE:, :] = rows.astype(BF16).astype(F32)


def far_more_kernel(flip, start, *refs):
    far_sums(flip, start, refs[:4], refs[4:8], *refs[8:])


def far_kernel(flip, wu_ref, wo_ref, bg_own, x_own, gg_own, cr_own, ht_own, x_ref, low_ref, cr_ref, g_ref, *refs):
    gg_ref, ht_ref, bg_ref = refs[:3]
    backward_other_kernel(wu_ref, wo_ref, bg_own, x_ref, low_ref, g_ref, gg_ref, ht_ref, bg_ref)
    far_sums(flip, 0, (x_own, gg_own, cr_own, ht_own), (x_ref, gg_ref, cr_ref, ht_ref), bg_ref, *refs[3:])


def near_kernel(*refs):
    own, other = refs[:4], refs[4:8]
    send_ref, keep_ref, lhs_ref, acc_ref = refs[8:]
    theirs, ours = products(0, 0, own[3], other[3], list(zip(own[:3], other[:3])), lhs_ref, acc_ref)
    send_ref[...] = acc_ref[theirs, :].astype(BF16)
    keep_ref[...] = acc_ref[ours, :]


def round_kernel(n_slabs, keep_ref, recv_ref, out_ref):
    out_ref[:-TILE, :] = (keep_ref[:-TILE, :] + recv_ref[:-TILE, :].astype(F32)).astype(BF16)
    rows = keep_ref[-TILE:, :] + recv_ref[-TILE:, :].astype(F32)
    out_ref[-TILE:, :] = bias_rows(bias_of(rows, n_slabs)).astype(BF16)


def final_kernel(scale, start, keep_ref, near_ref, sent_ref, far_ref, *refs):
    out_ref, bg_out, total_ref, bg_ref, sem_ref = refs[-5:]
    block, width = total_ref.shape
    n_slabs = width // SLAB
    copies = []

    def write(source, target, i):
        copies.append(pltpu.make_async_copy(source, target, sem_ref.at[i]))
        copies[-1].start()

    for j in range(n_slabs):
        w = slice(start + j * SLAB, start + (j + 1) * SLAB)
        total = keep_ref[:, w] + near_ref[:, w].astype(F32)
        total = total + far_ref[j * block : (j + 1) * block, :].astype(F32)
        total_ref[:, j * SLAB : (j + 1) * SLAB] = total * scale
        write(total_ref.at[:, pl.ds(j * SLAB, SLAB)], out_ref.at[:, pl.ds(w.start, SLAB)], j)
    ours, theirs = sent_ref[-TILE:, :].astype(F32), far_ref[-TILE:, :].astype(F32)
    bg_ref[...] = bias_of(ours, n_slabs) + bias_of(theirs, n_slabs)
    write(bg_ref, bg_out.at[:, pl.ds(start, width)], n_slabs)
    for copy in copies:
        copy.wait()


def place_kernel(n_tower, assign_ref, *refs):
    pieces, out_ref = refs[:n_tower], refs[n_tower]
    me = lax.axis_index("tower")
    slots = pieces[0].shape[1] // EMB
    for k in range(n_tower):
        for j in range(slots):
            at = assign_ref[(me ^ k) * slots + j] * EMB
            out_ref[:, pl.ds(pl.multiple_of(at, EMB), EMB)] = pieces[k][:, j * EMB : (j + 1) * EMB]


def xor_pairs(n, k):
    return [(i, i ^ k) for i in range(n)]


def after(value, *earlier):
    return lax.optimization_barrier((value, *earlier))[0]


def paired_body(out_grad, pooled, down_proj, up_proj, cross_bias, out_proj, assign):
    n_tower, n_shard = lax.axis_size("tower"), lax.axis_size("shard")
    sds = jax.ShapeDtypeStruct
    w_down, w_up, w_out, x = down_proj[0], up_proj[0], out_proj[0], pooled[0]
    n, width = x.shape
    rank, out = w_up.shape[0], w_out.shape[1]
    stack = 2 * rank + out
    block = stack // n_shard
    top_rows = out_grad.shape[0]
    cuts = (0, width // 2, width)
    n_cuts = len(cuts) - 1
    wide = sds((n, width), BF16)
    tall = sds((stack, n), BF16)
    low = sds((n, rank), BF16)
    row = sds((1, width), F32)

    def across(value, axis, k):
        return lax.ppermute(value, axis, xor_pairs(lax.axis_size(axis), k))

    x_other = across(x, "shard", 2)
    pieces = call(
        functools.partial(cut_kernel, n_tower),
        [sds((top_rows, out), BF16)] * n_tower,
        [pltpu.SemaphoreType.DMA((n_tower,))],
        [HBM],
        [out_grad],
        "cut_columns",
        48 * MIB,
        1,
    )
    pieces = [pieces[0]] + [across(pieces[k], "tower", k) for k in range(1, n_tower)]
    wd, wu, wo, x_own, low_own, cr_own, factor = call(
        forward_kernel,
        [sds(w.shape, BF16) for w in (w_down, w_up, w_out)] + [wide, low, wide, sds((n, width), F32)],
        [pltpu.SemaphoreType.DMA((4,))],
        [HBM] * 4 + [VMEM],
        [w_down, w_up, w_out, x, cross_bias],
        "forward_own",
        VM * MIB,
        1,
    )
    g_own, gh_own, ht_own, gg_own, bg_own, direct = call(
        functools.partial(backward_kernel, n_tower),
        [sds((n, out), BF16), low, tall, wide, row, sds((n, width), F32)],
        [],
        [VMEM] * (5 + n_tower),
        [wu, wo, x_own, low_own, factor, *pieces],
        "backward_own",
        cost=1,
    )
    g_other = across(g_own, "shard", 2)
    low_other, cr_other = call(
        forward_rows,
        [low, wide],
        [],
        [VMEM] * 4,
        [x_other, wd, wu, cross_bias],
        "forward_other",
    )

    def slab_outs(cut):
        shape = (block * cut // SLAB + TILE, SLAB)
        return [sds(shape, BF16), sds(shape, F32)]

    def sum_scratch(cut):
        return [pltpu.VMEM((2 * block, 2 * n), BF16), pltpu.VMEM((2 * block, cut), F32)]

    own = [x_own, gg_own, cr_own, ht_own]
    gg_other, ht_other, bias_sum, *far = call(
        functools.partial(far_kernel, FAR),
        [wide, tall, row] + slab_outs(cuts[1]),
        sum_scratch(cuts[1]),
        [VMEM] * 11,
        [wu, wo, bg_own, *own, x_other, low_other, cr_other, g_other],
        "far_sums",
    )
    other = [x_other, gg_other, cr_other, ht_other]
    far_parts = [far]
    for i in range(1, n_cuts):
        far_parts.append(
            call(
                functools.partial(far_more_kernel, FAR, cuts[i]),
                slab_outs(cuts[i + 1] - cuts[i]),
                sum_scratch(cuts[i + 1] - cuts[i]),
                [VMEM] * 9,
                [*own, *other, bias_sum],
                "far_sums_more",
            )
        )
    rounded, fars = [], []
    for i, (send, keep) in enumerate(far_parts):
        rounded += call(
            functools.partial(round_kernel, (cuts[i + 1] - cuts[i]) // SLAB),
            [sds(send.shape, BF16)],
            [],
            [VMEM] * 2,
            [keep, across(send, "shard", 1)],
            "far_round",
            cost=1,
        )
        fars.append(across(rounded[-1], "shard", FAR))
    (near_send, near_keep) = call(
        near_kernel,
        [sds((block, width), BF16), sds((block, width), F32)],
        sum_scratch(width),
        [VMEM] * 8,
        [*own, *other[:3], after(ht_other, *rounded)],
        "near_sums",
        cost=1,
    )
    near_other = across(near_send, "shard", 1)
    grad_inputs = call(
        functools.partial(inputs_kernel, n_tower),
        [sds((top_rows, width), BF16)] * n_tower,
        [pltpu.VMEM((n, width), BF16)],
        [VMEM] * 3,
        [wd, gh_own, after(direct, *rounded)],
        "grad_inputs",
    )
    returned = [grad_inputs[0]]
    for k in range(1, n_tower):
        piece = grad_inputs[k]
        returned.append(across(piece, "tower", k))
    (feature_grad,) = call(
        functools.partial(place_kernel, n_tower),
        [sds((top_rows, n_tower * width), BF16)],
        [],
        [SMEM] + [VMEM] * n_tower,
        [assign, *returned],
        "place_features",
        cost=1,
    )
    results = []
    for i, far in enumerate(fars):
        cut = cuts[i + 1] - cuts[i]
        results = call(
            functools.partial(final_kernel, 1.0 / math.sqrt(n * n_shard), cuts[i]),
            [sds((block, width), F32), row],
            [
                pltpu.VMEM((block, cut), F32),
                pltpu.VMEM((1, cut), F32),
                pltpu.SemaphoreType.DMA((cut // SLAB + 1,)),
            ],
            [VMEM] * 4 + [HBM] * len(results),
            [near_keep, near_other, rounded[i], far, *results],
            "add_up",
            out_space=HBM,
            aliases={4 + j: j for j in range(len(results))},
        )
    weight_grad, bias_grad = results
    return feature_grad, weight_grad[None], bias_grad


def general_body(out_grad, pooled, down_proj, up_proj, cross_bias, out_proj, assign):
    grad_out = lax.all_to_all(out_grad, "tower", split_axis=1, concat_axis=0, tiled=True)
    feature_in = pooled[0]
    w_down, w_up, w_out = down_proj[0], up_proj[0], out_proj[0]
    hidden_low = mm(feature_in, w_down).astype(BF16)
    factor = mm(hidden_low, w_up) + cross_bias + 1.0
    crossed = (feature_in * factor).astype(BF16)
    grad_crossed = mm_nt(grad_out, w_out).astype(BF16)
    grad_gate = grad_crossed.astype(F32) * feature_in
    grad_gate_low = grad_gate.astype(BF16)
    grad_hidden = mm_nt(grad_gate_low, w_up).astype(BF16)
    grad_inputs = (grad_crossed.astype(F32) * factor + mm_nt(grad_hidden, w_down)).astype(BF16)
    returned = lax.all_to_all(grad_inputs, "tower", split_axis=0, concat_axis=1, tiled=True)
    local_rows = returned.shape[0]
    blocks = returned.reshape(local_rows, -1, EMB)
    feature_grad = jnp.take(blocks, jnp.argsort(assign), axis=1).reshape(local_rows, -1)
    stacked = jnp.concatenate(
        [
            mm(grad_hidden.T, feature_in),
            mm(hidden_low.T, grad_gate_low),
            mm(grad_out.T, crossed),
        ],
        axis=0,
    )
    scale = 1.0 / math.sqrt(grad_out.shape[0] * lax.axis_size("shard"))
    summed = lax.psum_scatter(stacked, "shard", scatter_dimension=0, tiled=True)
    bias_grad = lax.psum(jnp.sum(grad_gate, axis=0), "shard")[None]
    return feature_grad, (summed * scale)[None], bias_grad


def solution(mesh):
    n_tower, n_shard = mesh.shape["tower"], mesh.shape["shard"]
    placed = (
        P(("tower", "shard"), None),
        P("tower", "shard", None),
        P("tower", None, None),
        P("tower", None, None),
        P("tower", None),
        P("tower", None, None),
        P(),
    )

    paired = n_shard == 2 * 4 and n_tower & (n_tower - 1) == 0
    return jax.shard_map(
        paired_body if paired else general_body,
        mesh=mesh,
        in_specs=placed,
        out_specs=(P(("tower", "shard"), None), P("tower", "shard", None), P("tower", None)),
        check_vma=False,
    )
```

```python
import functools
import math

import jax
import jax.numpy as jnp
from jax import lax
from jax.experimental import pallas as pl
from jax.experimental.pallas import tpu as pltpu
from jax.sharding import PartitionSpec as P

EMB = 128
SLAB = 256
TILE = 16
MIB = 1024 * 1024
VM = 48
COST = 10**10
C1 = 1
P2 = 2
PN = 4
CN = 10**9
C2 = 10**9
C3 = 1
C4 = 1
VMEM_LIMIT = 24 * MIB
BF16 = jnp.bfloat16
F32 = jnp.float32
HBM, VMEM, SMEM = pltpu.HBM, pltpu.VMEM, pltpu.SMEM


def mm(a, b):
    return jnp.dot(a, b, preferred_element_type=F32)


def mm_nt(a, b):
    return lax.dot_general(a, b, (((1,), (1,)), ((), ())), preferred_element_type=F32)


def call(kernel, outs, scratch, spaces, args, name, vmem=VMEM_LIMIT, cost=COST, out_space=None, aliases={}):
    return pl.pallas_call(
        kernel,
        out_shape=outs,
        in_specs=[pl.BlockSpec(memory_space=space) for space in spaces],
        out_specs=[pl.BlockSpec(memory_space=out_space or VMEM)] * len(outs),
        input_output_aliases=aliases,
        scratch_shapes=scratch,
        compiler_params=pltpu.CompilerParams(vmem_limit_bytes=vmem),
        cost_estimate=pl.CostEstimate(flops=cost, bytes_accessed=1, transcendentals=0),
        name=name,
    )(*args)


def column_chunks(width):
    step = 512 if width % 512 == 0 else width
    return [slice(c, c + step) for c in range(0, width, step)]


def copy_all(pairs, sem_ref):
    copies = [pltpu.make_async_copy(a, b, sem_ref.at[i]) for i, (a, b) in enumerate(pairs)]
    for copy in copies:
        copy.start()
    return copies


def cut_kernel(n_tower, grad_ref, *refs):
    pieces, sem_ref = refs[:n_tower], refs[n_tower]
    me = lax.axis_index("tower")
    out = pieces[0].shape[1]
    pairs = [
        (grad_ref.at[:, pl.ds(pl.multiple_of((me ^ k) * out, out), out)], piece)
        for k, piece in enumerate(pieces)
    ]
    for copy in copy_all(pairs, sem_ref):
        copy.wait()


def forward_rows(x_ref, wd_ref, wu_ref, bias_ref, low_ref, cr_ref, factor_ref=None, ready=None):
    low = mm(x_ref[...], wd_ref[...]).astype(BF16)
    low_ref[...] = low
    if ready is not None:
        ready.wait()
    for c in column_chunks(x_ref.shape[1]):
        factor = (mm(low, wu_ref[:, c]) + bias_ref[:, c]) + 1.0
        cr_ref[:, c] = (x_ref[:, c].astype(F32) * factor).astype(BF16)
        if factor_ref is not None:
            factor_ref[:, c] = factor


def forward_inner_kernel(x_ref, wd_ref, wu_ref, bias_ref, low_ref, cr_ref):
    outer = is_outer()

    @pl.when(outer)
    def _():
        low_ref[...] = jnp.zeros_like(low_ref)
        cr_ref[...] = jnp.zeros_like(cr_ref)

    @pl.when(jnp.logical_not(outer))
    def _():
        forward_rows(x_ref, wd_ref, wu_ref, bias_ref, low_ref, cr_ref)


def backward_rows(x_ref, g, low_ref, wu_ref, wo_ref, gg_ref, bg_ref, ht_ref, factor_ref, direct_ref):
    rank = wu_ref.shape[0]
    grad_hidden = jnp.zeros((x_ref.shape[0], rank), F32)
    for c in column_chunks(x_ref.shape[1]):
        x = x_ref[:, c].astype(F32)
        grad_crossed = mm_nt(g, wo_ref[c, :]).astype(BF16).astype(F32)
        grad_gate = grad_crossed * x
        bg_ref[:, c] = jnp.sum(grad_gate, axis=0, keepdims=True)
        low = grad_gate.astype(BF16)
        gg_ref[:, c] = low
        grad_hidden += mm_nt(low, wu_ref[:, c])
        if direct_ref is not None:
            direct_ref[:, c] = grad_crossed * factor_ref[:, c]
    grad_hidden = grad_hidden.astype(BF16)
    ht_ref[0:rank, :] = grad_hidden.T
    ht_ref[rank : 2 * rank, :] = low_ref[...].T
    ht_ref[2 * rank :, :] = g.T
    return grad_hidden


def forward_kernel(wd_hbm, wu_hbm, wo_hbm, x_hbm, bias_ref, wd_ref, wu_ref, wo_ref, x_ref, low_ref, cr_ref, factor_ref, sem_ref):
    copies = copy_all([(x_hbm, x_ref), (wd_hbm, wd_ref), (wu_hbm, wu_ref), (wo_hbm, wo_ref)], sem_ref)
    copies[0].wait()
    copies[1].wait()
    forward_rows(x_ref, wd_ref, wu_ref, bias_ref, low_ref, cr_ref, factor_ref, copies[2])
    copies[3].wait()


def backward_kernel(n_tower, wu_ref, wo_ref, x_ref, low_ref, factor_ref, *refs):
    pieces = refs[:n_tower]
    g_ref, gh_ref, ht_ref, gg_ref, bg_ref, direct_ref = refs[n_tower:]
    me = lax.axis_index("tower")
    rows = pieces[0].shape[0]
    for k, piece in enumerate(pieces):
        g_ref[pl.ds(pl.multiple_of((me ^ k) * rows, rows), rows), :] = piece[...]
    gh_ref[...] = backward_rows(
        x_ref, g_ref[...], low_ref, wu_ref, wo_ref, gg_ref, bg_ref, ht_ref, factor_ref, direct_ref
    )


def inputs_kernel(n_tower, wd_ref, gh_ref, direct_ref, *refs):
    pieces, gi_ref = refs[:n_tower], refs[n_tower]
    me = lax.axis_index("tower")
    rows = pieces[0].shape[0]
    grad_hidden = gh_ref[...]
    for c in column_chunks(gi_ref.shape[1]):
        gi_ref[:, c] = (direct_ref[:, c] + mm_nt(grad_hidden, wd_ref[c, :])).astype(BF16)
    for k, piece in enumerate(pieces):
        piece[...] = gi_ref[pl.ds(pl.multiple_of((me ^ k) * rows, rows), rows), :]


def products(flip, start, blocks, lhs_ref, acc_ref):
    shard = lax.axis_index("shard") ^ flip
    block = acc_ref.shape[0] // 2
    rank = blocks[0][3].shape[0] // 3
    n = blocks[0][3].shape[1]
    core = lax.rem(shard, 2)
    first = (shard - core) * block
    picked = pl.ds(pl.multiple_of(first, 2 * block), 2 * block)
    for i, rows in enumerate(blocks):
        lhs_ref[:, i * n : (i + 1) * n] = rows[3][picked, :]
    acc_ref[...] = jnp.zeros_like(acc_ref)
    for part in range(3):

        @pl.when((first < (part + 1) * rank) & (first + 2 * block > part * rank))
        def _():
            at = first + lax.broadcasted_iota(jnp.int32, lhs_ref.shape, 0)
            inside = (at >= part * rank) & (at < (part + 1) * rank)
            lhs = jnp.where(inside, lhs_ref[...].astype(F32), 0.0).astype(BF16)
            for c in column_chunks(acc_ref.shape[1]):
                at_c = slice(start + c.start, start + c.stop)
                rhs = [rows[part][:, at_c] for rows in blocks]
                acc_ref[:, c] += mm(lhs, jnp.concatenate(rhs, axis=0))

    theirs = pl.ds(pl.multiple_of((1 - core) * block, block), block)
    ours = pl.ds(pl.multiple_of(core * block, block), block)
    return theirs, ours


def bias_rows(bias):
    high = bias.astype(BF16).astype(F32)
    rest = bias - high
    slabs = [slice(c, c + SLAB) for c in range(0, bias.shape[1], SLAB)]
    filler = [jnp.zeros((1, SLAB), F32)] * (TILE - 2 * len(slabs))
    return jnp.concatenate([high[:, c] for c in slabs] + [rest[:, c] for c in slabs] + filler, axis=0)


def bias_of(rows, n_slabs):
    return jnp.concatenate([rows[j : j + 1] + rows[n_slabs + j : n_slabs + j + 1] for j in range(n_slabs)], axis=1)


def is_outer():
    chip = lax.div(lax.axis_index("shard"), 2)
    return (chip == 0) | (chip == lax.div(lax.axis_size("shard"), 2) - 1)


def store_slabs(acc_ref, theirs, ours, biases, send_refs, keep_ref):
    block = acc_ref.shape[0] // 2
    n_slabs = acc_ref.shape[1] // SLAB
    each = n_slabs // len(send_refs)
    for j in range(n_slabs):
        c, at = slice(j * SLAB, (j + 1) * SLAB), j % each * block
        send_refs[j // each][at : at + block, :] = acc_ref[theirs, c].astype(BF16)
        keep_ref[j * block : (j + 1) * block, :] = acc_ref[ours, c]
    for i, bias in enumerate(biases):
        low = bias_rows(bias).astype(BF16)
        at = each * block + i * TILE
        send_refs[-1][at : at + TILE, :] = low
        at = n_slabs * block + i * TILE
        keep_ref[at : at + TILE, :] = low.astype(F32)


def first_kernel(x_own, gg_own, cr_own, ht_own, bg_own, keep_ref, *refs):
    send_refs, (lhs_ref, acc_ref) = refs[:-2], refs[-2:]
    outer = is_outer()

    @pl.when(outer)
    def _():
        theirs, ours = products(6, 0, [(x_own, gg_own, cr_own, ht_own)], lhs_ref, acc_ref)
        store_slabs(acc_ref, theirs, ours, [bg_own[...]], send_refs, keep_ref)

    @pl.when(jnp.logical_not(outer))
    def _():
        for ref in (*send_refs, keep_ref):
            ref[...] = jnp.zeros_like(ref)


def second_kernel(wu_ref, wo_ref, bg_own, x_own, gg_own, cr_own, ht_own, x_ref, low_ref, cr_ref, g_ref, *refs):
    gg_ref, ht_ref, bg_ref, keep_ref = refs[:4]
    send_refs, (lhs_ref, acc_ref) = refs[4:-2], refs[-2:]
    outer = is_outer()

    @pl.when(outer)
    def _():
        for ref in (gg_ref, bg_ref, ht_ref):
            ref[...] = jnp.zeros_like(ref)
        theirs, ours = products(4, 0, [(x_own, gg_own, cr_own, ht_own)], lhs_ref, acc_ref)
        store_slabs(acc_ref, theirs, ours, [bg_own[...]], send_refs, keep_ref)

    @pl.when(jnp.logical_not(outer))
    def _():
        backward_rows(x_ref, g_ref[...], low_ref, wu_ref, wo_ref, gg_ref, bg_ref, ht_ref, None, None)
        theirs, ours = products(2, 0, [(x_ref, gg_ref, cr_ref, ht_ref)], lhs_ref, acc_ref)
        store_slabs(acc_ref, theirs, ours, [bg_ref[...]], send_refs, keep_ref)


def near_kernel(wu_ref, wo_ref, x_ref, low_ref, cr_ref, g_ref, *refs):
    own, inner, bg_own, bg_inner, first_ref, keep_ref = refs[:4], refs[4:8], *refs[8:12]
    send_refs, (gg_ref, ht_ref, bg_ref, lhs_ref, acc_ref) = refs[12:-5], refs[-5:]
    backward_rows(x_ref, g_ref[...], low_ref, wu_ref, wo_ref, gg_ref, bg_ref, ht_ref, None, None)
    theirs, ours = products(0, 0, [own, (x_ref, gg_ref, cr_ref, ht_ref), inner], lhs_ref, acc_ref)
    store_slabs(acc_ref, theirs, ours, [bg_own[...], bg_ref[...], bg_inner[...]], send_refs, keep_ref)
    sums = slice(0, first_ref.shape[0] - TILE)
    keep_ref[sums, :] += first_ref[sums, :].astype(F32)


def joined_bias(rows, n_slabs):
    return bias_rows(bias_of(rows, n_slabs)).astype(BF16)


def round_kernel(n_slabs, keep_ref, *refs):
    recv_refs, out_ref = refs[:-1], refs[-1]
    at = 0
    for recv_ref in recv_refs:
        rows = slice(at, at + recv_ref.shape[0])
        out_ref[rows, :] = (keep_ref[rows, :] + recv_ref[...].astype(F32)).astype(BF16)
        at = rows.stop
    out_ref[-TILE:, :] = joined_bias(keep_ref[-TILE:, :] + recv_refs[-1][-TILE:, :].astype(F32), n_slabs)


def final_kernel(scale, keep_ref, first_ref, second_ref, *refs):
    near_refs, (out_ref, bg_out, total_ref, bg_ref, sem_ref) = refs[:-5], refs[-5:]
    each = total_ref.shape[1] // SLAB // len(near_refs)
    block, width = total_ref.shape
    n_slabs = width // SLAB
    copies = []

    def write(source, target, i):
        copies.append(pltpu.make_async_copy(source, target, sem_ref.at[i]))
        copies[-1].start()

    for j in range(n_slabs):
        c, rows = slice(j * SLAB, (j + 1) * SLAB), slice(j * block, (j + 1) * block)
        at = j % each * block
        total = keep_ref[rows, :] + near_refs[j // each][at : at + block, :].astype(F32)
        total = total + second_ref[rows, :].astype(F32)
        total_ref[:, c] = total * scale
        write(total_ref.at[:, pl.ds(j * SLAB, SLAB)], out_ref.at[:, pl.ds(j * SLAB, SLAB)], j)
    here = []
    for i in range(3):
        rows = slice(n_slabs * block + i * TILE, n_slabs * block + (i + 1) * TILE)
        at = each * block + i * TILE
        joined = joined_bias(keep_ref[rows, :] + near_refs[-1][at : at + TILE, :].astype(F32), n_slabs)
        here.append(bias_of(joined.astype(F32), n_slabs))
    there = [bias_of(ref[-TILE:, :].astype(F32), n_slabs) for ref in (first_ref, second_ref)]
    bg_ref[...] = (here[0] + here[1]) + ((here[2] + there[0]) + there[1])
    write(bg_ref, bg_out, n_slabs)
    for copy in copies:
        copy.wait()


def place_kernel(n_tower, assign_ref, *refs):
    pieces, out_ref = refs[:n_tower], refs[n_tower]
    me = lax.axis_index("tower")
    slots = pieces[0].shape[1] // EMB
    for k in range(n_tower):
        for j in range(slots):
            at = assign_ref[(me ^ k) * slots + j] * EMB
            out_ref[:, pl.ds(pl.multiple_of(at, EMB), EMB)] = pieces[k][:, j * EMB : (j + 1) * EMB]


def xor_pairs(n, k):
    return [(i, i ^ k) for i in range(n)]


def after(value, *earlier):
    return lax.optimization_barrier((value, *earlier))[0]


def paired_body(out_grad, pooled, down_proj, up_proj, cross_bias, out_proj, assign):
    n_tower, n_shard = lax.axis_size("tower"), lax.axis_size("shard")
    sds = jax.ShapeDtypeStruct
    w_down, w_up, w_out, x = down_proj[0], up_proj[0], out_proj[0], pooled[0]
    n, width = x.shape
    rank, out = w_up.shape[0], w_out.shape[1]
    stack = 2 * rank + out
    block = stack // n_shard
    top_rows = out_grad.shape[0]
    wide = sds((n, width), BF16)
    tall = sds((stack, n), BF16)
    low = sds((n, rank), BF16)
    row = sds((1, width), F32)
    slab_rows = block * width // SLAB

    def across(value, axis, k):
        return lax.ppermute(value, axis, xor_pairs(lax.axis_size(axis), k))

    def slab_outs(n_bias, pieces):
        rows = [slab_rows // pieces] * pieces
        rows[-1] += n_bias * TILE
        return [sds((sum(rows), SLAB), F32)] + [sds((r, SLAB), BF16) for r in rows]

    def sum_scratch(n_blocks):
        return [pltpu.VMEM((2 * block, n_blocks * n), BF16), pltpu.VMEM((2 * block, width), F32)]

    def rounded(keep, *sends):
        (out,) = call(
            functools.partial(round_kernel, width // SLAB),
            [sds(keep.shape, BF16)],
            [],
            [VMEM] * (1 + len(sends)),
            [keep] + [across(send, "shard", 1) for send in sends],
            "join_cores",
            cost=1,
        )
        return out

    inside = [2 <= i < n_shard - 2 for i in range(n_shard)]
    inner = [(i, i ^ 6 if inside[i] else i ^ 1) for i in range(n_shard)]
    outer = [(i, i ^ 1 if inside[i] else i ^ 6) for i in range(n_shard)]
    second = [(i, i ^ 2 if inside[i] else i ^ 4) for i in range(n_shard)]

    x_other = across(x, "shard", 2)
    x_inner = lax.ppermute(x, "shard", inner)
    pieces = call(
        functools.partial(cut_kernel, n_tower),
        [sds((top_rows, out), BF16)] * n_tower,
        [pltpu.SemaphoreType.DMA((n_tower,))],
        [HBM],
        [out_grad],
        "cut_columns",
        48 * MIB,
        1,
    )
    pieces = [pieces[0]] + [across(pieces[k], "tower", k) for k in range(1, n_tower)]
    wd, wu, wo, x_own, low_own, cr_own, factor = call(
        forward_kernel,
        [sds(w.shape, BF16) for w in (w_down, w_up, w_out)] + [wide, low, wide, sds((n, width), F32)],
        [pltpu.SemaphoreType.DMA((4,))],
        [HBM] * 4 + [VMEM],
        [w_down, w_up, w_out, x, cross_bias],
        "forward_own",
        VM * MIB,
        1,
    )
    g_own, gh_own, ht_own, gg_own, bg_own, direct = call(
        functools.partial(backward_kernel, n_tower),
        [sds((n, out), BF16), low, tall, wide, row, sds((n, width), F32)],
        [],
        [VMEM] * (5 + n_tower),
        [wu, wo, x_own, low_own, factor, *pieces],
        "backward_own",
        cost=1,
    )
    own = [x_own, gg_own, cr_own, ht_own]
    g_inner = lax.ppermute(g_own, "shard", inner)
    g_other = across(g_own, "shard", 2)
    first = rounded(
        *call(first_kernel, slab_outs(1, 1), sum_scratch(1), [VMEM] * 5, [*own, bg_own], "first_sums", cost=C1)
    )
    from_first = lax.ppermute(first, "shard", outer)
    low_inner, cr_inner = call(
        forward_inner_kernel, [low, wide], [], [VMEM] * 4, [after(x_inner, first), wd, wu, cross_bias], "forward_inner", cost=C2
    )
    low_other, cr_other = call(
        forward_rows, [low, wide], [], [VMEM] * 4, [after(x_other, low_inner, g_other), wd, wu, cross_bias], "forward_other", cost=C2
    )
    gg_inner, ht_inner, bg_inner, *sums = call(
        second_kernel,
        [wide, tall, row] + slab_outs(1, P2),
        sum_scratch(1),
        [VMEM] * 11,
        [wu, wo, bg_own, *own, x_inner, after(low_inner, low_other), cr_inner, g_inner],
        "second_sums",
        cost=C2,
    )
    second_sum = rounded(*sums)
    from_second = lax.ppermute(second_sum, "shard", second)
    grad_inputs = call(
        functools.partial(inputs_kernel, n_tower),
        [sds((top_rows, width), BF16)] * n_tower,
        [pltpu.VMEM((n, width), BF16)],
        [VMEM] * 3,
        [wd, gh_own, after(direct, second_sum)],
        "grad_inputs",
        cost=C4,
    )
    near_keep, *near_sends = call(
        near_kernel,
        slab_outs(3, PN),
        [pltpu.VMEM((n, width), BF16), pltpu.VMEM((stack, n), BF16), pltpu.VMEM((1, width), F32)] + sum_scratch(3),
        [VMEM] * 17,
        [wu, wo, x_other, after(low_other, *grad_inputs), cr_other, g_other, *own, x_inner, gg_inner, cr_inner, ht_inner, bg_own, bg_inner, from_first],
        "near_sums",
        cost=CN,
    )
    near_others = [across(send, "shard", 1) for send in near_sends]
    returned = [grad_inputs[0]]
    for k in range(1, n_tower):
        piece = grad_inputs[k]
        returned.append(across(piece, "tower", k))
    (feature_grad,) = call(
        functools.partial(place_kernel, n_tower),
        [sds((top_rows, n_tower * width), BF16)],
        [],
        [SMEM] + [VMEM] * n_tower,
        [assign, *returned],
        "place_features",
        cost=1,
    )
    weight_grad, bias_grad = call(
        functools.partial(final_kernel, 1.0 / math.sqrt(n * n_shard)),
        [sds((block, width), F32), row],
        [
            pltpu.VMEM((block, width), F32),
            pltpu.VMEM((1, width), F32),
            pltpu.SemaphoreType.DMA((width // SLAB + 1,)),
        ],
        [VMEM] * (3 + len(near_others)),
        [near_keep, from_first, from_second, *near_others],
        "add_up",
        out_space=HBM,
    )
    return feature_grad, weight_grad[None], bias_grad


def general_body(out_grad, pooled, down_proj, up_proj, cross_bias, out_proj, assign):
    grad_out = lax.all_to_all(out_grad, "tower", split_axis=1, concat_axis=0, tiled=True)
    feature_in = pooled[0]
    w_down, w_up, w_out = down_proj[0], up_proj[0], out_proj[0]
    hidden_low = mm(feature_in, w_down).astype(BF16)
    factor = mm(hidden_low, w_up) + cross_bias + 1.0
    crossed = (feature_in * factor).astype(BF16)
    grad_crossed = mm_nt(grad_out, w_out).astype(BF16)
    grad_gate = grad_crossed.astype(F32) * feature_in
    grad_gate_low = grad_gate.astype(BF16)
    grad_hidden = mm_nt(grad_gate_low, w_up).astype(BF16)
    grad_inputs = (grad_crossed.astype(F32) * factor + mm_nt(grad_hidden, w_down)).astype(BF16)
    returned = lax.all_to_all(grad_inputs, "tower", split_axis=0, concat_axis=1, tiled=True)
    local_rows = returned.shape[0]
    blocks = returned.reshape(local_rows, -1, EMB)
    feature_grad = jnp.take(blocks, jnp.argsort(assign), axis=1).reshape(local_rows, -1)
    stacked = jnp.concatenate(
        [
            mm(grad_hidden.T, feature_in),
            mm(hidden_low.T, grad_gate_low),
            mm(grad_out.T, crossed),
        ],
        axis=0,
    )
    scale = 1.0 / math.sqrt(grad_out.shape[0] * lax.axis_size("shard"))
    summed = lax.psum_scatter(stacked, "shard", scatter_dimension=0, tiled=True)
    bias_grad = lax.psum(jnp.sum(grad_gate, axis=0), "shard")[None]
    return feature_grad, (summed * scale)[None], bias_grad


def solution(mesh):
    n_tower, n_shard = mesh.shape["tower"], mesh.shape["shard"]
    placed = (
        P(("tower", "shard"), None),
        P("tower", "shard", None),
        P("tower", None, None),
        P("tower", None, None),
        P("tower", None),
        P("tower", None, None),
        P(),
    )

    paired = n_shard == 2 * 4 and n_tower & (n_tower - 1) == 0
    return jax.shard_map(
        paired_body if paired else general_body,
        mesh=mesh,
        in_specs=placed,
        out_specs=(P(("tower", "shard"), None), P("tower", "shard", None), P("tower", None)),
        check_vma=False,
    )
```

```python
import functools
import math

import jax
import jax.numpy as jnp
from jax import lax
from jax.experimental import pallas as pl
from jax.experimental.pallas import tpu as pltpu
from jax.sharding import PartitionSpec as P

EMB = 128
SLAB = 256
TILE = 16
MIB = 1024 * 1024
VM = 48
COST = 10**10
C1 = 1
P2 = 2
PN = 4
CN = 10**9
C2 = 10**9
C3 = 1
C4 = 1
VMEM_LIMIT = 24 * MIB
BF16 = jnp.bfloat16
F32 = jnp.float32
HBM, VMEM, SMEM = pltpu.HBM, pltpu.VMEM, pltpu.SMEM


def mm(a, b):
    return jnp.dot(a, b, preferred_element_type=F32)


def mm_nt(a, b):
    return lax.dot_general(a, b, (((1,), (1,)), ((), ())), preferred_element_type=F32)


def call(kernel, outs, scratch, spaces, args, name, vmem=VMEM_LIMIT, cost=COST, out_space=None, aliases={}):
    return pl.pallas_call(
        kernel,
        out_shape=outs,
        in_specs=[pl.BlockSpec(memory_space=space) for space in spaces],
        out_specs=[pl.BlockSpec(memory_space=out_space or VMEM)] * len(outs),
        input_output_aliases=aliases,
        scratch_shapes=scratch,
        compiler_params=pltpu.CompilerParams(vmem_limit_bytes=vmem),
        cost_estimate=pl.CostEstimate(flops=cost, bytes_accessed=1, transcendentals=0),
        name=name,
    )(*args)


def column_chunks(width):
    step = 512 if width % 512 == 0 else width
    return [slice(c, c + step) for c in range(0, width, step)]


def copy_all(pairs, sem_ref):
    copies = [pltpu.make_async_copy(a, b, sem_ref.at[i]) for i, (a, b) in enumerate(pairs)]
    for copy in copies:
        copy.start()
    return copies


def cut_kernel(n_tower, grad_ref, *refs):
    pieces, sem_ref = refs[:n_tower], refs[n_tower]
    me = lax.axis_index("tower")
    out = pieces[0].shape[1]
    pairs = [
        (grad_ref.at[:, pl.ds(pl.multiple_of((me ^ k) * out, out), out)], piece)
        for k, piece in enumerate(pieces)
    ]
    for copy in copy_all(pairs, sem_ref):
        copy.wait()


def forward_rows(x_ref, wd_ref, wu_ref, bias_ref, low_ref, cr_ref, factor_ref=None, ready=None):
    low = mm(x_ref[...], wd_ref[...]).astype(BF16)
    low_ref[...] = low
    if ready is not None:
        ready.wait()
    for c in column_chunks(x_ref.shape[1]):
        factor = (mm(low, wu_ref[:, c]) + bias_ref[:, c]) + 1.0
        cr_ref[:, c] = (x_ref[:, c].astype(F32) * factor).astype(BF16)
        if factor_ref is not None:
            factor_ref[:, c] = factor


def forward_inner_kernel(x_ref, wd_ref, wu_ref, bias_ref, low_ref, cr_ref):
    outer = is_outer()

    @pl.when(outer)
    def _():
        low_ref[...] = jnp.zeros_like(low_ref)
        cr_ref[...] = jnp.zeros_like(cr_ref)

    @pl.when(jnp.logical_not(outer))
    def _():
        forward_rows(x_ref, wd_ref, wu_ref, bias_ref, low_ref, cr_ref)


def backward_rows(x_ref, g, low_ref, wu_ref, wo_ref, gg_ref, bg_ref, ht_ref, factor_ref, direct_ref):
    rank = wu_ref.shape[0]
    grad_hidden = jnp.zeros((x_ref.shape[0], rank), F32)
    for c in column_chunks(x_ref.shape[1]):
        x = x_ref[:, c].astype(F32)
        grad_crossed = mm_nt(g, wo_ref[c, :]).astype(BF16).astype(F32)
        grad_gate = grad_crossed * x
        bg_ref[:, c] = jnp.sum(grad_gate, axis=0, keepdims=True)
        low = grad_gate.astype(BF16)
        gg_ref[:, c] = low
        grad_hidden += mm_nt(low, wu_ref[:, c])
        if direct_ref is not None:
            direct_ref[:, c] = grad_crossed * factor_ref[:, c]
    grad_hidden = grad_hidden.astype(BF16)
    ht_ref[0:rank, :] = grad_hidden.T
    ht_ref[rank : 2 * rank, :] = low_ref[...].T
    ht_ref[2 * rank :, :] = g.T
    return grad_hidden


def forward_kernel(wd_hbm, wu_hbm, wo_hbm, x_hbm, bias_ref, wd_ref, wu_ref, wo_ref, x_ref, low_ref, cr_ref, factor_ref, sem_ref):
    copies = copy_all([(x_hbm, x_ref), (wd_hbm, wd_ref), (wu_hbm, wu_ref), (wo_hbm, wo_ref)], sem_ref)
    copies[0].wait()
    copies[1].wait()
    forward_rows(x_ref, wd_ref, wu_ref, bias_ref, low_ref, cr_ref, factor_ref, copies[2])
    copies[3].wait()


def backward_kernel(n_tower, wu_ref, wo_ref, x_ref, low_ref, factor_ref, *refs):
    pieces = refs[:n_tower]
    g_ref, gh_ref, ht_ref, gg_ref, bg_ref, direct_ref = refs[n_tower:]
    me = lax.axis_index("tower")
    rows = pieces[0].shape[0]
    for k, piece in zip(range(len(pieces) - 1, -1, -1), pieces):
        g_ref[pl.ds(pl.multiple_of((me ^ k) * rows, rows), rows), :] = piece[...]
    gh_ref[...] = backward_rows(
        x_ref, g_ref[...], low_ref, wu_ref, wo_ref, gg_ref, bg_ref, ht_ref, factor_ref, direct_ref
    )


def inputs_kernel(n_tower, wd_ref, gh_ref, direct_ref, *refs):
    pieces, gi_ref = refs[:n_tower], refs[n_tower]
    me = lax.axis_index("tower")
    rows = pieces[0].shape[0]
    grad_hidden = gh_ref[...]
    for c in column_chunks(gi_ref.shape[1]):
        gi_ref[:, c] = (direct_ref[:, c] + mm_nt(grad_hidden, wd_ref[c, :])).astype(BF16)
    for k, piece in enumerate(pieces):
        piece[...] = gi_ref[pl.ds(pl.multiple_of((me ^ k) * rows, rows), rows), :]


def products(flip, start, blocks, lhs_ref, acc_ref):
    shard = lax.axis_index("shard") ^ flip
    block = acc_ref.shape[0] // 2
    rank = blocks[0][3].shape[0] // 3
    n = blocks[0][3].shape[1]
    core = lax.rem(shard, 2)
    first = (shard - core) * block
    picked = pl.ds(pl.multiple_of(first, 2 * block), 2 * block)
    for i, rows in enumerate(blocks):
        lhs_ref[:, i * n : (i + 1) * n] = rows[3][picked, :]
    acc_ref[...] = jnp.zeros_like(acc_ref)
    for part in range(3):

        @pl.when((first < (part + 1) * rank) & (first + 2 * block > part * rank))
        def _():
            at = first + lax.broadcasted_iota(jnp.int32, lhs_ref.shape, 0)
            inside = (at >= part * rank) & (at < (part + 1) * rank)
            lhs = jnp.where(inside, lhs_ref[...].astype(F32), 0.0).astype(BF16)
            for c in column_chunks(acc_ref.shape[1]):
                at_c = slice(start + c.start, start + c.stop)
                rhs = [rows[part][:, at_c] for rows in blocks]
                acc_ref[:, c] += mm(lhs, jnp.concatenate(rhs, axis=0))

    theirs = pl.ds(pl.multiple_of((1 - core) * block, block), block)
    ours = pl.ds(pl.multiple_of(core * block, block), block)
    return theirs, ours


def bias_rows(bias):
    high = bias.astype(BF16).astype(F32)
    rest = bias - high
    slabs = [slice(c, c + SLAB) for c in range(0, bias.shape[1], SLAB)]
    filler = [jnp.zeros((1, SLAB), F32)] * (TILE - 2 * len(slabs))
    return jnp.concatenate([high[:, c] for c in slabs] + [rest[:, c] for c in slabs] + filler, axis=0)


def bias_of(rows, n_slabs):
    return jnp.concatenate([rows[j : j + 1] + rows[n_slabs + j : n_slabs + j + 1] for j in range(n_slabs)], axis=1)


def is_outer():
    chip = lax.div(lax.axis_index("shard"), 2)
    return (chip == 0) | (chip == lax.div(lax.axis_size("shard"), 2) - 1)


def store_slabs(acc_ref, theirs, ours, biases, send_refs, keep_ref):
    block = acc_ref.shape[0] // 2
    n_slabs = acc_ref.shape[1] // SLAB
    each = n_slabs // len(send_refs)
    for j in range(n_slabs):
        c, at = slice(j * SLAB, (j + 1) * SLAB), j % each * block
        send_refs[j // each][at : at + block, :] = acc_ref[theirs, c].astype(BF16)
        keep_ref[j * block : (j + 1) * block, :] = acc_ref[ours, c]
    for i, bias in enumerate(biases):
        low = bias_rows(bias).astype(BF16)
        at = each * block + i * TILE
        send_refs[-1][at : at + TILE, :] = low
        at = n_slabs * block + i * TILE
        keep_ref[at : at + TILE, :] = low.astype(F32)


def first_kernel(x_own, gg_own, cr_own, ht_own, bg_own, keep_ref, *refs):
    send_refs, (lhs_ref, acc_ref) = refs[:-2], refs[-2:]
    outer = is_outer()

    @pl.when(outer)
    def _():
        theirs, ours = products(6, 0, [(x_own, gg_own, cr_own, ht_own)], lhs_ref, acc_ref)
        store_slabs(acc_ref, theirs, ours, [bg_own[...]], send_refs, keep_ref)

    @pl.when(jnp.logical_not(outer))
    def _():
        for ref in (*send_refs, keep_ref):
            ref[...] = jnp.zeros_like(ref)


def second_kernel(wu_ref, wo_ref, bg_own, x_own, gg_own, cr_own, ht_own, x_ref, low_ref, cr_ref, g_ref, *refs):
    gg_ref, ht_ref, bg_ref, keep_ref = refs[:4]
    send_refs, (lhs_ref, acc_ref) = refs[4:-2], refs[-2:]
    outer = is_outer()

    @pl.when(outer)
    def _():
        for ref in (gg_ref, bg_ref, ht_ref):
            ref[...] = jnp.zeros_like(ref)
        theirs, ours = products(4, 0, [(x_own, gg_own, cr_own, ht_own)], lhs_ref, acc_ref)
        store_slabs(acc_ref, theirs, ours, [bg_own[...]], send_refs, keep_ref)

    @pl.when(jnp.logical_not(outer))
    def _():
        backward_rows(x_ref, g_ref[...], low_ref, wu_ref, wo_ref, gg_ref, bg_ref, ht_ref, None, None)
        theirs, ours = products(2, 0, [(x_ref, gg_ref, cr_ref, ht_ref)], lhs_ref, acc_ref)
        store_slabs(acc_ref, theirs, ours, [bg_ref[...]], send_refs, keep_ref)


def near_kernel(wu_ref, wo_ref, x_ref, low_ref, cr_ref, g_ref, *refs):
    own, inner, bg_own, bg_inner, first_ref, keep_ref = refs[:4], refs[4:8], *refs[8:12]
    send_refs, (gg_ref, ht_ref, bg_ref, lhs_ref, acc_ref) = refs[12:-5], refs[-5:]
    backward_rows(x_ref, g_ref[...], low_ref, wu_ref, wo_ref, gg_ref, bg_ref, ht_ref, None, None)
    theirs, ours = products(0, 0, [own, (x_ref, gg_ref, cr_ref, ht_ref), inner], lhs_ref, acc_ref)
    store_slabs(acc_ref, theirs, ours, [bg_own[...], bg_ref[...], bg_inner[...]], send_refs, keep_ref)
    sums = slice(0, first_ref.shape[0] - TILE)
    keep_ref[sums, :] += first_ref[sums, :].astype(F32)


def joined_bias(rows, n_slabs):
    return bias_rows(bias_of(rows, n_slabs)).astype(BF16)


def round_kernel(n_slabs, keep_ref, *refs):
    recv_refs, out_ref = refs[:-1], refs[-1]
    at = 0
    for recv_ref in recv_refs:
        rows = slice(at, at + recv_ref.shape[0])
        out_ref[rows, :] = (keep_ref[rows, :] + recv_ref[...].astype(F32)).astype(BF16)
        at = rows.stop
    out_ref[-TILE:, :] = joined_bias(keep_ref[-TILE:, :] + recv_refs[-1][-TILE:, :].astype(F32), n_slabs)


def final_kernel(scale, keep_ref, first_ref, second_ref, *refs):
    near_refs, (out_ref, bg_out, total_ref, bg_ref, sem_ref) = refs[:-5], refs[-5:]
    each = total_ref.shape[1] // SLAB // len(near_refs)
    block, width = total_ref.shape
    n_slabs = width // SLAB
    copies = []

    def write(source, target, i):
        copies.append(pltpu.make_async_copy(source, target, sem_ref.at[i]))
        copies[-1].start()

    for j in range(n_slabs):
        c, rows = slice(j * SLAB, (j + 1) * SLAB), slice(j * block, (j + 1) * block)
        at = j % each * block
        total = keep_ref[rows, :] + near_refs[j // each][at : at + block, :].astype(F32)
        total = total + second_ref[rows, :].astype(F32)
        total_ref[:, c] = total * scale
        write(total_ref.at[:, pl.ds(j * SLAB, SLAB)], out_ref.at[:, pl.ds(j * SLAB, SLAB)], j)
    here = []
    for i in range(3):
        rows = slice(n_slabs * block + i * TILE, n_slabs * block + (i + 1) * TILE)
        at = each * block + i * TILE
        joined = joined_bias(keep_ref[rows, :] + near_refs[-1][at : at + TILE, :].astype(F32), n_slabs)
        here.append(bias_of(joined.astype(F32), n_slabs))
    there = [bias_of(ref[-TILE:, :].astype(F32), n_slabs) for ref in (first_ref, second_ref)]
    bg_ref[...] = (here[0] + here[1]) + ((here[2] + there[0]) + there[1])
    write(bg_ref, bg_out, n_slabs)
    for copy in copies:
        copy.wait()


def place_kernel(n_tower, assign_ref, *refs):
    pieces, out_ref = refs[:n_tower], refs[n_tower]
    me = lax.axis_index("tower")
    slots = pieces[0].shape[1] // EMB
    for k in range(n_tower):
        for j in range(slots):
            at = assign_ref[(me ^ k) * slots + j] * EMB
            out_ref[:, pl.ds(pl.multiple_of(at, EMB), EMB)] = pieces[k][:, j * EMB : (j + 1) * EMB]


def xor_pairs(n, k):
    return [(i, i ^ k) for i in range(n)]


def after(value, *earlier):
    return lax.optimization_barrier((value, *earlier))[0]


def paired_body(out_grad, pooled, down_proj, up_proj, cross_bias, out_proj, assign):
    n_tower, n_shard = lax.axis_size("tower"), lax.axis_size("shard")
    sds = jax.ShapeDtypeStruct
    w_down, w_up, w_out, x = down_proj[0], up_proj[0], out_proj[0], pooled[0]
    n, width = x.shape
    rank, out = w_up.shape[0], w_out.shape[1]
    stack = 2 * rank + out
    block = stack // n_shard
    top_rows = out_grad.shape[0]
    wide = sds((n, width), BF16)
    tall = sds((stack, n), BF16)
    low = sds((n, rank), BF16)
    row = sds((1, width), F32)
    slab_rows = block * width // SLAB

    def across(value, axis, k):
        return lax.ppermute(value, axis, xor_pairs(lax.axis_size(axis), k))

    def slab_outs(n_bias, pieces):
        rows = [slab_rows // pieces] * pieces
        rows[-1] += n_bias * TILE
        return [sds((sum(rows), SLAB), F32)] + [sds((r, SLAB), BF16) for r in rows]

    def sum_scratch(n_blocks):
        return [pltpu.VMEM((2 * block, n_blocks * n), BF16), pltpu.VMEM((2 * block, width), F32)]

    def rounded(keep, *sends):
        (out,) = call(
            functools.partial(round_kernel, width // SLAB),
            [sds(keep.shape, BF16)],
            [],
            [VMEM] * (1 + len(sends)),
            [keep] + [across(send, "shard", 1) for send in sends],
            "join_cores",
            cost=1,
        )
        return out

    inside = [2 <= i < n_shard - 2 for i in range(n_shard)]
    inner = [(i, i ^ 6 if inside[i] else i ^ 1) for i in range(n_shard)]
    outer = [(i, i ^ 1 if inside[i] else i ^ 6) for i in range(n_shard)]
    second = [(i, i ^ 2 if inside[i] else i ^ 4) for i in range(n_shard)]

    x_other = across(x, "shard", 2)
    x_inner = lax.ppermute(x, "shard", inner)
    pieces = call(
        functools.partial(cut_kernel, n_tower),
        [sds((top_rows, out), BF16)] * n_tower,
        [pltpu.SemaphoreType.DMA((n_tower,))],
        [HBM],
        [out_grad],
        "cut_columns",
        48 * MIB,
        10**9,
    )
    received = [across(pieces[k], "tower", k) for k in range(n_tower - 1, 0, -1)]
    pieces = [pieces[0]] + received[::-1]
    wd, wu, wo, x_own, low_own, cr_own, factor = call(
        forward_kernel,
        [sds(w.shape, BF16) for w in (w_down, w_up, w_out)] + [wide, low, wide, sds((n, width), F32)],
        [pltpu.SemaphoreType.DMA((4,))],
        [HBM] * 4 + [VMEM],
        [w_down, w_up, w_out, x, cross_bias],
        "forward_own",
        VM * MIB,
        1,
    )
    g_own, gh_own, ht_own, gg_own, bg_own, direct = call(
        functools.partial(backward_kernel, n_tower),
        [sds((n, out), BF16), low, tall, wide, row, sds((n, width), F32)],
        [],
        [VMEM] * (5 + n_tower),
        [wu, wo, x_own, low_own, factor, *pieces[::-1]],
        "backward_own",
        cost=1,
    )
    own = [x_own, gg_own, cr_own, ht_own]
    g_inner = lax.ppermute(g_own, "shard", inner)
    g_other = across(g_own, "shard", 2)
    first = rounded(
        *call(first_kernel, slab_outs(1, 1), sum_scratch(1), [VMEM] * 5, [*own, bg_own], "first_sums", cost=C1)
    )
    from_first = lax.ppermute(first, "shard", outer)
    low_inner, cr_inner = call(
        forward_inner_kernel, [low, wide], [], [VMEM] * 4, [after(x_inner, first), wd, wu, cross_bias], "forward_inner", cost=C2
    )
    low_other, cr_other = call(
        forward_rows, [low, wide], [], [VMEM] * 4, [after(x_other, low_inner, g_other), wd, wu, cross_bias], "forward_other", cost=C2
    )
    gg_inner, ht_inner, bg_inner, *sums = call(
        second_kernel,
        [wide, tall, row] + slab_outs(1, P2),
        sum_scratch(1),
        [VMEM] * 11,
        [wu, wo, bg_own, *own, x_inner, after(low_inner, low_other), cr_inner, g_inner],
        "second_sums",
        cost=C2,
    )
    second_sum = rounded(*sums)
    from_second = lax.ppermute(second_sum, "shard", second)
    grad_inputs = call(
        functools.partial(inputs_kernel, n_tower),
        [sds((top_rows, width), BF16)] * n_tower,
        [pltpu.VMEM((n, width), BF16)],
        [VMEM] * 3,
        [wd, gh_own, after(direct, second_sum)],
        "grad_inputs",
        cost=C4,
    )
    near_keep, *near_sends = call(
        near_kernel,
        slab_outs(3, PN),
        [pltpu.VMEM((n, width), BF16), pltpu.VMEM((stack, n), BF16), pltpu.VMEM((1, width), F32)] + sum_scratch(3),
        [VMEM] * 17,
        [wu, wo, x_other, after(low_other, *grad_inputs), cr_other, g_other, *own, x_inner, gg_inner, cr_inner, ht_inner, bg_own, bg_inner, from_first],
        "near_sums",
        cost=CN,
    )
    near_others = [across(send, "shard", 1) for send in near_sends]
    returned = [grad_inputs[0]]
    for k in range(1, n_tower):
        piece = grad_inputs[k]
        returned.append(across(piece, "tower", k))
    (feature_grad,) = call(
        functools.partial(place_kernel, n_tower),
        [sds((top_rows, n_tower * width), BF16)],
        [],
        [SMEM] + [VMEM] * n_tower,
        [assign, *returned],
        "place_features",
        cost=1,
    )
    weight_grad, bias_grad = call(
        functools.partial(final_kernel, 1.0 / math.sqrt(n * n_shard)),
        [sds((block, width), F32), row],
        [
            pltpu.VMEM((block, width), F32),
            pltpu.VMEM((1, width), F32),
            pltpu.SemaphoreType.DMA((width // SLAB + 1,)),
        ],
        [VMEM] * (3 + len(near_others)),
        [near_keep, from_first, from_second, *near_others],
        "add_up",
        out_space=HBM,
    )
    return feature_grad, weight_grad[None], bias_grad


def general_body(out_grad, pooled, down_proj, up_proj, cross_bias, out_proj, assign):
    grad_out = lax.all_to_all(out_grad, "tower", split_axis=1, concat_axis=0, tiled=True)
    feature_in = pooled[0]
    w_down, w_up, w_out = down_proj[0], up_proj[0], out_proj[0]
    hidden_low = mm(feature_in, w_down).astype(BF16)
    factor = mm(hidden_low, w_up) + cross_bias + 1.0
    crossed = (feature_in * factor).astype(BF16)
    grad_crossed = mm_nt(grad_out, w_out).astype(BF16)
    grad_gate = grad_crossed.astype(F32) * feature_in
    grad_gate_low = grad_gate.astype(BF16)
    grad_hidden = mm_nt(grad_gate_low, w_up).astype(BF16)
    grad_inputs = (grad_crossed.astype(F32) * factor + mm_nt(grad_hidden, w_down)).astype(BF16)
    returned = lax.all_to_all(grad_inputs, "tower", split_axis=0, concat_axis=1, tiled=True)
    local_rows = returned.shape[0]
    blocks = returned.reshape(local_rows, -1, EMB)
    feature_grad = jnp.take(blocks, jnp.argsort(assign), axis=1).reshape(local_rows, -1)
    stacked = jnp.concatenate(
        [
            mm(grad_hidden.T, feature_in),
            mm(hidden_low.T, grad_gate_low),
            mm(grad_out.T, crossed),
        ],
        axis=0,
    )
    scale = 1.0 / math.sqrt(grad_out.shape[0] * lax.axis_size("shard"))
    summed = lax.psum_scatter(stacked, "shard", scatter_dimension=0, tiled=True)
    bias_grad = lax.psum(jnp.sum(grad_gate, axis=0), "shard")[None]
    return feature_grad, (summed * scale)[None], bias_grad


def solution(mesh):
    n_tower, n_shard = mesh.shape["tower"], mesh.shape["shard"]
    placed = (
        P(("tower", "shard"), None),
        P("tower", "shard", None),
        P("tower", None, None),
        P("tower", None, None),
        P("tower", None),
        P("tower", None, None),
        P(),
    )

    paired = n_shard == 2 * 4 and n_tower & (n_tower - 1) == 0
    return jax.shard_map(
        paired_body if paired else general_body,
        mesh=mesh,
        in_specs=placed,
        out_specs=(P(("tower", "shard"), None), P("tower", "shard", None), P("tower", None)),
        check_vma=False,
    )
```

```python
import functools
import math

import jax
import jax.numpy as jnp
from jax import lax
from jax.experimental import pallas as pl
from jax.experimental.pallas import tpu as pltpu
from jax.sharding import PartitionSpec as P

EMB = 128
SLAB = 256
TILE = 16
MIB = 1024 * 1024
VM = 48
COST = 10**10
C1 = 1
P2 = 2
PN = 4
CN = 10**9
C2 = 10**9
C3 = 1
C4 = 1
VMEM_LIMIT = 24 * MIB
BF16 = jnp.bfloat16
F32 = jnp.float32
HBM, VMEM, SMEM = pltpu.HBM, pltpu.VMEM, pltpu.SMEM


def mm(a, b):
    return jnp.dot(a, b, preferred_element_type=F32)


def mm_nt(a, b):
    return lax.dot_general(a, b, (((1,), (1,)), ((), ())), preferred_element_type=F32)


def call(kernel, outs, scratch, spaces, args, name, vmem=VMEM_LIMIT, cost=COST, out_space=None, aliases={}):
    return pl.pallas_call(
        kernel,
        out_shape=outs,
        in_specs=[pl.BlockSpec(memory_space=space) for space in spaces],
        out_specs=[pl.BlockSpec(memory_space=out_space or VMEM)] * len(outs),
        input_output_aliases=aliases,
        scratch_shapes=scratch,
        compiler_params=pltpu.CompilerParams(vmem_limit_bytes=vmem),
        cost_estimate=pl.CostEstimate(flops=cost, bytes_accessed=1, transcendentals=0),
        name=name,
    )(*args)


def column_chunks(width):
    step = 512 if width % 512 == 0 else width
    return [slice(c, c + step) for c in range(0, width, step)]


def copy_all(pairs, sem_ref):
    copies = [pltpu.make_async_copy(a, b, sem_ref.at[i]) for i, (a, b) in enumerate(pairs)]
    for copy in copies:
        copy.start()
    return copies


def cut_kernel(n_tower, grad_ref, *refs):
    pieces, sem_ref = refs[:n_tower], refs[n_tower]
    me = lax.axis_index("tower")
    out = pieces[0].shape[1]
    pairs = [
        (grad_ref.at[:, pl.ds(pl.multiple_of((me ^ k) * out, out), out)], piece)
        for k, piece in enumerate(pieces)
    ]
    for copy in copy_all(pairs, sem_ref):
        copy.wait()


def forward_rows(x_ref, wd_ref, wu_ref, bias_ref, low_ref, cr_ref, factor_ref=None, ready=None):
    low = mm(x_ref[...], wd_ref[...]).astype(BF16)
    low_ref[...] = low
    if ready is not None:
        ready.wait()
    for c in column_chunks(x_ref.shape[1]):
        factor = (mm(low, wu_ref[:, c]) + bias_ref[:, c]) + 1.0
        cr_ref[:, c] = (x_ref[:, c].astype(F32) * factor).astype(BF16)
        if factor_ref is not None:
            factor_ref[:, c] = factor


def forward_inner_kernel(x_ref, wd_ref, wu_ref, bias_ref, low_ref, cr_ref):
    outer = is_outer()

    @pl.when(outer)
    def _():
        low_ref[...] = jnp.zeros_like(low_ref)
        cr_ref[...] = jnp.zeros_like(cr_ref)

    @pl.when(jnp.logical_not(outer))
    def _():
        forward_rows(x_ref, wd_ref, wu_ref, bias_ref, low_ref, cr_ref)


def backward_rows(x_ref, g, low_ref, wu_ref, wo_ref, gg_ref, bg_ref, ht_ref, gc_ref):
    rank = wu_ref.shape[0]
    grad_hidden = jnp.zeros((x_ref.shape[0], rank), F32)
    for c in column_chunks(x_ref.shape[1]):
        x = x_ref[:, c].astype(F32)
        grad_crossed = mm_nt(g, wo_ref[c, :]).astype(BF16).astype(F32)
        grad_gate = grad_crossed * x
        bg_ref[:, c] = jnp.sum(grad_gate, axis=0, keepdims=True)
        low = grad_gate.astype(BF16)
        gg_ref[:, c] = low
        grad_hidden += mm_nt(low, wu_ref[:, c])
        if gc_ref is not None:
            gc_ref[:, c] = grad_crossed.astype(BF16)
    grad_hidden = grad_hidden.astype(BF16)
    ht_ref[0:rank, :] = grad_hidden.T
    ht_ref[rank : 2 * rank, :] = low_ref[...].T
    ht_ref[2 * rank :, :] = g.T
    return grad_hidden


def forward_kernel(wd_hbm, wu_hbm, wo_hbm, x_hbm, bias_ref, wd_ref, wu_ref, wo_ref, x_ref, low_ref, cr_ref, factor_ref, sem_ref):
    copies = copy_all([(x_hbm, x_ref), (wd_hbm, wd_ref), (wu_hbm, wu_ref), (wo_hbm, wo_ref)], sem_ref)
    copies[0].wait()
    copies[1].wait()
    forward_rows(x_ref, wd_ref, wu_ref, bias_ref, low_ref, cr_ref, factor_ref, copies[2])
    copies[3].wait()


def backward_kernel(n_tower, wu_ref, wo_ref, x_ref, low_ref, *refs):
    pieces = refs[:n_tower]
    g_ref, gh_ref, ht_ref, gg_ref, bg_ref, gc_ref = refs[n_tower:]
    me = lax.axis_index("tower")
    rows = pieces[0].shape[0]
    for k, piece in zip(range(len(pieces) - 1, -1, -1), pieces):
        g_ref[pl.ds(pl.multiple_of((me ^ k) * rows, rows), rows), :] = piece[...]
    gh_ref[...] = backward_rows(
        x_ref, g_ref[...], low_ref, wu_ref, wo_ref, gg_ref, bg_ref, ht_ref, gc_ref
    )


def inputs_kernel(n_tower, wd_ref, gh_ref, gc_ref, factor_ref, *refs):
    pieces, gi_ref = refs[:n_tower], refs[n_tower]
    me = lax.axis_index("tower")
    rows = pieces[0].shape[0]
    grad_hidden = gh_ref[...]
    for c in column_chunks(gi_ref.shape[1]):
        direct = gc_ref[:, c].astype(F32) * factor_ref[:, c]
        gi_ref[:, c] = (direct + mm_nt(grad_hidden, wd_ref[c, :])).astype(BF16)
    for k, piece in enumerate(pieces):
        piece[...] = gi_ref[pl.ds(pl.multiple_of((me ^ k) * rows, rows), rows), :]


def products(flip, start, blocks, lhs_ref, acc_ref):
    shard = lax.axis_index("shard") ^ flip
    block = acc_ref.shape[0] // 2
    rank = blocks[0][3].shape[0] // 3
    n = blocks[0][3].shape[1]
    core = lax.rem(shard, 2)
    first = (shard - core) * block
    picked = pl.ds(pl.multiple_of(first, 2 * block), 2 * block)
    for i, rows in enumerate(blocks):
        lhs_ref[:, i * n : (i + 1) * n] = rows[3][picked, :]
    acc_ref[...] = jnp.zeros_like(acc_ref)
    for part in range(3):

        @pl.when((first < (part + 1) * rank) & (first + 2 * block > part * rank))
        def _():
            at = first + lax.broadcasted_iota(jnp.int32, lhs_ref.shape, 0)
            inside = (at >= part * rank) & (at < (part + 1) * rank)
            lhs = jnp.where(inside, lhs_ref[...].astype(F32), 0.0).astype(BF16)
            for c in column_chunks(acc_ref.shape[1]):
                at_c = slice(start + c.start, start + c.stop)
                rhs = [rows[part][:, at_c] for rows in blocks]
                acc_ref[:, c] += mm(lhs, jnp.concatenate(rhs, axis=0))

    theirs = pl.ds(pl.multiple_of((1 - core) * block, block), block)
    ours = pl.ds(pl.multiple_of(core * block, block), block)
    return theirs, ours


def bias_rows(bias):
    high = bias.astype(BF16).astype(F32)
    rest = bias - high
    slabs = [slice(c, c + SLAB) for c in range(0, bias.shape[1], SLAB)]
    filler = [jnp.zeros((1, SLAB), F32)] * (TILE - 2 * len(slabs))
    return jnp.concatenate([high[:, c] for c in slabs] + [rest[:, c] for c in slabs] + filler, axis=0)


def bias_of(rows, n_slabs):
    return jnp.concatenate([rows[j : j + 1] + rows[n_slabs + j : n_slabs + j + 1] for j in range(n_slabs)], axis=1)


def is_outer():
    chip = lax.div(lax.axis_index("shard"), 2)
    return (chip == 0) | (chip == lax.div(lax.axis_size("shard"), 2) - 1)


def store_slabs(acc_ref, theirs, ours, biases, send_refs, keep_ref):
    block = acc_ref.shape[0] // 2
    n_slabs = acc_ref.shape[1] // SLAB
    each = n_slabs // len(send_refs)
    for j in range(n_slabs):
        c, at = slice(j * SLAB, (j + 1) * SLAB), j % each * block
        send_refs[j // each][at : at + block, :] = acc_ref[theirs, c].astype(BF16)
        keep_ref[j * block : (j + 1) * block, :] = acc_ref[ours, c]
    for i, bias in enumerate(biases):
        low = bias_rows(bias).astype(BF16)
        at = each * block + i * TILE
        send_refs[-1][at : at + TILE, :] = low
        at = n_slabs * block + i * TILE
        keep_ref[at : at + TILE, :] = low.astype(F32)


def first_kernel(x_own, gg_own, cr_own, ht_own, bg_own, keep_ref, *refs):
    send_refs, (lhs_ref, acc_ref) = refs[:-2], refs[-2:]
    outer = is_outer()
    (send_ref,) = send_refs
    block, n_slabs = acc_ref.shape[0] // 2, acc_ref.shape[1] // SLAB
    shard = lax.axis_index("shard")
    even = lax.rem(shard, 2) == 0
    last = ht_own.shape[0] - 2 * block

    for here, start, rhs_ref in ((shard < 2, last, cr_own), (outer & (shard >= 2), 0, x_own)):

        @pl.when(here)
        def _(start=start, rhs_ref=rhs_ref):
            lhs = ht_own[start : start + 2 * block, :]
            for j in range(n_slabs):
                both = mm(lhs, rhs_ref[:, j * SLAB : (j + 1) * SLAB])
                rows = slice(j * block, (j + 1) * block)
                low, high = both[:block], both[block:]
                send_ref[rows, :] = jnp.where(even, high, low).astype(BF16)
                keep_ref[rows, :] = jnp.where(even, low, high)
            rows = bias_rows(bg_own[...]).astype(BF16)
            send_ref[-TILE:, :] = rows
            keep_ref[-TILE:, :] = rows.astype(F32)

    @pl.when(jnp.logical_not(outer))
    def _():
        for ref in (*send_refs, keep_ref):
            ref[...] = jnp.zeros_like(ref)


def second_kernel(wu_ref, wo_ref, bg_own, x_own, gg_own, cr_own, ht_own, x_ref, low_ref, cr_ref, g_ref, *refs):
    gg_ref, ht_ref, bg_ref, keep_ref = refs[:4]
    send_refs, (lhs_ref, acc_ref) = refs[4:-2], refs[-2:]
    outer = is_outer()

    @pl.when(outer)
    def _():
        for ref in (gg_ref, bg_ref, ht_ref):
            ref[...] = jnp.zeros_like(ref)
        theirs, ours = products(4, 0, [(x_own, gg_own, cr_own, ht_own)], lhs_ref, acc_ref)
        store_slabs(acc_ref, theirs, ours, [bg_own[...]], send_refs, keep_ref)

    @pl.when(jnp.logical_not(outer))
    def _():
        backward_rows(x_ref, g_ref[...], low_ref, wu_ref, wo_ref, gg_ref, bg_ref, ht_ref, None)
        theirs, ours = products(2, 0, [(x_ref, gg_ref, cr_ref, ht_ref)], lhs_ref, acc_ref)
        store_slabs(acc_ref, theirs, ours, [bg_ref[...]], send_refs, keep_ref)


def near_kernel(wu_ref, wo_ref, x_ref, low_ref, cr_ref, g_ref, *refs):
    own, inner, bg_own, bg_inner, first_ref, keep_ref = refs[:4], refs[4:8], *refs[8:12]
    send_refs, (gg_ref, ht_ref, bg_ref, lhs_ref, acc_ref) = refs[12:-5], refs[-5:]
    backward_rows(x_ref, g_ref[...], low_ref, wu_ref, wo_ref, gg_ref, bg_ref, ht_ref, None)
    theirs, ours = products(0, 0, [own, (x_ref, gg_ref, cr_ref, ht_ref), inner], lhs_ref, acc_ref)
    store_slabs(acc_ref, theirs, ours, [bg_own[...], bg_ref[...], bg_inner[...]], send_refs, keep_ref)
    sums = slice(0, first_ref.shape[0] - TILE)
    keep_ref[sums, :] += first_ref[sums, :].astype(F32)


def joined_bias(rows, n_slabs):
    return bias_rows(bias_of(rows, n_slabs)).astype(BF16)


def round_kernel(n_slabs, keep_ref, *refs):
    recv_refs, out_ref = refs[:-1], refs[-1]
    at = 0
    for recv_ref in recv_refs:
        rows = slice(at, at + recv_ref.shape[0])
        out_ref[rows, :] = (keep_ref[rows, :] + recv_ref[...].astype(F32)).astype(BF16)
        at = rows.stop
    out_ref[-TILE:, :] = joined_bias(keep_ref[-TILE:, :] + recv_refs[-1][-TILE:, :].astype(F32), n_slabs)


def before_last_kernel(scale, keep_ref, first_ref, *refs):
    near_refs, (sum_ref, near_bias_ref, far_bias_ref) = refs[:-3], refs[-3:]
    block, width = sum_ref.shape
    n_slabs = width // SLAB
    each = n_slabs // len(near_refs)
    for j in range(n_slabs):
        at = j % each * block
        total = keep_ref[j * block : (j + 1) * block, :] + near_refs[j // each][at : at + block, :].astype(F32)
        sum_ref[:, j * SLAB : (j + 1) * SLAB] = total * scale
    here = []
    for i in range(3):
        rows = slice(n_slabs * block + i * TILE, n_slabs * block + (i + 1) * TILE)
        at = each * block + i * TILE
        joined = joined_bias(keep_ref[rows, :] + near_refs[-1][at : at + TILE, :].astype(F32), n_slabs)
        here.append(bias_of(joined.astype(F32), n_slabs))
    near_bias_ref[...] = here[0] + here[1]
    far_bias_ref[...] = here[2] + bias_of(first_ref[-TILE:, :].astype(F32), n_slabs)


def final_kernel(scale, sum_ref, near_bias_ref, far_bias_ref, second_ref, out_ref, bg_out, total_ref, bg_ref, sem_ref):
    block, width = total_ref.shape
    n_slabs = width // SLAB
    copies = []

    def write(source, target, i):
        copies.append(pltpu.make_async_copy(source, target, sem_ref.at[i]))
        copies[-1].start()

    for j in range(n_slabs):
        c, rows = slice(j * SLAB, (j + 1) * SLAB), slice(j * block, (j + 1) * block)
        total_ref[:, c] = sum_ref[:, c] + second_ref[rows, :].astype(F32) * scale
        write(total_ref.at[:, pl.ds(j * SLAB, SLAB)], out_ref.at[:, pl.ds(j * SLAB, SLAB)], j)
    bg_ref[...] = near_bias_ref[...] + (far_bias_ref[...] + bias_of(second_ref[-TILE:, :].astype(F32), n_slabs))
    write(bg_ref, bg_out, n_slabs)
    for copy in copies:
        copy.wait()


def place_kernel(n_tower, assign_ref, *refs):
    pieces, out_ref = refs[:n_tower], refs[n_tower]
    me = lax.axis_index("tower")
    slots = pieces[0].shape[1] // EMB
    for k in range(n_tower):
        for j in range(slots):
            at = assign_ref[(me ^ k) * slots + j] * EMB
            out_ref[:, pl.ds(pl.multiple_of(at, EMB), EMB)] = pieces[k][:, j * EMB : (j + 1) * EMB]


def xor_pairs(n, k):
    return [(i, i ^ k) for i in range(n)]


def after(value, *earlier):
    return lax.optimization_barrier((value, *earlier))[0]


def paired_body(out_grad, pooled, down_proj, up_proj, cross_bias, out_proj, assign):
    n_tower, n_shard = lax.axis_size("tower"), lax.axis_size("shard")
    sds = jax.ShapeDtypeStruct
    w_down, w_up, w_out, x = down_proj[0], up_proj[0], out_proj[0], pooled[0]
    n, width = x.shape
    rank, out = w_up.shape[0], w_out.shape[1]
    stack = 2 * rank + out
    block = stack // n_shard
    top_rows = out_grad.shape[0]
    wide = sds((n, width), BF16)
    tall = sds((stack, n), BF16)
    low = sds((n, rank), BF16)
    row = sds((1, width), F32)
    slab_rows = block * width // SLAB

    def across(value, axis, k):
        return lax.ppermute(value, axis, xor_pairs(lax.axis_size(axis), k))

    def slab_outs(n_bias, pieces):
        rows = [slab_rows // pieces] * pieces
        rows[-1] += n_bias * TILE
        return [sds((sum(rows), SLAB), F32)] + [sds((r, SLAB), BF16) for r in rows]

    def sum_scratch(n_blocks):
        return [pltpu.VMEM((2 * block, n_blocks * n), BF16), pltpu.VMEM((2 * block, width), F32)]

    def rounded(keep, *sends):
        (out,) = call(
            functools.partial(round_kernel, width // SLAB),
            [sds(keep.shape, BF16)],
            [],
            [VMEM] * (1 + len(sends)),
            [keep] + [across(send, "shard", 1) for send in sends],
            "join_cores",
            cost=1,
        )
        return out

    inside = [2 <= i < n_shard - 2 for i in range(n_shard)]
    inner = [(i, i ^ 6 if inside[i] else i ^ 1) for i in range(n_shard)]
    outer = [(i, i ^ 1 if inside[i] else i ^ 6) for i in range(n_shard)]
    second = [(i, i ^ 2 if inside[i] else i ^ 4) for i in range(n_shard)]

    x_other = across(x, "shard", 2)
    x_inner = lax.ppermute(x, "shard", inner)
    pieces = call(
        functools.partial(cut_kernel, n_tower),
        [sds((top_rows, out), BF16)] * n_tower,
        [pltpu.SemaphoreType.DMA((n_tower,))],
        [HBM],
        [out_grad],
        "cut_columns",
        48 * MIB,
        10**9,
    )
    received = [across(pieces[k], "tower", k) for k in range(n_tower - 1, 0, -1)]
    pieces = [pieces[0]] + received[::-1]
    wd, wu, wo, x_own, low_own, cr_own, factor = call(
        forward_kernel,
        [sds(w.shape, BF16) for w in (w_down, w_up, w_out)] + [wide, low, wide, sds((n, width), F32)],
        [pltpu.SemaphoreType.DMA((4,))],
        [HBM] * 4 + [VMEM],
        [w_down, w_up, w_out, x, cross_bias],
        "forward_own",
        VM * MIB,
        1,
    )
    g_own, gh_own, ht_own, gg_own, bg_own, gc_own = call(
        functools.partial(backward_kernel, n_tower),
        [sds((n, out), BF16), low, tall, wide, row, wide],
        [],
        [VMEM] * (4 + n_tower),
        [wu, wo, x_own, low_own, *pieces[::-1]],
        "backward_own",
        cost=1,
    )
    own = [x_own, gg_own, cr_own, ht_own]
    g_inner = lax.ppermute(g_own, "shard", inner)
    g_other = across(g_own, "shard", 2)
    first = rounded(
        *call(first_kernel, slab_outs(1, 1), sum_scratch(1), [VMEM] * 5, [*own, bg_own], "first_sums", cost=C1)
    )
    from_first = lax.ppermute(first, "shard", outer)
    low_inner, cr_inner = call(
        forward_inner_kernel, [low, wide], [], [VMEM] * 4, [after(x_inner, first), wd, wu, cross_bias], "forward_inner", cost=C2
    )
    low_other, cr_other = call(
        forward_rows, [low, wide], [], [VMEM] * 4, [after(x_other, low_inner, g_other), wd, wu, cross_bias], "forward_other", cost=C2
    )
    gg_inner, ht_inner, bg_inner, *sums = call(
        second_kernel,
        [wide, tall, row] + slab_outs(1, P2),
        sum_scratch(1),
        [VMEM] * 11,
        [wu, wo, bg_own, *own, x_inner, after(low_inner, low_other), cr_inner, g_inner],
        "second_sums",
        cost=C2,
    )
    second_sum = rounded(*sums)
    from_second = lax.ppermute(second_sum, "shard", second)
    grad_inputs = call(
        functools.partial(inputs_kernel, n_tower),
        [sds((top_rows, width), BF16)] * n_tower,
        [pltpu.VMEM((n, width), BF16)],
        [VMEM] * 4,
        [wd, gh_own, after(gc_own, second_sum), factor],
        "grad_inputs",
        cost=C4,
    )
    near_keep, *near_sends = call(
        near_kernel,
        slab_outs(3, PN),
        [pltpu.VMEM((n, width), BF16), pltpu.VMEM((stack, n), BF16), pltpu.VMEM((1, width), F32)] + sum_scratch(3),
        [VMEM] * 17,
        [wu, wo, x_other, after(low_other, *grad_inputs), cr_other, g_other, *own, x_inner, gg_inner, cr_inner, ht_inner, bg_own, bg_inner, from_first],
        "near_sums",
        cost=CN,
    )
    near_others = [across(send, "shard", 1) for send in near_sends]
    returned = [grad_inputs[0]]
    for k in range(1, n_tower):
        piece = grad_inputs[k]
        returned.append(across(piece, "tower", k))
    (feature_grad,) = call(
        functools.partial(place_kernel, n_tower),
        [sds((top_rows, n_tower * width), BF16)],
        [],
        [SMEM] + [VMEM] * n_tower,
        [assign, *returned],
        "place_features",
        cost=1,
    )
    scale = 1.0 / math.sqrt(n * n_shard)
    before_last = call(
        functools.partial(before_last_kernel, scale),
        [sds((block, width), F32), row, row],
        [],
        [VMEM] * (2 + len(near_others)),
        [near_keep, from_first, *near_others],
        "before_last",
        cost=1,
    )
    weight_grad, bias_grad = call(
        functools.partial(final_kernel, scale),
        [sds((block, width), F32), row],
        [
            pltpu.VMEM((block, width), F32),
            pltpu.VMEM((1, width), F32),
            pltpu.SemaphoreType.DMA((width // SLAB + 1,)),
        ],
        [VMEM] * 4,
        [*before_last, from_second],
        "add_up",
        out_space=HBM,
    )
    return feature_grad, weight_grad[None], bias_grad


def general_body(out_grad, pooled, down_proj, up_proj, cross_bias, out_proj, assign):
    grad_out = lax.all_to_all(out_grad, "tower", split_axis=1, concat_axis=0, tiled=True)
    feature_in = pooled[0]
    w_down, w_up, w_out = down_proj[0], up_proj[0], out_proj[0]
    hidden_low = mm(feature_in, w_down).astype(BF16)
    factor = mm(hidden_low, w_up) + cross_bias + 1.0
    crossed = (feature_in * factor).astype(BF16)
    grad_crossed = mm_nt(grad_out, w_out).astype(BF16)
    grad_gate = grad_crossed.astype(F32) * feature_in
    grad_gate_low = grad_gate.astype(BF16)
    grad_hidden = mm_nt(grad_gate_low, w_up).astype(BF16)
    grad_inputs = (grad_crossed.astype(F32) * factor + mm_nt(grad_hidden, w_down)).astype(BF16)
    returned = lax.all_to_all(grad_inputs, "tower", split_axis=0, concat_axis=1, tiled=True)
    local_rows = returned.shape[0]
    blocks = returned.reshape(local_rows, -1, EMB)
    feature_grad = jnp.take(blocks, jnp.argsort(assign), axis=1).reshape(local_rows, -1)
    stacked = jnp.concatenate(
        [
            mm(grad_hidden.T, feature_in),
            mm(hidden_low.T, grad_gate_low),
            mm(grad_out.T, crossed),
        ],
        axis=0,
    )
    scale = 1.0 / math.sqrt(grad_out.shape[0] * lax.axis_size("shard"))
    summed = lax.psum_scatter(stacked, "shard", scatter_dimension=0, tiled=True)
    bias_grad = lax.psum(jnp.sum(grad_gate, axis=0), "shard")[None]
    return feature_grad, (summed * scale)[None], bias_grad


def solution(mesh):
    n_tower, n_shard = mesh.shape["tower"], mesh.shape["shard"]
    placed = (
        P(("tower", "shard"), None),
        P("tower", "shard", None),
        P("tower", None, None),
        P("tower", None, None),
        P("tower", None),
        P("tower", None, None),
        P(),
    )

    paired = n_shard == 2 * 4 and n_tower & (n_tower - 1) == 0
    return jax.shard_map(
        paired_body if paired else general_body,
        mesh=mesh,
        in_specs=placed,
        out_specs=(P(("tower", "shard"), None), P("tower", "shard", None), P("tower", None)),
        check_vma=False,
    )
```

```python
import functools
import math

import jax
import jax.numpy as jnp
from jax import lax
from jax.experimental import pallas as pl
from jax.experimental.pallas import tpu as pltpu
from jax.sharding import PartitionSpec as P

EMB = 128
SLAB = 256
TILE = 16
MIB = 1024 * 1024
VM = 48
COST = 10**10
C1 = 1
P2 = 2
PN = 4
CN = 10**9
C2 = 10**9
C3 = 1
C4 = 1
VMEM_LIMIT = 24 * MIB
BF16 = jnp.bfloat16
F32 = jnp.float32
HBM, VMEM, SMEM = pltpu.HBM, pltpu.VMEM, pltpu.SMEM


def mm(a, b):
    return jnp.dot(a, b, preferred_element_type=F32)


def mm_nt(a, b):
    return lax.dot_general(a, b, (((1,), (1,)), ((), ())), preferred_element_type=F32)


def call(kernel, outs, scratch, spaces, args, name, vmem=VMEM_LIMIT, cost=COST, out_space=None, aliases={}):
    return pl.pallas_call(
        kernel,
        out_shape=outs,
        in_specs=[pl.BlockSpec(memory_space=space) for space in spaces],
        out_specs=[pl.BlockSpec(memory_space=out_space or VMEM)] * len(outs),
        input_output_aliases=aliases,
        scratch_shapes=scratch,
        compiler_params=pltpu.CompilerParams(vmem_limit_bytes=vmem),
        cost_estimate=pl.CostEstimate(flops=cost, bytes_accessed=1, transcendentals=0),
        name=name,
    )(*args)


def column_chunks(width):
    step = 256 if width % 256 == 0 else width
    return [slice(c, c + step) for c in range(0, width, step)]


def copy_all(pairs, sem_ref):
    copies = [pltpu.make_async_copy(a, b, sem_ref.at[i]) for i, (a, b) in enumerate(pairs)]
    for copy in copies:
        copy.start()
    return copies


def cut_kernel(n_tower, grad_ref, *refs):
    pieces, sem_ref = refs[:n_tower], refs[n_tower]
    me = lax.axis_index("tower")
    out = pieces[0].shape[1]
    pairs = [
        (grad_ref.at[:, pl.ds(pl.multiple_of((me ^ k) * out, out), out)], piece)
        for k, piece in enumerate(pieces)
    ]
    for copy in copy_all(pairs, sem_ref):
        copy.wait()


def forward_rows(x_ref, wd_ref, wu_ref, bias_ref, low_ref, cr_ref, factor_ref=None, ready=None):
    low = mm(x_ref[...], wd_ref[...]).astype(BF16)
    low_ref[...] = low
    if ready is not None:
        ready.wait()
    for c in column_chunks(x_ref.shape[1]):
        factor = (mm(low, wu_ref[:, c]) + bias_ref[:, c]) + 1.0
        cr_ref[:, c] = (x_ref[:, c].astype(F32) * factor).astype(BF16)
        if factor_ref is not None:
            factor_ref[:, c] = factor


def forward_inner_kernel(x_ref, wd_ref, wu_ref, bias_ref, low_ref, cr_ref):
    outer = is_outer()

    @pl.when(outer)
    def _():
        low_ref[...] = jnp.zeros_like(low_ref)
        cr_ref[...] = jnp.zeros_like(cr_ref)

    @pl.when(jnp.logical_not(outer))
    def _():
        forward_rows(x_ref, wd_ref, wu_ref, bias_ref, low_ref, cr_ref)


def backward_rows(x_ref, g, low_ref, wu_ref, wo_ref, gg_ref, bg_ref, ht_ref, gc_ref):
    rank = wu_ref.shape[0]
    grad_hidden = jnp.zeros((x_ref.shape[0], rank), F32)
    for c in column_chunks(x_ref.shape[1]):
        x = x_ref[:, c].astype(F32)
        grad_crossed = mm_nt(g, wo_ref[c, :]).astype(BF16).astype(F32)
        grad_gate = grad_crossed * x
        bg_ref[:, c] = jnp.sum(grad_gate, axis=0, keepdims=True)
        low = grad_gate.astype(BF16)
        gg_ref[:, c] = low
        grad_hidden += mm_nt(low, wu_ref[:, c])
        if gc_ref is not None:
            gc_ref[:, c] = grad_crossed.astype(BF16)
    grad_hidden = grad_hidden.astype(BF16)
    ht_ref[0:rank, :] = grad_hidden.T
    ht_ref[rank : 2 * rank, :] = low_ref[...].T
    ht_ref[2 * rank :, :] = g.T
    return grad_hidden


def forward_kernel(wd_hbm, wu_hbm, wo_hbm, x_hbm, bias_ref, wd_ref, wu_ref, wo_ref, x_ref, low_ref, cr_ref, factor_ref, sem_ref):
    copies = copy_all([(x_hbm, x_ref), (wd_hbm, wd_ref), (wu_hbm, wu_ref), (wo_hbm, wo_ref)], sem_ref)
    copies[0].wait()
    copies[1].wait()
    forward_rows(x_ref, wd_ref, wu_ref, bias_ref, low_ref, cr_ref, factor_ref, copies[2])
    copies[3].wait()


def backward_kernel(n_tower, wu_ref, wo_ref, x_ref, low_ref, *refs):
    pieces = refs[:n_tower]
    g_ref, gh_ref, ht_ref, gg_ref, bg_ref, gc_ref = refs[n_tower:]
    me = lax.axis_index("tower")
    rows = pieces[0].shape[0]
    for k, piece in zip(range(len(pieces) - 1, -1, -1), pieces):
        g_ref[pl.ds(pl.multiple_of((me ^ k) * rows, rows), rows), :] = piece[...]
    gh_ref[...] = backward_rows(
        x_ref, g_ref[...], low_ref, wu_ref, wo_ref, gg_ref, bg_ref, ht_ref, gc_ref
    )


def inputs_kernel(n_tower, wd_ref, gh_ref, gc_ref, factor_ref, *refs):
    pieces, gi_ref = refs[:n_tower], refs[n_tower]
    me = lax.axis_index("tower")
    rows = pieces[0].shape[0]
    grad_hidden = gh_ref[...]
    for c in column_chunks(gi_ref.shape[1]):
        direct = gc_ref[:, c].astype(F32) * factor_ref[:, c]
        gi_ref[:, c] = (direct + mm_nt(grad_hidden, wd_ref[c, :])).astype(BF16)
    for k, piece in enumerate(pieces):
        piece[...] = gi_ref[pl.ds(pl.multiple_of((me ^ k) * rows, rows), rows), :]


def products(flip, start, blocks, lhs_ref, acc_ref):
    shard = lax.axis_index("shard") ^ flip
    block = acc_ref.shape[0] // 2
    rank = blocks[0][3].shape[0] // 3
    n = blocks[0][3].shape[1]
    core = lax.rem(shard, 2)
    first = (shard - core) * block
    picked = pl.ds(pl.multiple_of(first, 2 * block), 2 * block)
    for i, rows in enumerate(blocks):
        lhs_ref[:, i * n : (i + 1) * n] = rows[3][picked, :]
    acc_ref[...] = jnp.zeros_like(acc_ref)
    for part in range(3):

        @pl.when((first < (part + 1) * rank) & (first + 2 * block > part * rank))
        def _():
            at = first + lax.broadcasted_iota(jnp.int32, lhs_ref.shape, 0)
            inside = (at >= part * rank) & (at < (part + 1) * rank)
            lhs = jnp.where(inside, lhs_ref[...].astype(F32), 0.0).astype(BF16)
            for c in column_chunks(acc_ref.shape[1]):
                at_c = slice(start + c.start, start + c.stop)
                rhs = [rows[part][:, at_c] for rows in blocks]
                acc_ref[:, c] += mm(lhs, jnp.concatenate(rhs, axis=0))

    theirs = pl.ds(pl.multiple_of((1 - core) * block, block), block)
    ours = pl.ds(pl.multiple_of(core * block, block), block)
    return theirs, ours


def bias_rows(bias):
    high = bias.astype(BF16).astype(F32)
    rest = bias - high
    slabs = [slice(c, c + SLAB) for c in range(0, bias.shape[1], SLAB)]
    filler = [jnp.zeros((1, SLAB), F32)] * (TILE - 2 * len(slabs))
    return jnp.concatenate([high[:, c] for c in slabs] + [rest[:, c] for c in slabs] + filler, axis=0)


def bias_of(rows, n_slabs):
    return jnp.concatenate([rows[j : j + 1] + rows[n_slabs + j : n_slabs + j + 1] for j in range(n_slabs)], axis=1)


def is_outer():
    chip = lax.div(lax.axis_index("shard"), 2)
    return (chip == 0) | (chip == lax.div(lax.axis_size("shard"), 2) - 1)


def store_slabs(acc_ref, theirs, ours, biases, send_refs, keep_ref):
    block = acc_ref.shape[0] // 2
    n_slabs = acc_ref.shape[1] // SLAB
    each = n_slabs // len(send_refs)
    for j in range(n_slabs):
        c, at = slice(j * SLAB, (j + 1) * SLAB), j % each * block
        send_refs[j // each][at : at + block, :] = acc_ref[theirs, c].astype(BF16)
        keep_ref[j * block : (j + 1) * block, :] = acc_ref[ours, c]
    for i, bias in enumerate(biases):
        low = bias_rows(bias).astype(BF16)
        at = each * block + i * TILE
        send_refs[-1][at : at + TILE, :] = low
        at = n_slabs * block + i * TILE
        keep_ref[at : at + TILE, :] = low.astype(F32)


def first_kernel(x_own, gg_own, cr_own, ht_own, bg_own, keep_ref, *refs):
    send_refs, (lhs_ref, acc_ref) = refs[:-2], refs[-2:]
    outer = is_outer()
    (send_ref,) = send_refs
    block, n_slabs = acc_ref.shape[0] // 2, acc_ref.shape[1] // SLAB
    shard = lax.axis_index("shard")
    even = lax.rem(shard, 2) == 0
    last = ht_own.shape[0] - 2 * block

    for here, start, rhs_ref in ((shard < 2, last, cr_own), (outer & (shard >= 2), 0, x_own)):

        @pl.when(here)
        def _(start=start, rhs_ref=rhs_ref):
            lhs = ht_own[start : start + 2 * block, :]
            for j in range(n_slabs):
                both = mm(lhs, rhs_ref[:, j * SLAB : (j + 1) * SLAB])
                rows = slice(j * block, (j + 1) * block)
                low, high = both[:block], both[block:]
                send_ref[rows, :] = jnp.where(even, high, low).astype(BF16)
                keep_ref[rows, :] = jnp.where(even, low, high)
            rows = bias_rows(bg_own[...]).astype(BF16)
            send_ref[-TILE:, :] = rows
            keep_ref[-TILE:, :] = rows.astype(F32)

    @pl.when(jnp.logical_not(outer))
    def _():
        for ref in (*send_refs, keep_ref):
            ref[...] = jnp.zeros_like(ref)


def second_kernel(wu_ref, wo_ref, bg_own, x_own, gg_own, cr_own, ht_own, x_ref, low_ref, cr_ref, g_ref, *refs):
    gg_ref, ht_ref, bg_ref, keep_ref = refs[:4]
    send_refs, (lhs_ref, acc_ref) = refs[4:-2], refs[-2:]
    outer = is_outer()

    @pl.when(outer)
    def _():
        for ref in (gg_ref, bg_ref, ht_ref):
            ref[...] = jnp.zeros_like(ref)
        theirs, ours = products(4, 0, [(x_own, gg_own, cr_own, ht_own)], lhs_ref, acc_ref)
        store_slabs(acc_ref, theirs, ours, [bg_own[...]], send_refs, keep_ref)

    @pl.when(jnp.logical_not(outer))
    def _():
        backward_rows(x_ref, g_ref[...], low_ref, wu_ref, wo_ref, gg_ref, bg_ref, ht_ref, None)
        theirs, ours = products(2, 0, [(x_ref, gg_ref, cr_ref, ht_ref)], lhs_ref, acc_ref)
        store_slabs(acc_ref, theirs, ours, [bg_ref[...]], send_refs, keep_ref)


def near_kernel(wu_ref, wo_ref, x_ref, low_ref, cr_ref, g_ref, *refs):
    own, inner, bg_own, bg_inner, first_ref, keep_ref = refs[:4], refs[4:8], *refs[8:12]
    send_refs, (gg_ref, ht_ref, bg_ref, lhs_ref, acc_ref) = refs[12:-5], refs[-5:]
    backward_rows(x_ref, g_ref[...], low_ref, wu_ref, wo_ref, gg_ref, bg_ref, ht_ref, None)
    theirs, ours = products(0, 0, [own, (x_ref, gg_ref, cr_ref, ht_ref), inner], lhs_ref, acc_ref)
    store_slabs(acc_ref, theirs, ours, [bg_own[...], bg_ref[...], bg_inner[...]], send_refs, keep_ref)
    sums = slice(0, first_ref.shape[0] - TILE)
    keep_ref[sums, :] += first_ref[sums, :].astype(F32)


def joined_bias(rows, n_slabs):
    return bias_rows(bias_of(rows, n_slabs)).astype(BF16)


def round_kernel(n_slabs, keep_ref, *refs):
    recv_refs, out_ref = refs[:-1], refs[-1]
    at = 0
    for recv_ref in recv_refs:
        rows = slice(at, at + recv_ref.shape[0])
        out_ref[rows, :] = (keep_ref[rows, :] + recv_ref[...].astype(F32)).astype(BF16)
        at = rows.stop
    out_ref[-TILE:, :] = joined_bias(keep_ref[-TILE:, :] + recv_refs[-1][-TILE:, :].astype(F32), n_slabs)


def before_last_kernel(scale, keep_ref, first_ref, *refs):
    near_refs, (sum_ref, near_bias_ref, far_bias_ref) = refs[:-3], refs[-3:]
    block, width = sum_ref.shape
    n_slabs = width // SLAB
    each = n_slabs // len(near_refs)
    for j in range(n_slabs):
        at = j % each * block
        total = keep_ref[j * block : (j + 1) * block, :] + near_refs[j // each][at : at + block, :].astype(F32)
        sum_ref[:, j * SLAB : (j + 1) * SLAB] = total * scale
    here = []
    for i in range(3):
        rows = slice(n_slabs * block + i * TILE, n_slabs * block + (i + 1) * TILE)
        at = each * block + i * TILE
        joined = joined_bias(keep_ref[rows, :] + near_refs[-1][at : at + TILE, :].astype(F32), n_slabs)
        here.append(bias_of(joined.astype(F32), n_slabs))
    near_bias_ref[...] = here[0] + here[1]
    far_bias_ref[...] = here[2] + bias_of(first_ref[-TILE:, :].astype(F32), n_slabs)


def final_kernel(scale, sum_ref, near_bias_ref, far_bias_ref, second_ref, out_ref, bg_out, total_ref, bg_ref, sem_ref):
    block, width = total_ref.shape
    n_slabs = width // SLAB
    copies = []

    def write(source, target, i):
        copies.append(pltpu.make_async_copy(source, target, sem_ref.at[i]))
        copies[-1].start()

    for j in range(n_slabs):
        c, rows = slice(j * SLAB, (j + 1) * SLAB), slice(j * block, (j + 1) * block)
        total_ref[:, c] = sum_ref[:, c] + second_ref[rows, :].astype(F32) * scale
        write(total_ref.at[:, pl.ds(j * SLAB, SLAB)], out_ref.at[:, pl.ds(j * SLAB, SLAB)], j)
    bg_ref[...] = near_bias_ref[...] + (far_bias_ref[...] + bias_of(second_ref[-TILE:, :].astype(F32), n_slabs))
    write(bg_ref, bg_out, n_slabs)
    for copy in copies:
        copy.wait()


def place_kernel(n_tower, assign_ref, *refs):
    pieces, out_ref = refs[:n_tower], refs[n_tower]
    me = lax.axis_index("tower")
    slots = pieces[0].shape[1] // EMB
    for k in range(n_tower):
        for j in range(slots):
            at = assign_ref[(me ^ k) * slots + j] * EMB
            out_ref[:, pl.ds(pl.multiple_of(at, EMB), EMB)] = pieces[k][:, j * EMB : (j + 1) * EMB]


def xor_pairs(n, k):
    return [(i, i ^ k) for i in range(n)]


def after(value, *earlier):
    return lax.optimization_barrier((value, *earlier))[0]


def paired_body(out_grad, pooled, down_proj, up_proj, cross_bias, out_proj, assign):
    n_tower, n_shard = lax.axis_size("tower"), lax.axis_size("shard")
    sds = jax.ShapeDtypeStruct
    w_down, w_up, w_out, x = down_proj[0], up_proj[0], out_proj[0], pooled[0]
    n, width = x.shape
    rank, out = w_up.shape[0], w_out.shape[1]
    stack = 2 * rank + out
    block = stack // n_shard
    top_rows = out_grad.shape[0]
    wide = sds((n, width), BF16)
    tall = sds((stack, n), BF16)
    low = sds((n, rank), BF16)
    row = sds((1, width), F32)
    slab_rows = block * width // SLAB

    def across(value, axis, k):
        return lax.ppermute(value, axis, xor_pairs(lax.axis_size(axis), k))

    def slab_outs(n_bias, pieces):
        rows = [slab_rows // pieces] * pieces
        rows[-1] += n_bias * TILE
        return [sds((sum(rows), SLAB), F32)] + [sds((r, SLAB), BF16) for r in rows]

    def sum_scratch(n_blocks):
        return [pltpu.VMEM((2 * block, n_blocks * n), BF16), pltpu.VMEM((2 * block, width), F32)]

    def rounded(keep, *sends):
        (out,) = call(
            functools.partial(round_kernel, width // SLAB),
            [sds(keep.shape, BF16)],
            [],
            [VMEM] * (1 + len(sends)),
            [keep] + [across(send, "shard", 1) for send in sends],
            "join_cores",
            cost=1,
        )
        return out

    inside = [2 <= i < n_shard - 2 for i in range(n_shard)]
    inner = [(i, i ^ 6 if inside[i] else i ^ 1) for i in range(n_shard)]
    outer = [(i, i ^ 1 if inside[i] else i ^ 6) for i in range(n_shard)]
    second = [(i, i ^ 2 if inside[i] else i ^ 4) for i in range(n_shard)]

    x_other = across(x, "shard", 2)
    x_inner = lax.ppermute(x, "shard", inner)
    pieces = call(
        functools.partial(cut_kernel, n_tower),
        [sds((top_rows, out), BF16)] * n_tower,
        [pltpu.SemaphoreType.DMA((n_tower,))],
        [HBM],
        [out_grad],
        "cut_columns",
        48 * MIB,
        10**9,
    )
    received = [across(pieces[k], "tower", k) for k in range(n_tower - 1, 0, -1)]
    pieces = [pieces[0]] + received[::-1]
    wd, wu, wo, x_own, low_own, cr_own, factor = call(
        forward_kernel,
        [sds(w.shape, BF16) for w in (w_down, w_up, w_out)] + [wide, low, wide, sds((n, width), F32)],
        [pltpu.SemaphoreType.DMA((4,))],
        [HBM] * 4 + [VMEM],
        [w_down, w_up, w_out, x, cross_bias],
        "forward_own",
        VM * MIB,
        1,
    )
    g_own, gh_own, ht_own, gg_own, bg_own, gc_own = call(
        functools.partial(backward_kernel, n_tower),
        [sds((n, out), BF16), low, tall, wide, row, wide],
        [],
        [VMEM] * (4 + n_tower),
        [wu, wo, x_own, low_own, *pieces[::-1]],
        "backward_own",
        cost=1,
    )
    own = [x_own, gg_own, cr_own, ht_own]
    g_inner = lax.ppermute(g_own, "shard", inner)
    g_other = across(g_own, "shard", 2)
    first = rounded(
        *call(first_kernel, slab_outs(1, 1), sum_scratch(1), [VMEM] * 5, [*own, bg_own], "first_sums", cost=C1)
    )
    from_first = lax.ppermute(first, "shard", outer)
    low_inner, cr_inner = call(
        forward_inner_kernel, [low, wide], [], [VMEM] * 4, [after(x_inner, first), wd, wu, cross_bias], "forward_inner", cost=C2
    )
    low_other, cr_other = call(
        forward_rows, [low, wide], [], [VMEM] * 4, [after(x_other, low_inner, g_other), wd, wu, cross_bias], "forward_other", cost=C2
    )
    gg_inner, ht_inner, bg_inner, *sums = call(
        second_kernel,
        [wide, tall, row] + slab_outs(1, P2),
        sum_scratch(1),
        [VMEM] * 11,
        [wu, wo, bg_own, *own, x_inner, after(low_inner, low_other), cr_inner, g_inner],
        "second_sums",
        cost=C2,
    )
    second_sum = rounded(*sums)
    from_second = lax.ppermute(second_sum, "shard", second)
    grad_inputs = call(
        functools.partial(inputs_kernel, n_tower),
        [sds((top_rows, width), BF16)] * n_tower,
        [pltpu.VMEM((n, width), BF16)],
        [VMEM] * 4,
        [wd, gh_own, after(gc_own, second_sum), factor],
        "grad_inputs",
        cost=C4,
    )
    near_keep, *near_sends = call(
        near_kernel,
        slab_outs(3, PN),
        [pltpu.VMEM((n, width), BF16), pltpu.VMEM((stack, n), BF16), pltpu.VMEM((1, width), F32)] + sum_scratch(3),
        [VMEM] * 17,
        [wu, wo, x_other, after(low_other, *grad_inputs), cr_other, g_other, *own, x_inner, gg_inner, cr_inner, ht_inner, bg_own, bg_inner, from_first],
        "near_sums",
        cost=CN,
    )
    near_others = [across(send, "shard", 1) for send in near_sends]
    returned = [grad_inputs[0]]
    for k in range(1, n_tower):
        piece = grad_inputs[k]
        returned.append(across(piece, "tower", k))
    (feature_grad,) = call(
        functools.partial(place_kernel, n_tower),
        [sds((top_rows, n_tower * width), BF16)],
        [],
        [SMEM] + [VMEM] * n_tower,
        [assign, *returned],
        "place_features",
        cost=1,
    )
    scale = 1.0 / math.sqrt(n * n_shard)
    before_last = call(
        functools.partial(before_last_kernel, scale),
        [sds((block, width), F32), row, row],
        [],
        [VMEM] * (2 + len(near_others)),
        [near_keep, from_first, *near_others],
        "before_last",
        cost=1,
    )
    weight_grad, bias_grad = call(
        functools.partial(final_kernel, scale),
        [sds((block, width), F32), row],
        [
            pltpu.VMEM((block, width), F32),
            pltpu.VMEM((1, width), F32),
            pltpu.SemaphoreType.DMA((width // SLAB + 1,)),
        ],
        [VMEM] * 4,
        [*before_last, from_second],
        "add_up",
        out_space=HBM,
    )
    return feature_grad, weight_grad[None], bias_grad


def general_body(out_grad, pooled, down_proj, up_proj, cross_bias, out_proj, assign):
    grad_out = lax.all_to_all(out_grad, "tower", split_axis=1, concat_axis=0, tiled=True)
    feature_in = pooled[0]
    w_down, w_up, w_out = down_proj[0], up_proj[0], out_proj[0]
    hidden_low = mm(feature_in, w_down).astype(BF16)
    factor = mm(hidden_low, w_up) + cross_bias + 1.0
    crossed = (feature_in * factor).astype(BF16)
    grad_crossed = mm_nt(grad_out, w_out).astype(BF16)
    grad_gate = grad_crossed.astype(F32) * feature_in
    grad_gate_low = grad_gate.astype(BF16)
    grad_hidden = mm_nt(grad_gate_low, w_up).astype(BF16)
    grad_inputs = (grad_crossed.astype(F32) * factor + mm_nt(grad_hidden, w_down)).astype(BF16)
    returned = lax.all_to_all(grad_inputs, "tower", split_axis=0, concat_axis=1, tiled=True)
    local_rows = returned.shape[0]
    blocks = returned.reshape(local_rows, -1, EMB)
    feature_grad = jnp.take(blocks, jnp.argsort(assign), axis=1).reshape(local_rows, -1)
    stacked = jnp.concatenate(
        [
            mm(grad_hidden.T, feature_in),
            mm(hidden_low.T, grad_gate_low),
            mm(grad_out.T, crossed),
        ],
        axis=0,
    )
    scale = 1.0 / math.sqrt(grad_out.shape[0] * lax.axis_size("shard"))
    summed = lax.psum_scatter(stacked, "shard", scatter_dimension=0, tiled=True)
    bias_grad = lax.psum(jnp.sum(grad_gate, axis=0), "shard")[None]
    return feature_grad, (summed * scale)[None], bias_grad


def solution(mesh):
    n_tower, n_shard = mesh.shape["tower"], mesh.shape["shard"]
    placed = (
        P(("tower", "shard"), None),
        P("tower", "shard", None),
        P("tower", None, None),
        P("tower", None, None),
        P("tower", None),
        P("tower", None, None),
        P(),
    )

    paired = n_shard == 2 * 4 and n_tower & (n_tower - 1) == 0
    return jax.shard_map(
        paired_body if paired else general_body,
        mesh=mesh,
        in_specs=placed,
        out_specs=(P(("tower", "shard"), None), P("tower", "shard", None), P("tower", None)),
        check_vma=False,
    )
```

```python
import functools
import math

import jax
import jax.numpy as jnp
from jax import lax
from jax.experimental import pallas as pl
from jax.experimental.pallas import tpu as pltpu
from jax.sharding import PartitionSpec as P

EMB = 128
SLAB = 256
TILE = 16
MIB = 1024 * 1024
VM = 48
COST = 10**10
C1 = 1
P2 = 2
PN = 4
CN = 10**9
C2 = 10**9
C3 = 1
C4 = 1
VMEM_LIMIT = 24 * MIB
BF16 = jnp.bfloat16
F32 = jnp.float32
HBM, VMEM, SMEM = pltpu.HBM, pltpu.VMEM, pltpu.SMEM


def mm(a, b):
    return jnp.dot(a, b, preferred_element_type=F32)


def mm_nt(a, b):
    return lax.dot_general(a, b, (((1,), (1,)), ((), ())), preferred_element_type=F32)


def call(kernel, outs, scratch, spaces, args, name, vmem=VMEM_LIMIT, cost=COST, out_space=None, aliases={}):
    return pl.pallas_call(
        kernel,
        out_shape=outs,
        in_specs=[pl.BlockSpec(memory_space=space) for space in spaces],
        out_specs=[pl.BlockSpec(memory_space=out_space or VMEM)] * len(outs),
        input_output_aliases=aliases,
        scratch_shapes=scratch,
        compiler_params=pltpu.CompilerParams(vmem_limit_bytes=vmem),
        cost_estimate=pl.CostEstimate(flops=cost, bytes_accessed=1, transcendentals=0),
        name=name,
    )(*args)


def column_chunks(width):
    step = 512 if width % 512 == 0 else width
    return [slice(c, c + step) for c in range(0, width, step)]


def copy_all(pairs, sem_ref):
    copies = [pltpu.make_async_copy(a, b, sem_ref.at[i]) for i, (a, b) in enumerate(pairs)]
    for copy in copies:
        copy.start()
    return copies


def cut_kernel(n_tower, grad_ref, *refs):
    pieces, sem_ref = refs[:n_tower], refs[n_tower]
    me = lax.axis_index("tower")
    out = pieces[0].shape[1]
    pairs = [
        (grad_ref.at[:, pl.ds(pl.multiple_of((me ^ k) * out, out), out)], piece)
        for k, piece in enumerate(pieces)
    ]
    for copy in copy_all(pairs, sem_ref):
        copy.wait()


def forward_rows(x_ref, wd_ref, wu_ref, bias_ref, low_ref, cr_ref, factor_ref=None, ready=None):
    low = mm(x_ref[...], wd_ref[...]).astype(BF16)
    low_ref[...] = low
    if ready is not None:
        ready.wait()
    for c in column_chunks(x_ref.shape[1]):
        factor = (mm(low, wu_ref[:, c]) + bias_ref[:, c]) + 1.0
        cr_ref[:, c] = (x_ref[:, c].astype(F32) * factor).astype(BF16)
        if factor_ref is not None:
            factor_ref[:, c] = factor


def forward_inner_kernel(x_ref, wd_ref, wu_ref, bias_ref, low_ref, cr_ref):
    outer = is_outer()

    @pl.when(outer)
    def _():
        low_ref[...] = jnp.zeros_like(low_ref)
        cr_ref[...] = jnp.zeros_like(cr_ref)

    @pl.when(jnp.logical_not(outer))
    def _():
        forward_rows(x_ref, wd_ref, wu_ref, bias_ref, low_ref, cr_ref)


def backward_rows(x_ref, g, low_ref, wu_ref, wo_ref, gg_ref, bg_ref, ht_ref, gc_ref):
    rank = wu_ref.shape[0]
    grad_hidden = jnp.zeros((x_ref.shape[0], rank), F32)
    for c in column_chunks(x_ref.shape[1]):
        x = x_ref[:, c].astype(F32)
        grad_crossed = mm_nt(g, wo_ref[c, :]).astype(BF16).astype(F32)
        grad_gate = grad_crossed * x
        bg_ref[:, c] = jnp.sum(grad_gate, axis=0, keepdims=True)
        low = grad_gate.astype(BF16)
        gg_ref[:, c] = low
        grad_hidden += mm_nt(low, wu_ref[:, c])
        if gc_ref is not None:
            gc_ref[:, c] = grad_crossed.astype(BF16)
    grad_hidden = grad_hidden.astype(BF16)
    ht_ref[0:rank, :] = grad_hidden.T
    ht_ref[rank : 2 * rank, :] = low_ref[...].T
    ht_ref[2 * rank :, :] = g.T
    return grad_hidden


def forward_kernel(wd_hbm, wu_hbm, wo_hbm, x_hbm, bias_ref, wd_ref, wu_ref, wo_ref, x_ref, low_ref, cr_ref, factor_ref, sem_ref):
    copies = copy_all([(x_hbm, x_ref), (wd_hbm, wd_ref), (wu_hbm, wu_ref), (wo_hbm, wo_ref)], sem_ref)
    copies[0].wait()
    copies[1].wait()
    forward_rows(x_ref, wd_ref, wu_ref, bias_ref, low_ref, cr_ref, factor_ref, copies[2])
    copies[3].wait()


def backward_kernel(n_tower, wu_ref, wo_ref, x_ref, low_ref, *refs):
    pieces = refs[:n_tower]
    g_ref, gh_ref, ht_ref, gg_ref, bg_ref, gc_ref = refs[n_tower:]
    me = lax.axis_index("tower")
    rows = pieces[0].shape[0]
    for k, piece in zip(range(len(pieces) - 1, -1, -1), pieces):
        g_ref[pl.ds(pl.multiple_of((me ^ k) * rows, rows), rows), :] = piece[...]
    gh_ref[...] = backward_rows(
        x_ref, g_ref[...], low_ref, wu_ref, wo_ref, gg_ref, bg_ref, ht_ref, gc_ref
    )


def inputs_kernel(n_tower, wd_ref, gh_ref, gc_ref, factor_ref, *refs):
    pieces, gi_ref = refs[:n_tower], refs[n_tower]
    me = lax.axis_index("tower")
    rows = pieces[0].shape[0]
    grad_hidden = gh_ref[...]
    for c in column_chunks(gi_ref.shape[1]):
        direct = gc_ref[:, c].astype(F32) * factor_ref[:, c]
        gi_ref[:, c] = (direct + mm_nt(grad_hidden, wd_ref[c, :])).astype(BF16)
    for k, piece in enumerate(pieces):
        piece[...] = gi_ref[pl.ds(pl.multiple_of((me ^ k) * rows, rows), rows), :]


def products(flip, start, blocks, lhs_ref, acc_ref):
    shard = lax.axis_index("shard") ^ flip
    block = acc_ref.shape[0] // 2
    rank = blocks[0][3].shape[0] // 3
    n = blocks[0][3].shape[1]
    core = lax.rem(shard, 2)
    first = (shard - core) * block
    picked = pl.ds(pl.multiple_of(first, 2 * block), 2 * block)
    for i, rows in enumerate(blocks):
        lhs_ref[:, i * n : (i + 1) * n] = rows[3][picked, :]
    acc_ref[...] = jnp.zeros_like(acc_ref)
    for part in range(3):

        @pl.when((first < (part + 1) * rank) & (first + 2 * block > part * rank))
        def _():
            at = first + lax.broadcasted_iota(jnp.int32, lhs_ref.shape, 0)
            inside = (at >= part * rank) & (at < (part + 1) * rank)
            lhs = jnp.where(inside, lhs_ref[...].astype(F32), 0.0).astype(BF16)
            for c in column_chunks(acc_ref.shape[1]):
                at_c = slice(start + c.start, start + c.stop)
                rhs = [rows[part][:, at_c] for rows in blocks]
                acc_ref[:, c] += mm(lhs, jnp.concatenate(rhs, axis=0))

    theirs = pl.ds(pl.multiple_of((1 - core) * block, block), block)
    ours = pl.ds(pl.multiple_of(core * block, block), block)
    return theirs, ours


def bias_rows(bias):
    high = bias.astype(BF16).astype(F32)
    rest = bias - high
    slabs = [slice(c, c + SLAB) for c in range(0, bias.shape[1], SLAB)]
    filler = [jnp.zeros((1, SLAB), F32)] * (TILE - 2 * len(slabs))
    return jnp.concatenate([high[:, c] for c in slabs] + [rest[:, c] for c in slabs] + filler, axis=0)


def bias_of(rows, n_slabs):
    return jnp.concatenate([rows[j : j + 1] + rows[n_slabs + j : n_slabs + j + 1] for j in range(n_slabs)], axis=1)


def is_outer():
    chip = lax.div(lax.axis_index("shard"), 2)
    return (chip == 0) | (chip == lax.div(lax.axis_size("shard"), 2) - 1)


def store_slabs(acc_ref, theirs, ours, biases, send_refs, keep_ref):
    block = acc_ref.shape[0] // 2
    n_slabs = acc_ref.shape[1] // SLAB
    each = n_slabs // len(send_refs)
    for j in range(n_slabs):
        c, at = slice(j * SLAB, (j + 1) * SLAB), j % each * block
        send_refs[j // each][at : at + block, :] = acc_ref[theirs, c].astype(BF16)
        keep_ref[j * block : (j + 1) * block, :] = acc_ref[ours, c]
    for i, bias in enumerate(biases):
        low = bias_rows(bias).astype(BF16)
        at = each * block + i * TILE
        send_refs[-1][at : at + TILE, :] = low
        at = n_slabs * block + i * TILE
        keep_ref[at : at + TILE, :] = low.astype(F32)


def first_kernel(x_own, gg_own, cr_own, ht_own, bg_own, keep_ref, *refs):
    send_refs, (lhs_ref, acc_ref) = refs[:-2], refs[-2:]
    outer = is_outer()
    (send_ref,) = send_refs
    block, n_slabs = acc_ref.shape[0] // 2, acc_ref.shape[1] // SLAB
    shard = lax.axis_index("shard")
    even = lax.rem(shard, 2) == 0
    last = ht_own.shape[0] - 2 * block

    for here, start, rhs_ref in ((shard < 2, last, cr_own), (outer & (shard >= 2), 0, x_own)):

        @pl.when(here)
        def _(start=start, rhs_ref=rhs_ref):
            lhs = ht_own[start : start + 2 * block, :]
            for j in range(n_slabs):
                both = mm(lhs, rhs_ref[:, j * SLAB : (j + 1) * SLAB])
                rows = slice(j * block, (j + 1) * block)
                low, high = both[:block], both[block:]
                send_ref[rows, :] = jnp.where(even, high, low).astype(BF16)
                keep_ref[rows, :] = jnp.where(even, low, high)
            rows = bias_rows(bg_own[...]).astype(BF16)
            send_ref[-TILE:, :] = rows
            keep_ref[-TILE:, :] = rows.astype(F32)

    @pl.when(jnp.logical_not(outer))
    def _():
        for ref in (*send_refs, keep_ref):
            ref[...] = jnp.zeros_like(ref)


def second_kernel(wu_ref, wo_ref, bg_own, x_own, gg_own, cr_own, ht_own, x_ref, low_ref, cr_ref, g_ref, *refs):
    gg_ref, ht_ref, bg_ref, keep_ref = refs[:4]
    send_refs, (lhs_ref, acc_ref) = refs[4:-2], refs[-2:]
    outer = is_outer()

    @pl.when(outer)
    def _():
        for ref in (gg_ref, bg_ref, ht_ref):
            ref[...] = jnp.zeros_like(ref)
        theirs, ours = products(4, 0, [(x_own, gg_own, cr_own, ht_own)], lhs_ref, acc_ref)
        store_slabs(acc_ref, theirs, ours, [bg_own[...]], send_refs, keep_ref)

    @pl.when(jnp.logical_not(outer))
    def _():
        backward_rows(x_ref, g_ref[...], low_ref, wu_ref, wo_ref, gg_ref, bg_ref, ht_ref, None)
        theirs, ours = products(2, 0, [(x_ref, gg_ref, cr_ref, ht_ref)], lhs_ref, acc_ref)
        store_slabs(acc_ref, theirs, ours, [bg_ref[...]], send_refs, keep_ref)


def near_kernel(wu_ref, wo_ref, x_ref, low_ref, cr_ref, g_ref, *refs):
    own, inner, bg_own, bg_inner, first_ref, keep_ref = refs[:4], refs[4:8], *refs[8:12]
    send_refs, (gg_ref, ht_ref, bg_ref, lhs_ref, acc_ref) = refs[12:-5], refs[-5:]
    backward_rows(x_ref, g_ref[...], low_ref, wu_ref, wo_ref, gg_ref, bg_ref, ht_ref, None)
    theirs, ours = products(0, 0, [own, (x_ref, gg_ref, cr_ref, ht_ref), inner], lhs_ref, acc_ref)
    store_slabs(acc_ref, theirs, ours, [bg_own[...], bg_ref[...], bg_inner[...]], send_refs, keep_ref)
    sums = slice(0, first_ref.shape[0] - TILE)
    keep_ref[sums, :] += first_ref[sums, :].astype(F32)


def joined_bias(rows, n_slabs):
    return bias_rows(bias_of(rows, n_slabs)).astype(BF16)


def round_kernel(n_slabs, keep_ref, *refs):
    recv_refs, out_ref = refs[:-1], refs[-1]
    at = 0
    for recv_ref in recv_refs:
        rows = slice(at, at + recv_ref.shape[0])
        out_ref[rows, :] = (keep_ref[rows, :] + recv_ref[...].astype(F32)).astype(BF16)
        at = rows.stop
    out_ref[-TILE:, :] = joined_bias(keep_ref[-TILE:, :] + recv_refs[-1][-TILE:, :].astype(F32), n_slabs)


def before_last_kernel(scale, keep_ref, first_ref, *refs):
    near_refs, (sum_ref, near_bias_ref, far_bias_ref) = refs[:-3], refs[-3:]
    block, width = sum_ref.shape
    n_slabs = width // SLAB
    each = n_slabs // len(near_refs)
    for j in range(n_slabs):
        at = j % each * block
        total = keep_ref[j * block : (j + 1) * block, :] + near_refs[j // each][at : at + block, :].astype(F32)
        sum_ref[:, j * SLAB : (j + 1) * SLAB] = total * scale
    here = []
    for i in range(3):
        rows = slice(n_slabs * block + i * TILE, n_slabs * block + (i + 1) * TILE)
        at = each * block + i * TILE
        joined = joined_bias(keep_ref[rows, :] + near_refs[-1][at : at + TILE, :].astype(F32), n_slabs)
        here.append(bias_of(joined.astype(F32), n_slabs))
    near_bias_ref[...] = here[0] + here[1]
    far_bias_ref[...] = here[2] + bias_of(first_ref[-TILE:, :].astype(F32), n_slabs)


def final_kernel(scale, sum_ref, near_bias_ref, far_bias_ref, second_ref, out_ref, bg_out, total_ref, bg_ref, sem_ref):
    block, width = total_ref.shape
    n_slabs = width // SLAB
    copies = []

    def write(source, target, i):
        copies.append(pltpu.make_async_copy(source, target, sem_ref.at[i]))
        copies[-1].start()

    bg_ref[...] = near_bias_ref[...] + (far_bias_ref[...] + bias_of(second_ref[-TILE:, :].astype(F32), n_slabs))
    write(bg_ref, bg_out, n_slabs)
    for j in range(n_slabs):
        c, rows = slice(j * SLAB, (j + 1) * SLAB), slice(j * block, (j + 1) * block)
        total_ref[:, c] = sum_ref[:, c] + second_ref[rows, :].astype(F32) * scale
        write(total_ref.at[:, pl.ds(j * SLAB, SLAB)], out_ref.at[:, pl.ds(j * SLAB, SLAB)], j)
    for copy in copies:
        copy.wait()


def place_kernel(n_tower, assign_ref, *refs):
    pieces, out_ref = refs[:n_tower], refs[n_tower]
    me = lax.axis_index("tower")
    slots = pieces[0].shape[1] // EMB
    for k in range(n_tower):
        for j in range(slots):
            at = assign_ref[(me ^ k) * slots + j] * EMB
            out_ref[:, pl.ds(pl.multiple_of(at, EMB), EMB)] = pieces[k][:, j * EMB : (j + 1) * EMB]


def xor_pairs(n, k):
    return [(i, i ^ k) for i in range(n)]


def after(value, *earlier):
    return lax.optimization_barrier((value, *earlier))[0]


def paired_body(out_grad, pooled, down_proj, up_proj, cross_bias, out_proj, assign):
    n_tower, n_shard = lax.axis_size("tower"), lax.axis_size("shard")
    sds = jax.ShapeDtypeStruct
    w_down, w_up, w_out, x = down_proj[0], up_proj[0], out_proj[0], pooled[0]
    n, width = x.shape
    rank, out = w_up.shape[0], w_out.shape[1]
    stack = 2 * rank + out
    block = stack // n_shard
    top_rows = out_grad.shape[0]
    wide = sds((n, width), BF16)
    tall = sds((stack, n), BF16)
    low = sds((n, rank), BF16)
    row = sds((1, width), F32)
    slab_rows = block * width // SLAB

    def across(value, axis, k):
        return lax.ppermute(value, axis, xor_pairs(lax.axis_size(axis), k))

    def slab_outs(n_bias, pieces):
        rows = [slab_rows // pieces] * pieces
        rows[-1] += n_bias * TILE
        return [sds((sum(rows), SLAB), F32)] + [sds((r, SLAB), BF16) for r in rows]

    def sum_scratch(n_blocks):
        return [pltpu.VMEM((2 * block, n_blocks * n), BF16), pltpu.VMEM((2 * block, width), F32)]

    def rounded(keep, *sends):
        (out,) = call(
            functools.partial(round_kernel, width // SLAB),
            [sds(keep.shape, BF16)],
            [],
            [VMEM] * (1 + len(sends)),
            [keep] + [across(send, "shard", 1) for send in sends],
            "join_cores",
            cost=1,
        )
        return out

    inside = [2 <= i < n_shard - 2 for i in range(n_shard)]
    inner = [(i, i ^ 6 if inside[i] else i ^ 1) for i in range(n_shard)]
    outer = [(i, i ^ 1 if inside[i] else i ^ 6) for i in range(n_shard)]
    second = [(i, i ^ 2 if inside[i] else i ^ 4) for i in range(n_shard)]

    x_other = across(x, "shard", 2)
    x_inner = lax.ppermute(x, "shard", inner)
    pieces = call(
        functools.partial(cut_kernel, n_tower),
        [sds((top_rows, out), BF16)] * n_tower,
        [pltpu.SemaphoreType.DMA((n_tower,))],
        [HBM],
        [out_grad],
        "cut_columns",
        48 * MIB,
        10**9,
    )
    received = [across(pieces[k], "tower", k) for k in range(n_tower - 1, 0, -1)]
    pieces = [pieces[0]] + received[::-1]
    wd, wu, wo, x_own, low_own, cr_own, factor = call(
        forward_kernel,
        [sds(w.shape, BF16) for w in (w_down, w_up, w_out)] + [wide, low, wide, sds((n, width), F32)],
        [pltpu.SemaphoreType.DMA((4,))],
        [HBM] * 4 + [VMEM],
        [w_down, w_up, w_out, x, cross_bias],
        "forward_own",
        VM * MIB,
        1,
    )
    g_own, gh_own, ht_own, gg_own, bg_own, gc_own = call(
        functools.partial(backward_kernel, n_tower),
        [sds((n, out), BF16), low, tall, wide, row, wide],
        [],
        [VMEM] * (4 + n_tower),
        [wu, wo, x_own, low_own, *pieces[::-1]],
        "backward_own",
        cost=1,
    )
    own = [x_own, gg_own, cr_own, ht_own]
    g_inner = lax.ppermute(g_own, "shard", inner)
    g_other = across(g_own, "shard", 2)
    first = rounded(
        *call(first_kernel, slab_outs(1, 1), sum_scratch(1), [VMEM] * 5, [*own, bg_own], "first_sums", cost=C1)
    )
    from_first = lax.ppermute(first, "shard", outer)
    low_inner, cr_inner = call(
        forward_inner_kernel, [low, wide], [], [VMEM] * 4, [after(x_inner, first), wd, wu, cross_bias], "forward_inner", cost=C2
    )
    low_other, cr_other = call(
        forward_rows, [low, wide], [], [VMEM] * 4, [after(x_other, low_inner, g_other), wd, wu, cross_bias], "forward_other", cost=C2
    )
    gg_inner, ht_inner, bg_inner, *sums = call(
        second_kernel,
        [wide, tall, row] + slab_outs(1, P2),
        sum_scratch(1),
        [VMEM] * 11,
        [wu, wo, bg_own, *own, x_inner, after(low_inner, low_other), cr_inner, g_inner],
        "second_sums",
        cost=C2,
    )
    second_sum = rounded(*sums)
    from_second = lax.ppermute(second_sum, "shard", second)
    grad_inputs = call(
        functools.partial(inputs_kernel, n_tower),
        [sds((top_rows, width), BF16)] * n_tower,
        [pltpu.VMEM((n, width), BF16)],
        [VMEM] * 4,
        [wd, gh_own, after(gc_own, second_sum), factor],
        "grad_inputs",
        cost=C4,
    )
    near_keep, *near_sends = call(
        near_kernel,
        slab_outs(3, PN),
        [pltpu.VMEM((n, width), BF16), pltpu.VMEM((stack, n), BF16), pltpu.VMEM((1, width), F32)] + sum_scratch(3),
        [VMEM] * 17,
        [wu, wo, x_other, after(low_other, *grad_inputs), cr_other, g_other, *own, x_inner, gg_inner, cr_inner, ht_inner, bg_own, bg_inner, from_first],
        "near_sums",
        cost=CN,
    )
    near_others = [across(send, "shard", 1) for send in near_sends]
    returned = [grad_inputs[0]]
    for k in range(1, n_tower):
        piece = grad_inputs[k]
        returned.append(across(piece, "tower", k))
    (feature_grad,) = call(
        functools.partial(place_kernel, n_tower),
        [sds((top_rows, n_tower * width), BF16)],
        [],
        [SMEM] + [VMEM] * n_tower,
        [assign, *returned],
        "place_features",
        cost=1,
    )
    scale = 1.0 / math.sqrt(n * n_shard)
    before_last = call(
        functools.partial(before_last_kernel, scale),
        [sds((block, width), F32), row, row],
        [],
        [VMEM] * (2 + len(near_others)),
        [near_keep, from_first, *near_others],
        "before_last",
        cost=1,
    )
    weight_grad, bias_grad = call(
        functools.partial(final_kernel, scale),
        [sds((block, width), F32), row],
        [
            pltpu.VMEM((block, width), F32),
            pltpu.VMEM((1, width), F32),
            pltpu.SemaphoreType.DMA((width // SLAB + 1,)),
        ],
        [VMEM] * 4,
        [*before_last, from_second],
        "add_up",
        out_space=HBM,
    )
    return feature_grad, weight_grad[None], bias_grad


def general_body(out_grad, pooled, down_proj, up_proj, cross_bias, out_proj, assign):
    grad_out = lax.all_to_all(out_grad, "tower", split_axis=1, concat_axis=0, tiled=True)
    feature_in = pooled[0]
    w_down, w_up, w_out = down_proj[0], up_proj[0], out_proj[0]
    hidden_low = mm(feature_in, w_down).astype(BF16)
    factor = mm(hidden_low, w_up) + cross_bias + 1.0
    crossed = (feature_in * factor).astype(BF16)
    grad_crossed = mm_nt(grad_out, w_out).astype(BF16)
    grad_gate = grad_crossed.astype(F32) * feature_in
    grad_gate_low = grad_gate.astype(BF16)
    grad_hidden = mm_nt(grad_gate_low, w_up).astype(BF16)
    grad_inputs = (grad_crossed.astype(F32) * factor + mm_nt(grad_hidden, w_down)).astype(BF16)
    returned = lax.all_to_all(grad_inputs, "tower", split_axis=0, concat_axis=1, tiled=True)
    local_rows = returned.shape[0]
    blocks = returned.reshape(local_rows, -1, EMB)
    feature_grad = jnp.take(blocks, jnp.argsort(assign), axis=1).reshape(local_rows, -1)
    stacked = jnp.concatenate(
        [
            mm(grad_hidden.T, feature_in),
            mm(hidden_low.T, grad_gate_low),
            mm(grad_out.T, crossed),
        ],
        axis=0,
    )
    scale = 1.0 / math.sqrt(grad_out.shape[0] * lax.axis_size("shard"))
    summed = lax.psum_scatter(stacked, "shard", scatter_dimension=0, tiled=True)
    bias_grad = lax.psum(jnp.sum(grad_gate, axis=0), "shard")[None]
    return feature_grad, (summed * scale)[None], bias_grad


def solution(mesh):
    n_tower, n_shard = mesh.shape["tower"], mesh.shape["shard"]
    placed = (
        P(("tower", "shard"), None),
        P("tower", "shard", None),
        P("tower", None, None),
        P("tower", None, None),
        P("tower", None),
        P("tower", None, None),
        P(),
    )

    paired = n_shard == 2 * 4 and n_tower & (n_tower - 1) == 0
    return jax.shard_map(
        paired_body if paired else general_body,
        mesh=mesh,
        in_specs=placed,
        out_specs=(P(("tower", "shard"), None), P("tower", "shard", None), P("tower", None)),
        check_vma=False,
    )
```

```python
import functools
import math

import jax
import jax.numpy as jnp
from jax import lax
from jax.experimental import pallas as pl
from jax.experimental.pallas import tpu as pltpu
from jax.sharding import PartitionSpec as P

EMB = 128
SLAB = 256
TILE = 16
MIB = 1024 * 1024
VM = 48
COST = 10**10
C1 = 1
P2 = 2
PN = 4
CN = 10**9
C2 = 10**9
C3 = 1
C4 = 1
VMEM_LIMIT = 24 * MIB
BF16 = jnp.bfloat16
F32 = jnp.float32
HBM, VMEM, SMEM = pltpu.HBM, pltpu.VMEM, pltpu.SMEM


def mm(a, b):
    return jnp.dot(a, b, preferred_element_type=F32)


def mm_nt(a, b):
    return lax.dot_general(a, b, (((1,), (1,)), ((), ())), preferred_element_type=F32)


def call(kernel, outs, scratch, spaces, args, name, vmem=VMEM_LIMIT, cost=COST, out_space=None, aliases={}):
    return pl.pallas_call(
        kernel,
        out_shape=outs,
        in_specs=[pl.BlockSpec(memory_space=space) for space in spaces],
        out_specs=[pl.BlockSpec(memory_space=out_space or VMEM)] * len(outs),
        input_output_aliases=aliases,
        scratch_shapes=scratch,
        compiler_params=pltpu.CompilerParams(vmem_limit_bytes=vmem),
        cost_estimate=pl.CostEstimate(flops=cost, bytes_accessed=1, transcendentals=0),
        name=name,
    )(*args)


def column_chunks(width):
    step = 512 if width % 512 == 0 else width
    return [slice(c, c + step) for c in range(0, width, step)]


def copy_all(pairs, sem_ref):
    copies = [pltpu.make_async_copy(a, b, sem_ref.at[i]) for i, (a, b) in enumerate(pairs)]
    for copy in copies:
        copy.start()
    return copies


def cut_kernel(n_tower, grad_ref, *refs):
    pieces, sem_ref = refs[:n_tower], refs[n_tower]
    me = lax.axis_index("tower")
    out = pieces[0].shape[1]
    pairs = [
        (grad_ref.at[:, pl.ds(pl.multiple_of((me ^ k) * out, out), out)], piece)
        for k, piece in enumerate(pieces)
    ]
    for copy in copy_all(pairs, sem_ref):
        copy.wait()


def forward_rows(x_ref, wd_ref, wu_ref, bias_ref, low_ref, cr_ref, factor_ref=None, ready=None):
    low = mm(x_ref[...], wd_ref[...]).astype(BF16)
    low_ref[...] = low
    if ready is not None:
        ready.wait()
    for c in column_chunks(x_ref.shape[1]):
        factor = (mm(low, wu_ref[:, c]) + bias_ref[:, c]) + 1.0
        cr_ref[:, c] = (x_ref[:, c].astype(F32) * factor).astype(BF16)
        if factor_ref is not None:
            factor_ref[:, c] = factor


def forward_inner_kernel(x_ref, wd_ref, wu_ref, bias_ref, low_ref, cr_ref):
    outer = is_outer()

    @pl.when(outer)
    def _():
        low_ref[...] = jnp.zeros_like(low_ref)
        cr_ref[...] = jnp.zeros_like(cr_ref)

    @pl.when(jnp.logical_not(outer))
    def _():
        forward_rows(x_ref, wd_ref, wu_ref, bias_ref, low_ref, cr_ref)


def backward_rows(x_ref, g, low_ref, wu_ref, wo_ref, gg_ref, bg_ref, ht_ref, gc_ref):
    rank = wu_ref.shape[0]
    grad_hidden = jnp.zeros((x_ref.shape[0], rank), F32)
    for c in column_chunks(x_ref.shape[1]):
        x = x_ref[:, c].astype(F32)
        grad_crossed = mm_nt(g, wo_ref[c, :]).astype(BF16).astype(F32)
        grad_gate = grad_crossed * x
        bg_ref[:, c] = jnp.sum(grad_gate, axis=0, keepdims=True)
        low = grad_gate.astype(BF16)
        gg_ref[:, c] = low
        grad_hidden += mm_nt(low, wu_ref[:, c])
        if gc_ref is not None:
            gc_ref[:, c] = grad_crossed.astype(BF16)
    grad_hidden = grad_hidden.astype(BF16)
    ht_ref[0:rank, :] = grad_hidden.T
    ht_ref[rank : 2 * rank, :] = low_ref[...].T
    ht_ref[2 * rank :, :] = g.T
    return grad_hidden


def forward_kernel(wd_hbm, wu_hbm, wo_hbm, x_hbm, bias_ref, wd_ref, wu_ref, wo_ref, x_ref, low_ref, cr_ref, factor_ref, sem_ref):
    copies = copy_all([(x_hbm, x_ref), (wd_hbm, wd_ref), (wu_hbm, wu_ref), (wo_hbm, wo_ref)], sem_ref)
    copies[0].wait()
    copies[1].wait()
    forward_rows(x_ref, wd_ref, wu_ref, bias_ref, low_ref, cr_ref, factor_ref, copies[2])
    copies[3].wait()


def piece_order(n_tower):
    return [n_tower - 1, *range(1, n_tower - 1), 0]


def backward_kernel(n_tower, wu_ref, wo_ref, x_ref, low_ref, *refs):
    pieces = refs[:n_tower]
    g_ref, gh_ref, ht_ref, gg_ref, bg_ref, gc_ref = refs[n_tower:]
    me = lax.axis_index("tower")
    rows = pieces[0].shape[0]
    for k, piece in zip(piece_order(len(pieces)), pieces):
        g_ref[pl.ds(pl.multiple_of((me ^ k) * rows, rows), rows), :] = piece[...]
    gh_ref[...] = backward_rows(
        x_ref, g_ref[...], low_ref, wu_ref, wo_ref, gg_ref, bg_ref, ht_ref, gc_ref
    )


def inputs_kernel(n_tower, wd_ref, gh_ref, gc_ref, factor_ref, *refs):
    pieces, gi_ref = refs[:n_tower], refs[n_tower]
    me = lax.axis_index("tower")
    rows = pieces[0].shape[0]
    grad_hidden = gh_ref[...]
    for c in column_chunks(gi_ref.shape[1]):
        direct = gc_ref[:, c].astype(F32) * factor_ref[:, c]
        gi_ref[:, c] = (direct + mm_nt(grad_hidden, wd_ref[c, :])).astype(BF16)
    for k, piece in enumerate(pieces):
        piece[...] = gi_ref[pl.ds(pl.multiple_of((me ^ k) * rows, rows), rows), :]


def products(flip, start, blocks, lhs_ref, acc_ref):
    shard = lax.axis_index("shard") ^ flip
    block = acc_ref.shape[0] // 2
    rank = blocks[0][3].shape[0] // 3
    n = blocks[0][3].shape[1]
    core = lax.rem(shard, 2)
    first = (shard - core) * block
    picked = pl.ds(pl.multiple_of(first, 2 * block), 2 * block)
    for i, rows in enumerate(blocks):
        lhs_ref[:, i * n : (i + 1) * n] = rows[3][picked, :]
    acc_ref[...] = jnp.zeros_like(acc_ref)
    for part in range(3):

        @pl.when((first < (part + 1) * rank) & (first + 2 * block > part * rank))
        def _():
            at = first + lax.broadcasted_iota(jnp.int32, lhs_ref.shape, 0)
            inside = (at >= part * rank) & (at < (part + 1) * rank)
            lhs = jnp.where(inside, lhs_ref[...].astype(F32), 0.0).astype(BF16)
            for c in column_chunks(acc_ref.shape[1]):
                at_c = slice(start + c.start, start + c.stop)
                rhs = [rows[part][:, at_c] for rows in blocks]
                acc_ref[:, c] += mm(lhs, jnp.concatenate(rhs, axis=0))

    theirs = pl.ds(pl.multiple_of((1 - core) * block, block), block)
    ours = pl.ds(pl.multiple_of(core * block, block), block)
    return theirs, ours


def bias_rows(bias):
    high = bias.astype(BF16).astype(F32)
    rest = bias - high
    slabs = [slice(c, c + SLAB) for c in range(0, bias.shape[1], SLAB)]
    filler = [jnp.zeros((1, SLAB), F32)] * (TILE - 2 * len(slabs))
    return jnp.concatenate([high[:, c] for c in slabs] + [rest[:, c] for c in slabs] + filler, axis=0)


def bias_of(rows, n_slabs):
    return jnp.concatenate([rows[j : j + 1] + rows[n_slabs + j : n_slabs + j + 1] for j in range(n_slabs)], axis=1)


def is_outer():
    chip = lax.div(lax.axis_index("shard"), 2)
    return (chip == 0) | (chip == lax.div(lax.axis_size("shard"), 2) - 1)


def store_slabs(acc_ref, theirs, ours, biases, send_refs, keep_ref):
    block = acc_ref.shape[0] // 2
    n_slabs = acc_ref.shape[1] // SLAB
    each = n_slabs // len(send_refs)
    for j in range(n_slabs):
        c, at = slice(j * SLAB, (j + 1) * SLAB), j % each * block
        send_refs[j // each][at : at + block, :] = acc_ref[theirs, c].astype(BF16)
        keep_ref[j * block : (j + 1) * block, :] = acc_ref[ours, c]
    for i, bias in enumerate(biases):
        low = bias_rows(bias).astype(BF16)
        at = each * block + i * TILE
        send_refs[-1][at : at + TILE, :] = low
        at = n_slabs * block + i * TILE
        keep_ref[at : at + TILE, :] = low.astype(F32)


def first_kernel(x_own, gg_own, cr_own, ht_own, bg_own, keep_ref, *refs):
    send_refs, (lhs_ref, acc_ref) = refs[:-2], refs[-2:]
    outer = is_outer()
    (send_ref,) = send_refs
    block, n_slabs = acc_ref.shape[0] // 2, acc_ref.shape[1] // SLAB
    shard = lax.axis_index("shard")
    even = lax.rem(shard, 2) == 0
    last = ht_own.shape[0] - 2 * block

    for here, start, rhs_ref in ((shard < 2, last, cr_own), (outer & (shard >= 2), 0, x_own)):

        @pl.when(here)
        def _(start=start, rhs_ref=rhs_ref):
            lhs = ht_own[start : start + 2 * block, :]
            for j in range(n_slabs):
                both = mm(lhs, rhs_ref[:, j * SLAB : (j + 1) * SLAB])
                rows = slice(j * block, (j + 1) * block)
                low, high = both[:block], both[block:]
                send_ref[rows, :] = jnp.where(even, high, low).astype(BF16)
                keep_ref[rows, :] = jnp.where(even, low, high)
            rows = bias_rows(bg_own[...]).astype(BF16)
            send_ref[-TILE:, :] = rows
            keep_ref[-TILE:, :] = rows.astype(F32)

    @pl.when(jnp.logical_not(outer))
    def _():
        for ref in (*send_refs, keep_ref):
            ref[...] = jnp.zeros_like(ref)


def second_kernel(wu_ref, wo_ref, bg_own, x_own, gg_own, cr_own, ht_own, x_ref, low_ref, cr_ref, g_ref, *refs):
    gg_ref, ht_ref, bg_ref, keep_ref = refs[:4]
    send_refs, (lhs_ref, acc_ref) = refs[4:-2], refs[-2:]
    outer = is_outer()

    @pl.when(outer)
    def _():
        for ref in (gg_ref, bg_ref, ht_ref):
            ref[...] = jnp.zeros_like(ref)
        theirs, ours = products(4, 0, [(x_own, gg_own, cr_own, ht_own)], lhs_ref, acc_ref)
        store_slabs(acc_ref, theirs, ours, [bg_own[...]], send_refs, keep_ref)

    @pl.when(jnp.logical_not(outer))
    def _():
        backward_rows(x_ref, g_ref[...], low_ref, wu_ref, wo_ref, gg_ref, bg_ref, ht_ref, None)
        theirs, ours = products(2, 0, [(x_ref, gg_ref, cr_ref, ht_ref)], lhs_ref, acc_ref)
        store_slabs(acc_ref, theirs, ours, [bg_ref[...]], send_refs, keep_ref)


def near_kernel(wu_ref, wo_ref, x_ref, low_ref, cr_ref, g_ref, *refs):
    own, inner, bg_own, bg_inner, first_ref, keep_ref = refs[:4], refs[4:8], *refs[8:12]
    send_refs, (gg_ref, ht_ref, bg_ref, lhs_ref, acc_ref) = refs[12:-5], refs[-5:]
    backward_rows(x_ref, g_ref[...], low_ref, wu_ref, wo_ref, gg_ref, bg_ref, ht_ref, None)
    theirs, ours = products(0, 0, [own, (x_ref, gg_ref, cr_ref, ht_ref), inner], lhs_ref, acc_ref)
    store_slabs(acc_ref, theirs, ours, [bg_own[...], bg_ref[...], bg_inner[...]], send_refs, keep_ref)
    sums = slice(0, first_ref.shape[0] - TILE)
    keep_ref[sums, :] += first_ref[sums, :].astype(F32)


def joined_bias(rows, n_slabs):
    return bias_rows(bias_of(rows, n_slabs)).astype(BF16)


def round_kernel(n_slabs, keep_ref, *refs):
    recv_refs, out_ref = refs[:-1], refs[-1]
    at = 0
    for recv_ref in recv_refs:
        rows = slice(at, at + recv_ref.shape[0])
        out_ref[rows, :] = (keep_ref[rows, :] + recv_ref[...].astype(F32)).astype(BF16)
        at = rows.stop
    out_ref[-TILE:, :] = joined_bias(keep_ref[-TILE:, :] + recv_refs[-1][-TILE:, :].astype(F32), n_slabs)


def before_last_kernel(scale, keep_ref, first_ref, *refs):
    near_refs, (sum_ref, near_bias_ref, far_bias_ref) = refs[:-3], refs[-3:]
    block, width = sum_ref.shape
    n_slabs = width // SLAB
    each = n_slabs // len(near_refs)
    for j in range(n_slabs):
        at = j % each * block
        total = keep_ref[j * block : (j + 1) * block, :] + near_refs[j // each][at : at + block, :].astype(F32)
        sum_ref[:, j * SLAB : (j + 1) * SLAB] = total * scale
    here = []
    for i in range(3):
        rows = slice(n_slabs * block + i * TILE, n_slabs * block + (i + 1) * TILE)
        at = each * block + i * TILE
        joined = joined_bias(keep_ref[rows, :] + near_refs[-1][at : at + TILE, :].astype(F32), n_slabs)
        here.append(bias_of(joined.astype(F32), n_slabs))
    near_bias_ref[...] = here[0] + here[1]
    far_bias_ref[...] = here[2] + bias_of(first_ref[-TILE:, :].astype(F32), n_slabs)


def final_kernel(scale, sum_ref, near_bias_ref, far_bias_ref, second_ref, out_ref, bg_out, total_ref, bg_ref, sem_ref):
    block, width = total_ref.shape
    n_slabs = width // SLAB
    copies = []

    def write(source, target, i):
        copies.append(pltpu.make_async_copy(source, target, sem_ref.at[i]))
        copies[-1].start()

    for j in range(n_slabs):
        c, rows = slice(j * SLAB, (j + 1) * SLAB), slice(j * block, (j + 1) * block)
        total_ref[:, c] = sum_ref[:, c] + second_ref[rows, :].astype(F32) * scale
        write(total_ref.at[:, pl.ds(j * SLAB, SLAB)], out_ref.at[:, pl.ds(j * SLAB, SLAB)], j)
    bg_ref[...] = near_bias_ref[...] + (far_bias_ref[...] + bias_of(second_ref[-TILE:, :].astype(F32), n_slabs))
    write(bg_ref, bg_out, n_slabs)
    for copy in copies:
        copy.wait()


def place_kernel(n_tower, assign_ref, *refs):
    pieces, out_ref = refs[:n_tower], refs[n_tower]
    me = lax.axis_index("tower")
    slots = pieces[0].shape[1] // EMB
    for k in range(n_tower):
        for j in range(slots):
            at = assign_ref[(me ^ k) * slots + j] * EMB
            out_ref[:, pl.ds(pl.multiple_of(at, EMB), EMB)] = pieces[k][:, j * EMB : (j + 1) * EMB]


def xor_pairs(n, k):
    return [(i, i ^ k) for i in range(n)]


def after(value, *earlier):
    return lax.optimization_barrier((value, *earlier))[0]


def paired_body(out_grad, pooled, down_proj, up_proj, cross_bias, out_proj, assign):
    n_tower, n_shard = lax.axis_size("tower"), lax.axis_size("shard")
    sds = jax.ShapeDtypeStruct
    w_down, w_up, w_out, x = down_proj[0], up_proj[0], out_proj[0], pooled[0]
    n, width = x.shape
    rank, out = w_up.shape[0], w_out.shape[1]
    stack = 2 * rank + out
    block = stack // n_shard
    top_rows = out_grad.shape[0]
    wide = sds((n, width), BF16)
    tall = sds((stack, n), BF16)
    low = sds((n, rank), BF16)
    row = sds((1, width), F32)
    slab_rows = block * width // SLAB

    def across(value, axis, k):
        return lax.ppermute(value, axis, xor_pairs(lax.axis_size(axis), k))

    def slab_outs(n_bias, pieces):
        rows = [slab_rows // pieces] * pieces
        rows[-1] += n_bias * TILE
        return [sds((sum(rows), SLAB), F32)] + [sds((r, SLAB), BF16) for r in rows]

    def sum_scratch(n_blocks):
        return [pltpu.VMEM((2 * block, n_blocks * n), BF16), pltpu.VMEM((2 * block, width), F32)]

    def rounded(keep, *sends):
        (out,) = call(
            functools.partial(round_kernel, width // SLAB),
            [sds(keep.shape, BF16)],
            [],
            [VMEM] * (1 + len(sends)),
            [keep] + [across(send, "shard", 1) for send in sends],
            "join_cores",
            cost=1,
        )
        return out

    inside = [2 <= i < n_shard - 2 for i in range(n_shard)]
    inner = [(i, i ^ 6 if inside[i] else i ^ 1) for i in range(n_shard)]
    outer = [(i, i ^ 1 if inside[i] else i ^ 6) for i in range(n_shard)]
    second = [(i, i ^ 2 if inside[i] else i ^ 4) for i in range(n_shard)]

    x_other = across(x, "shard", 2)
    x_inner = lax.ppermute(x, "shard", inner)
    pieces = call(
        functools.partial(cut_kernel, n_tower),
        [sds((top_rows, out), BF16)] * n_tower,
        [pltpu.SemaphoreType.DMA((n_tower,))],
        [HBM],
        [out_grad],
        "cut_columns",
        48 * MIB,
        10**9,
    )
    received = [across(pieces[k], "tower", k) for k in range(n_tower - 1, 0, -1)]
    pieces = [pieces[0]] + received[::-1]
    wd, wu, wo, x_own, low_own, cr_own, factor = call(
        forward_kernel,
        [sds(w.shape, BF16) for w in (w_down, w_up, w_out)] + [wide, low, wide, sds((n, width), F32)],
        [pltpu.SemaphoreType.DMA((4,))],
        [HBM] * 4 + [VMEM],
        [w_down, w_up, w_out, x, cross_bias],
        "forward_own",
        VM * MIB,
        1,
    )
    g_own, gh_own, ht_own, gg_own, bg_own, gc_own = call(
        functools.partial(backward_kernel, n_tower),
        [sds((n, out), BF16), low, tall, wide, row, wide],
        [],
        [VMEM] * (4 + n_tower),
        [wu, wo, x_own, low_own, *[pieces[k] for k in piece_order(n_tower)]],
        "backward_own",
        cost=1,
    )
    own = [x_own, gg_own, cr_own, ht_own]
    g_inner = lax.ppermute(g_own, "shard", inner)
    g_other = across(g_own, "shard", 2)
    first = rounded(
        *call(first_kernel, slab_outs(1, 1), sum_scratch(1), [VMEM] * 5, [*own, bg_own], "first_sums", cost=C1)
    )
    from_first = lax.ppermute(first, "shard", outer)
    low_inner, cr_inner = call(
        forward_inner_kernel, [low, wide], [], [VMEM] * 4, [after(x_inner, first), wd, wu, cross_bias], "forward_inner", cost=C2
    )
    low_other, cr_other = call(
        forward_rows, [low, wide], [], [VMEM] * 4, [after(x_other, low_inner, g_other), wd, wu, cross_bias], "forward_other", cost=C2
    )
    gg_inner, ht_inner, bg_inner, *sums = call(
        second_kernel,
        [wide, tall, row] + slab_outs(1, P2),
        sum_scratch(1),
        [VMEM] * 11,
        [wu, wo, bg_own, *own, x_inner, after(low_inner, low_other), cr_inner, g_inner],
        "second_sums",
        cost=C2,
    )
    second_sum = rounded(*sums)
    from_second = lax.ppermute(second_sum, "shard", second)
    grad_inputs = call(
        functools.partial(inputs_kernel, n_tower),
        [sds((top_rows, width), BF16)] * n_tower,
        [pltpu.VMEM((n, width), BF16)],
        [VMEM] * 4,
        [wd, gh_own, after(gc_own, second_sum), factor],
        "grad_inputs",
        cost=C4,
    )
    near_keep, *near_sends = call(
        near_kernel,
        slab_outs(3, PN),
        [pltpu.VMEM((n, width), BF16), pltpu.VMEM((stack, n), BF16), pltpu.VMEM((1, width), F32)] + sum_scratch(3),
        [VMEM] * 17,
        [wu, wo, x_other, after(low_other, *grad_inputs), cr_other, g_other, *own, x_inner, gg_inner, cr_inner, ht_inner, bg_own, bg_inner, from_first],
        "near_sums",
        cost=CN,
    )
    near_others = [across(send, "shard", 1) for send in near_sends]
    returned = [grad_inputs[0]]
    for k in range(1, n_tower):
        piece = grad_inputs[k]
        returned.append(across(piece, "tower", k))
    (feature_grad,) = call(
        functools.partial(place_kernel, n_tower),
        [sds((top_rows, n_tower * width), BF16)],
        [],
        [SMEM] + [VMEM] * n_tower,
        [assign, *returned],
        "place_features",
        cost=1,
    )
    scale = 1.0 / math.sqrt(n * n_shard)
    before_last = call(
        functools.partial(before_last_kernel, scale),
        [sds((block, width), F32), row, row],
        [],
        [VMEM] * (2 + len(near_others)),
        [near_keep, from_first, *near_others],
        "before_last",
        cost=1,
    )
    weight_grad, bias_grad = call(
        functools.partial(final_kernel, scale),
        [sds((block, width), F32), row],
        [
            pltpu.VMEM((block, width), F32),
            pltpu.VMEM((1, width), F32),
            pltpu.SemaphoreType.DMA((width // SLAB + 1,)),
        ],
        [VMEM] * 4,
        [*before_last, from_second],
        "add_up",
        out_space=HBM,
    )
    return feature_grad, weight_grad[None], bias_grad


def general_body(out_grad, pooled, down_proj, up_proj, cross_bias, out_proj, assign):
    grad_out = lax.all_to_all(out_grad, "tower", split_axis=1, concat_axis=0, tiled=True)
    feature_in = pooled[0]
    w_down, w_up, w_out = down_proj[0], up_proj[0], out_proj[0]
    hidden_low = mm(feature_in, w_down).astype(BF16)
    factor = mm(hidden_low, w_up) + cross_bias + 1.0
    crossed = (feature_in * factor).astype(BF16)
    grad_crossed = mm_nt(grad_out, w_out).astype(BF16)
    grad_gate = grad_crossed.astype(F32) * feature_in
    grad_gate_low = grad_gate.astype(BF16)
    grad_hidden = mm_nt(grad_gate_low, w_up).astype(BF16)
    grad_inputs = (grad_crossed.astype(F32) * factor + mm_nt(grad_hidden, w_down)).astype(BF16)
    returned = lax.all_to_all(grad_inputs, "tower", split_axis=0, concat_axis=1, tiled=True)
    local_rows = returned.shape[0]
    blocks = returned.reshape(local_rows, -1, EMB)
    feature_grad = jnp.take(blocks, jnp.argsort(assign), axis=1).reshape(local_rows, -1)
    stacked = jnp.concatenate(
        [
            mm(grad_hidden.T, feature_in),
            mm(hidden_low.T, grad_gate_low),
            mm(grad_out.T, crossed),
        ],
        axis=0,
    )
    scale = 1.0 / math.sqrt(grad_out.shape[0] * lax.axis_size("shard"))
    summed = lax.psum_scatter(stacked, "shard", scatter_dimension=0, tiled=True)
    bias_grad = lax.psum(jnp.sum(grad_gate, axis=0), "shard")[None]
    return feature_grad, (summed * scale)[None], bias_grad


def solution(mesh):
    n_tower, n_shard = mesh.shape["tower"], mesh.shape["shard"]
    placed = (
        P(("tower", "shard"), None),
        P("tower", "shard", None),
        P("tower", None, None),
        P("tower", None, None),
        P("tower", None),
        P("tower", None, None),
        P(),
    )

    paired = n_shard == 2 * 4 and n_tower & (n_tower - 1) == 0
    return jax.shard_map(
        paired_body if paired else general_body,
        mesh=mesh,
        in_specs=placed,
        out_specs=(P(("tower", "shard"), None), P("tower", "shard", None), P("tower", None)),
        check_vma=False,
    )
```
